128 devices in a mesh: dp: 32 (over x, y, core), tensor: 4 (over z).
Axes of the slice: x: 4, y: 4, z: 4, core: 2. Of those that a mesh axis runs over, the one named last changes fastest.
Arguments:
- flat_weight: bfloat16 [37120, 8192], P(('dp', 'tensor')), may hold values from -0.0625 to 0.0625
- offsets: int32 [5], replicated, may hold values from 0 to 36864, as said below
- group_owner: int32 [8], replicated, may hold values from 0 to 3, as said below
- hidden: bfloat16 [256, 8192], P(None, 'dp'), may hold values from -6 to 6
- decay_rate: float32 [256], replicated, may hold values from 0.003 to 0.12
- dt_bias: float32 [256], replicated, may hold values from -1.5 to 1
- skip_gain: float32 [256], replicated, may hold values from 0.3 to 1.5
- norm_gain: float32 [16384], replicated, may hold values from 0.25 to 1.75
Outputs:
- w_rollout: bfloat16 [8192, 37120], P('dp', 'tensor')
- mixed: bfloat16 [256, 16384], P(None, ('dp', 'tensor'))
The draws below stay inside these ranges and needn't reach their ends.
Inputs may be any that keep to these rules, and one draw needn't show every extreme that they name: `offsets`: the five segments z, x, B, C, dt, of lengths 16384, 16384, 2048, 2048, 256, lie end to end starting at row 0, z, x, B, C in some order and dt last. `group_owner`: each owner holds exactly 2 groups.
All inputs are finite; a program needn't handle non-finite values.
Results may differ from the reference program's by a relative error of at most 0.002.
Values may be sent and summed in bfloat16 or wider, within the bound.
A program may use at most 128 MiB of HBM per device.

```python
import math
import jax
import jax.numpy as jnp
from jax import lax

D = 8192
H = 256
P_SIZE = 64
N = 256
G = 8
L = 128
DI = 16384
PROJ = 37120
TOKENS = 256
HG = 32
HL = 64
GL = 2
HD = 2
N_TENSOR = 4


def draw_offsets(key, part):
    key = jax.random.fold_in(key, 11)
    first = jax.random.permutation(key, 4)
    order = jnp.concatenate([first, jnp.array([4], jnp.int32)]).astype(jnp.int32)
    seg_lens = jnp.array([H * P_SIZE, H * P_SIZE, G * N, G * N, H], jnp.int32)
    position = jnp.argsort(order, stable=True)
    earlier = position[None, :] < position[:, None]
    return jnp.sum(jnp.where(earlier, seg_lens[None, :], 0), axis=1).astype(jnp.int32)


def draw_group_owner(key, part):
    key = jax.random.fold_in(key, 12)
    shuffled = jax.random.permutation(key, G)
    return (shuffled // (G // N_TENSOR)).astype(jnp.int32)


def level_of(stream_key, extent, shards, low, high):
    loudness, own = 1.0, jax.random.fold_in(stream_key, 6)
    for dim, parts in shards:
        draws = jnp.exp(jax.random.uniform(jax.random.fold_in(own, dim), (parts,), jnp.float32, low / len(shards), high / len(shards)))
        loudness = loudness * jnp.repeat(draws, extent[dim] // parts).reshape([-1 if axis == dim else 1 for axis in range(len(extent))])
    return loudness


def normal_values(rng, dims, deviation, limit, split=(), kind=jnp.bfloat16):
    drawn = deviation * jax.random.normal(rng, dims, jnp.float32)
    if split:
        drawn = drawn * level_of(rng, dims, split, -0.22, 0.18)
    return jnp.clip(drawn, -limit, limit).astype(kind)


def setup_inputs(seed: int = 0) -> dict:
    key_list = jax.random.split(jax.random.key(seed), 9)
    flat_weight = normal_values(key_list[0], (PROJ, D), D ** -0.5, 0.0625, ((0, 128),))
    offsets = draw_offsets(jax.random.fold_in(key_list[8], 71), 0)
    group_owner = draw_group_owner(jax.random.fold_in(key_list[8], 71), 0)
    hidden = normal_values(key_list[3], (TOKENS, D), 1.0, 6.0, ((1, 32),))
    decay_rate = jnp.clip(jnp.exp(jax.random.uniform(key_list[4], (H,), jnp.float32, math.log(0.003), math.log(0.12))), 0.003, 0.12)
    dt_bias = jnp.clip(jax.random.uniform(key_list[5], (H,), jnp.float32, -1.5, 1.0), -1.5, 1.0)
    skip_gain = jnp.clip(jax.random.uniform(key_list[6], (H,), jnp.float32, 0.3, 1.5), 0.3, 1.5)
    norm_gain = jnp.clip(1.0 + 0.15 * jax.random.normal(key_list[7], (DI,), jnp.float32), 0.25, 1.75)
    return {"flat_weight": flat_weight, "offsets": offsets, "group_owner": group_owner, "hidden": hidden, "decay_rate": decay_rate, "dt_bias": dt_bias, "skip_gain": skip_gain, "norm_gain": norm_gain}


def owner_rows(offsets, group_owner, owner, locals_n, groups_n):
    groups = jnp.nonzero(group_owner == owner, size=groups_n)[0].astype(jnp.int32)
    local = jnp.arange(locals_n, dtype=jnp.int32)
    heads = groups[local // HG] * HG + local % HG
    cols = jnp.arange(P_SIZE, dtype=jnp.int32)
    z_rows = offsets[0] + heads[:, None] * P_SIZE + cols[None, :]
    x_rows = offsets[1] + heads[:, None] * P_SIZE + cols[None, :]
    zx_rows = jnp.concatenate([z_rows, x_rows], axis=1).reshape(-1)
    states = jnp.arange(N, dtype=jnp.int32)
    b_rows = (offsets[2] + groups[:, None] * N + states[None, :]).reshape(-1)
    c_rows = (offsets[3] + groups[:, None] * N + states[None, :]).reshape(-1)
    dt_rows = offsets[4] + heads
    return (jnp.concatenate([zx_rows, b_rows, c_rows, dt_rows]).astype(jnp.int32), heads)

def mix_heads(xh, bmat, cmat, dt_raw, rate, bias, skip):
    step = jax.nn.softplus(dt_raw + bias)
    cumul = jnp.cumsum(-rate * step, axis=1)
    diff = cumul[:, :, None, :] - cumul[:, None, :, :]
    length = xh.shape[1]
    lower = jnp.arange(length)[:, None] >= jnp.arange(length)[None, :]
    lower = lower[None, :, :, None]
    decay = jnp.where(lower, jnp.exp(jnp.where(lower, diff, 0.0)), 0.0)
    scores = jnp.einsum('sthn,suhn->stuh', cmat, bmat, precision=lax.Precision.HIGHEST)
    weights = scores * decay * step[:, None, :, :]
    out = jnp.einsum('stuh,suhp->sthp', weights, xh, precision=lax.Precision.HIGHEST)
    return out + skip[None, None, :, None] * xh

def reference(flat_weight, offsets, group_owner, hidden, decay_rate, dt_bias, skip_gain, norm_gain):
    owners = G // GL
    blocks = []
    outs = []
    seqs_n = hidden.shape[0] // L
    for owner in range(owners):
        rows, heads = owner_rows(offsets, group_owner, owner, HL, GL)
        w_block = jnp.take(flat_weight, rows, axis=0).T
        blocks.append(w_block)
        proj = jnp.dot(hidden, w_block, preferred_element_type=jnp.float32)
        zx = proj[:, :HL * 2 * P_SIZE].reshape(seqs_n, L, HL, 2, P_SIZE)
        gate = zx[:, :, :, 0, :]
        xh = zx[:, :, :, 1, :]
        base = HL * 2 * P_SIZE
        bmat = proj[:, base:base + GL * N].reshape(seqs_n, L, GL, N)
        cmat = proj[:, base + GL * N:base + 2 * GL * N].reshape(seqs_n, L, GL, N)
        dt_raw = proj[:, base + 2 * GL * N:].reshape(seqs_n, L, HL)
        which = jnp.arange(HL) // HG
        y = mix_heads(xh, bmat[:, :, which], cmat[:, :, which], dt_raw, decay_rate[heads], dt_bias[heads], skip_gain[heads])
        v = y * jax.nn.silu(gate)
        grouped = v.reshape(seqs_n, L, GL, HG * P_SIZE)
        scale = lax.rsqrt(lax.optimization_barrier(jnp.mean(grouped * grouped, axis=-1, keepdims=True)) + 1e-05)
        gains = norm_gain.reshape(H, P_SIZE)[heads]
        normed = (grouped * scale).reshape(seqs_n * L, HL, P_SIZE) * gains[None]
        outs.append(normed)
    w_rollout = jnp.concatenate(blocks, axis=1)
    stacked = jnp.stack(outs, axis=1)
    tokens_n = stacked.shape[0]
    per_dev = HD
    stacked = stacked.reshape(tokens_n, owners, HL // per_dev, per_dev, P_SIZE)
    mixed = jnp.transpose(stacked, (0, 2, 1, 3, 4)).reshape(tokens_n, H * P_SIZE)
    return (w_rollout, mixed.astype(jnp.bfloat16))
```

```python
import functools

import jax
import jax.numpy as jnp
import numpy as np
from jax import lax
from jax.experimental import pallas as pl
from jax.experimental.pallas import tpu as pltpu
from jax.sharding import PartitionSpec as P

H = 256
P_SIZE = 64
N = 256
G = 8
L = 128
ROWS = 290
D = 8192
F = 256
NDP = 32
NT = 4
TILE = 16
CHUNK = 19
BLOCKS = 18
BT = 128
PARTS = (4, 5, 5, 5)
STARTS = (0, 4, 9, 14)
MESH = pl.DeviceIdType.MESH
BF16 = jnp.bfloat16
F32 = jnp.float32


def first_tile(chunk):
    return ROWS * chunk // TILE


def make_tables():
    n = len(PARTS)
    lo = np.full((n, NT, BLOCKS), 10**6)
    hi = np.full((n, NT, BLOCKS), -1)
    where = {}
    for k in range(NDP * NT):
        for l in range(CHUNK):
            p = max(i for i in range(n) if STARTS[i] <= l)
            b, tau = divmod(first_tile(k) + l, BT)
            if b >= BLOCKS:
                continue
            i = (k // NT) * PARTS[p] + l - STARTS[p]
            where.setdefault((b, tau), []).append((k % NT, p, i))
            lo[p, k % NT, b] = min(lo[p, k % NT, b], i)
            hi[p, k % NT, b] = max(hi[p, k % NT, b], i)
    caps = [int((hi[p] - lo[p] + 1).max()) for p in range(n)]
    start = np.zeros((n, NT, BLOCKS), np.int32)
    for p in range(n):
        start[p] = np.clip(lo[p], 0, NDP * PARTS[p] - caps[p])
    offs = np.concatenate([[0], np.cumsum(caps)])
    slot = int(offs[-1])
    place = np.full((BLOCKS, BT, 2), -1, np.int32)
    for (b, tau), found in where.items():
        for e, (t, p, i) in enumerate(found):
            place[b, tau, e] = t * 6 * slot + offs[p] + i - start[p, t, b]
    return caps, [int(o) for o in offs], slot, start, place


CAPS, OFFS, SLOT, START, PLACE = make_tables()
NP = len(PARTS)


def dp_order():
    steps = [(a, b, c) for a in range(4) for b in range(4) for c in range(2) if (a, b, c) != (0, 0, 0)]
    steps.sort(key=lambda s: -(min(s[0], 4 - s[0]) + min(s[1], 4 - s[1])))
    out = []
    for a, b, c in steps:
        for q in ((a, b, c), (b, a, c), (-a % 4, -b % 4, c), (-b % 4, -a % 4, c)):
            if q not in out:
                out.append(q)
    return out[::-1]


ORDER = dp_order()


def dp_partner(d, step):
    x, y, c = d // 8, (d // 2) % 4, d % 2
    return ((x + step[0]) % 4) * 8 + ((y + step[1]) % 4) * 2 + (c + step[2]) % 2


def owner_groups(owner_ref, owner):
    first, last = jnp.int32(G), jnp.int32(-1)
    for g in range(G):
        mine = owner_ref[g] == owner
        first = jnp.where(mine, jnp.minimum(first, g), first)
        last = jnp.where(mine, g, last)
    return jnp.clip(first, 0, G - 1), jnp.clip(last, 0, G - 1)


def prep_kernel(off_ref, own_ref, start_ref, windows_ref):
    t = lax.axis_index("tensor")
    seg = [off_ref[i] // 2048 for i in range(4)]
    for shift in range(NT):
        g = owner_groups(own_ref, (t + shift) % NT)
        for p in range(NP):
            for s in range(4):
                windows_ref[p * 18 + shift * 4 + s] = start_ref[(p * NT + t) * BLOCKS + seg[s // 2] + g[s % 2]]
        for i in range(2):
            windows_ref[NP * 18 + shift * 2 + i] = 2 * g[i]
    for p in range(NP):
        for i in range(2):
            windows_ref[p * 18 + 16 + i] = start_ref[(p * NT + t) * BLOCKS + seg[2 + i]]


def prep(offsets, group_owner):
    smem = pl.BlockSpec(memory_space=pltpu.SMEM)
    return pl.pallas_call(
        prep_kernel,
        out_shape=jax.ShapeDtypeStruct((NP * 18 + 8,), jnp.int32),
        in_specs=[smem] * 3,
        out_specs=smem,
        name="prep",
    )(offsets, group_owner, jnp.asarray(START.reshape(-1)))


def exchange_kernel(windows_ref, flat_ref, out_ref, dt_ref, *scratch):
    shifted = scratch[:NP]
    recv = scratch[NP : 2 * NP]
    send = scratch[2 * NP : 3 * NP]
    both = scratch[3 * NP : 4 * NP]
    dtbuf, dtsend, dp_send, dp_recv, z_send, z_recv, self_sem = scratch[4 * NP :]
    d = lax.axis_index("dp")
    t = lax.axis_index("tensor")

    barrier = pltpu.get_barrier_semaphore()

    @pl.loop(1, NDP)
    def _(i):
        pl.semaphore_signal(barrier, inc=1, device_id=((d + i) % NDP, t), device_id_type=MESH)

    @pl.loop(1, NT)
    def _(i):
        pl.semaphore_signal(barrier, inc=1, device_id=(d, (t + i) % NT), device_id_type=MESH)

    pl.semaphore_wait(barrier, NDP - 1 + NT - 1)

    phase = (ROWS * (d * NT + t)) % TILE
    for p in range(NP):
        a, rows = STARTS[p] * TILE, PARTS[p] * TILE
        w0, w1 = max(a - TILE, 0), min(a + rows, ROWS)
        to = lax.broadcasted_iota(jnp.int32, (rows, w1 - w0), 0) + (a - phase)
        frm = lax.broadcasted_iota(jnp.int32, (rows, w1 - w0), 1) + w0
        pick = jnp.where(to == frm, 1.0, 0.0).astype(BF16)

        @pl.loop(0, D // 1024)
        def _(i):
            cols = pl.ds(pl.multiple_of(i * 1024, 1024), 1024)
            moved = jnp.dot(pick, flat_ref[w0:w1, cols], preferred_element_type=F32)
            shifted[p][:, :, cols] = moved.astype(BF16).reshape(PARTS[p], TILE, 1024)

        mine = pl.ds(d * PARTS[p], PARTS[p])
        for step in ORDER:
            peer = dp_partner(d, step)
            pltpu.make_async_remote_copy(
                src_ref=shifted[p].at[:, :, pl.ds(pl.multiple_of(peer * F, F), F)],
                dst_ref=recv[p].at[mine],
                send_sem=dp_send.at[p],
                recv_sem=dp_recv.at[p],
                device_id=(peer, t),
                device_id_type=MESH,
            ).start()
        pltpu.make_async_copy(
            shifted[p].at[:, :, pl.ds(pl.multiple_of(d * F, F), F)], recv[p].at[mine], dp_recv.at[p]
        ).start()

    copies = []
    for p in range(NP):
        pltpu.make_async_copy(recv[p], recv[p], dp_recv.at[p]).wait()

        def pack(dst, window):
            first = windows_ref[window]

            @pl.loop(0, CAPS[p], unroll=2)
            def _(j):
                dst[j] = recv[p][first + j]

        for i in range(2):
            pack(both[p].at[i], p * 18 + 16 + i)
        for l in range(max(STARTS[p], 3), STARTS[p] + PARTS[p]):
            dtbuf[l - 3] = recv[p][31 * PARTS[p] + l - STARTS[p]]
        for shift in (1, 3, 2, 0):
            for s in range(4):
                pack(send[p].at[shift, s], p * 18 + shift * 4 + s)
            target = (d, (t + shift) % NT)
            span = pl.ds(OFFS[p], CAPS[p])
            pairs = [
                (send[p].at[shift], out_ref.at[t, 0:4, span]),
                (both[p], out_ref.at[t, 4:6, span]),
            ]
            for n, (src, dst) in enumerate(pairs):
                if shift == 0:
                    cp = pltpu.make_async_copy(src, dst, self_sem.at[2 * p + n])
                else:
                    cp = pltpu.make_async_remote_copy(
                        src_ref=src,
                        dst_ref=dst,
                        send_sem=z_send.at[shift - 1, 2 * p + n],
                        recv_sem=z_recv.at[shift - 1, 2 * p + n],
                        device_id=target,
                        device_id_type=MESH,
                    )
                cp.start()
                copies.append(cp)
    for shift in (1, 3, 2, 0):
        for i in range(2):
            for j in range(2):
                dtsend[shift, 2 * i + j] = dtbuf[windows_ref[NP * 18 + shift * 2 + i] + j]
        if shift == 0:
            cp = pltpu.make_async_copy(dtsend.at[0], dt_ref.at[t], self_sem.at[2 * NP])
        else:
            cp = pltpu.make_async_remote_copy(
                src_ref=dtsend.at[shift],
                dst_ref=dt_ref.at[t],
                send_sem=z_send.at[shift - 1, 2 * NP],
                recv_sem=z_recv.at[shift - 1, 2 * NP],
                device_id=(d, (t + shift) % NT),
                device_id_type=MESH,
            )
        cp.start()
        copies.append(cp)
    for cp in copies:
        cp.wait()
    for p in range(NP):
        sent = shifted[p].at[:, :, 0 : (NDP - 1) * F]
        pltpu.make_async_copy(sent, sent, dp_send.at[p]).wait()


def exchange(windows, flat):
    any_ = pl.BlockSpec(memory_space=pl.ANY)
    return pl.pallas_call(
        exchange_kernel,
        out_shape=(
            jax.ShapeDtypeStruct((NT, 6, SLOT, TILE, F), BF16),
            jax.ShapeDtypeStruct((NT, 4, TILE, F), BF16),
        ),
        in_specs=[pl.BlockSpec(memory_space=pltpu.SMEM), pl.BlockSpec(memory_space=pltpu.VMEM)],
        out_specs=(any_, any_),
        scratch_shapes=[pltpu.VMEM((w, TILE, D), BF16) for w in PARTS]
        + [pltpu.VMEM((NDP * w, TILE, F), BF16) for w in PARTS]
        + [pltpu.VMEM((NT, 4, c, TILE, F), BF16) for c in CAPS]
        + [pltpu.VMEM((2, c, TILE, F), BF16) for c in CAPS]
        + [
            pltpu.VMEM((16, TILE, F), BF16),
            pltpu.VMEM((NT, 4, TILE, F), BF16),
            pltpu.SemaphoreType.DMA((NP,)),
            pltpu.SemaphoreType.DMA((NP,)),
            pltpu.SemaphoreType.DMA((NT - 1, 2 * NP + 1)),
            pltpu.SemaphoreType.DMA((NT - 1, 2 * NP + 1)),
            pltpu.SemaphoreType.DMA((2 * NP + 1,)),
        ],
        compiler_params=pltpu.CompilerParams(
            collective_id=1, has_side_effects=True, vmem_limit_bytes=56 << 20
        ),
        name="exchange",
    )(windows, flat)


WIDE = 1024


def place_kernel(off_ref, own_ref, place_ref, got_ref, dt_ref, out_ref, rows_ref):
    step = pl.program_id(0)
    g = owner_groups(own_ref, lax.axis_index("tensor"))
    eye = jnp.where(
        lax.broadcasted_iota(jnp.int32, (F, F), 0) == lax.broadcasted_iota(jnp.int32, (F, F), 1), 1.0, 0.0
    ).astype(BF16)

    def tile(slot, block, tau):
        at = (block * BT + tau) * 2
        one, two = place_ref[at], place_ref[at + 1]
        base = slot * SLOT
        first = got_ref[one + base]
        second = got_ref[jnp.maximum(two, 0) + base]
        return first + jnp.where(two >= 0, second, jnp.zeros_like(second))

    def emit(width):
        out_ref[:, :width] = lax.dot_general(
            eye, rows_ref[:width], (((1,), (1,)), ((), ())), preferred_element_type=F32
        ).astype(BF16)

    @pl.when(step < 8)
    def _():
        k = step // 4
        gk = jnp.where(k == 0, g[0], g[1])
        for seg in range(2):
            block = off_ref[seg] // 2048 + gk
            for j in range(8):
                u = (step % 4) * 8 + j
                for q in range(4):
                    r = j * 128 + seg * 64 + q * TILE
                    rows_ref[r : r + TILE] = tile(2 * seg + k, block, 4 * u + q)
        emit(WIDE)

    @pl.when(step == 8)
    def _():
        for seg in range(2):
            block = off_ref[2 + seg] // 2048
            for k in range(2):
                for q in range(16):
                    r = (seg * 2 + k) * 256 + q * TILE
                    rows_ref[r : r + TILE] = tile(4 + seg, block, g[k] * 16 + q)
        emit(WIDE)

    @pl.when(step == 9)
    def _():
        for j in range(4):
            rows_ref[j * TILE : (j + 1) * TILE] = dt_ref[3, j]
        emit(128)


def place(offsets, group_owner, got, dt):
    smem = pl.BlockSpec(memory_space=pltpu.SMEM)
    table = jnp.asarray(PLACE.reshape(-1))
    got = got.reshape(NT * 6 * SLOT, TILE, F)
    return pl.pallas_call(
        place_kernel,
        grid=(10,),
        out_shape=jax.ShapeDtypeStruct((F, 9280), BF16),
        in_specs=[
            smem,
            smem,
            smem,
            pl.BlockSpec((NT * 6 * SLOT, TILE, F), lambda i: (0, 0, 0)),
            pl.BlockSpec((NT, 4, TILE, F), lambda i: (0, 0, 0, 0)),
        ],
        out_specs=pl.BlockSpec((F, WIDE), lambda i: (0, i)),
        scratch_shapes=[pltpu.VMEM((WIDE, F), BF16)],
        compiler_params=pltpu.CompilerParams(vmem_limit_bytes=48 << 20),
        name="place",
    )(offsets, group_owner, table, got, dt)


def mix_heads(xh, bmat, cmat, dt_raw, rate, bias, skip):
    step = jax.nn.softplus(dt_raw + bias)
    cumul = jnp.cumsum(-rate * step, axis=1)
    diff = cumul[:, :, None, :] - cumul[:, None, :, :]
    length = xh.shape[1]
    lower = jnp.arange(length)[:, None] >= jnp.arange(length)[None, :]
    lower = lower[None, :, :, None]
    decay = jnp.where(lower, jnp.exp(jnp.where(lower, diff, 0.0)), 0.0)
    scores = jnp.einsum("sthn,suhn->stuh", cmat, bmat, precision=lax.Precision.HIGHEST)
    weights = scores * decay * step[:, None, :, :]
    out = jnp.einsum("stuh,suhp->sthp", weights, xh, precision=lax.Precision.HIGHEST)
    return out + skip[None, None, :, None] * xh


def shards(flat_weight, offsets, group_owner, hidden, decay_rate, dt_bias, skip_gain, norm_gain):
    n_data = lax.axis_size("dp")
    n_owner = lax.axis_size("tensor")
    rank_data = lax.axis_index("dp")
    rank_owner = lax.axis_index("tensor")
    group_heads = H // G
    locals_n = H // n_owner
    groups_n = G // n_owner
    dev_heads = locals_n // n_data
    got, dt_rows = exchange(prep(offsets, group_owner), flat_weight)
    w_local = place(offsets, group_owner, got, dt_rows)
    groups = jnp.nonzero(group_owner == rank_owner, size=groups_n)[0].astype(jnp.int32)
    zx_width = locals_n * 2 * P_SIZE
    tokens_n = hidden.shape[0]
    seqs_n = tokens_n // L
    first_head = rank_data * dev_heads
    proj = jnp.dot(hidden, w_local, preferred_element_type=jnp.float32)
    summed = lax.psum(proj, "dp")
    zx_mine = lax.dynamic_slice_in_dim(summed, first_head * 2 * P_SIZE, dev_heads * 2 * P_SIZE, 1)
    rest = summed[:, zx_width:]
    local_group = first_head // group_heads
    zx = zx_mine.reshape(seqs_n, L, dev_heads, 2, P_SIZE)
    gate = zx[:, :, :, 0, :]
    xh = zx[:, :, :, 1, :]
    bvec = lax.dynamic_slice_in_dim(rest, local_group * N, N, 1)
    cvec = lax.dynamic_slice_in_dim(rest, groups_n * N + local_group * N, N, 1)
    dt_raw = lax.dynamic_slice_in_dim(rest, 2 * groups_n * N + first_head, dev_heads, 1)
    bmat = jnp.broadcast_to(bvec.reshape(seqs_n, L, 1, N), (seqs_n, L, dev_heads, N))
    cmat = jnp.broadcast_to(cvec.reshape(seqs_n, L, 1, N), (seqs_n, L, dev_heads, N))
    heads = (
        groups[local_group] * group_heads
        + first_head % group_heads
        + jnp.arange(dev_heads, dtype=jnp.int32)
    )
    y = mix_heads(
        xh,
        bmat,
        cmat,
        dt_raw.reshape(seqs_n, L, dev_heads),
        decay_rate[heads],
        dt_bias[heads],
        skip_gain[heads],
    )
    v = y * jax.nn.silu(gate)
    squares = jnp.sum(v * v, axis=(2, 3)).reshape(tokens_n, 1)
    onehot = (jnp.arange(groups_n, dtype=jnp.int32)[None, :] == local_group).astype(jnp.float32)
    totals = lax.psum(squares * onehot, "dp")
    total_mine = lax.dynamic_slice_in_dim(totals, local_group, 1, 1)
    scale = lax.rsqrt(total_mine / (group_heads * P_SIZE) + 1e-05)
    gains = norm_gain.reshape(H, P_SIZE)[heads]
    normed = v.reshape(tokens_n, dev_heads, P_SIZE) * scale[:, :, None] * gains[None]
    return (w_local, normed.reshape(tokens_n, dev_heads * P_SIZE).astype(jnp.bfloat16))


def solution(mesh):
    placed = (P(("dp", "tensor"), None), P(), P(), P(None, "dp"), P(), P(), P(), P())
    return jax.shard_map(
        shards,
        mesh=mesh,
        in_specs=placed,
        out_specs=(P("dp", "tensor"), P(None, ("dp", "tensor"))),
        check_vma=False,
    )
```

```python
import functools

import jax
import jax.numpy as jnp
import numpy as np
from jax import lax
from jax.experimental import pallas as pl
from jax.experimental.pallas import tpu as pltpu
from jax.sharding import PartitionSpec as P

H = 256
P_SIZE = 64
N = 256
G = 8
L = 128
ROWS = 290
D = 8192
F = 256
NDP = 32
NT = 4
TILE = 16
CHUNK = 19
BLOCKS = 18
BT = 128
PARTS = (4, 5, 5, 5)
STARTS = (0, 4, 9, 14)
MESH = pl.DeviceIdType.MESH
BF16 = jnp.bfloat16
F32 = jnp.float32


def first_tile(chunk):
    return ROWS * chunk // TILE


def make_tables():
    n = len(PARTS)
    lo = np.full((n, NT, BLOCKS), 10**6)
    hi = np.full((n, NT, BLOCKS), -1)
    where = {}
    for k in range(NDP * NT):
        for l in range(CHUNK):
            p = max(i for i in range(n) if STARTS[i] <= l)
            b, tau = divmod(first_tile(k) + l, BT)
            if b >= BLOCKS:
                continue
            i = (k // NT) * PARTS[p] + l - STARTS[p]
            where.setdefault((b, tau), []).append((k % NT, p, i))
            lo[p, k % NT, b] = min(lo[p, k % NT, b], i)
            hi[p, k % NT, b] = max(hi[p, k % NT, b], i)
    caps = [int((hi[p] - lo[p] + 1).max()) for p in range(n)]
    start = np.zeros((n, NT, BLOCKS), np.int32)
    for p in range(n):
        start[p] = np.clip(lo[p], 0, NDP * PARTS[p] - caps[p])
    offs = np.concatenate([[0], np.cumsum(caps)])
    slot = int(offs[-1])
    place = np.full((BLOCKS, BT, 2), -1, np.int32)
    for (b, tau), found in where.items():
        for e, (t, p, i) in enumerate(found):
            place[b, tau, e] = t * 6 * slot + offs[p] + i - start[p, t, b]
    return caps, [int(o) for o in offs], slot, start, place


PICKS = 3
PT = 6 * PICKS + 1
ZERO2 = 2 * NDP
ZERO3 = NT * PT


def make_product_tables():
    pick = np.full((NT, 16, BLOCKS, PICKS), ZERO2, np.int32)
    merge = np.full((16, BLOCKS, 8, 2), -1, np.int32)
    count = np.zeros((NT, 16, BLOCKS), np.int32)
    seen = np.zeros((16, BLOCKS, 8), np.int32)
    for k in range(NDP * NT):
        for l in range(CHUNK):
            tile = first_tile(k) + l
            b, tau = divmod(tile, BT)
            if b >= BLOCKS:
                continue
            t, e, m = k % NT, tau % 16, tau // 16
            n = count[t, e, b]
            pick[t, e, b, n] = (k // NT) * 2 + l // 16
            merge[e, b, m, seen[e, b, m]] = t * PT + n
            count[t, e, b] += 1
            seen[e, b, m] += 1
    return pick, merge


CAPS, OFFS, SLOT, START, PLACE = make_tables()
PICK, MERGE = make_product_tables()
NP = len(PARTS)
W_DT = NP * 18
W_PICK = W_DT + 8
W_MERGE = W_PICK + 18 * PICKS
W_HEAD = W_MERGE + 72
W_SIZE = W_HEAD + 3


def dp_order():
    steps = [(a, b, c) for a in range(4) for b in range(4) for c in range(2) if (a, b, c) != (0, 0, 0)]
    steps.sort(key=lambda s: -(min(s[0], 4 - s[0]) + min(s[1], 4 - s[1])))
    out = []
    for a, b, c in steps:
        for q in ((a, b, c), (b, a, c), (-a % 4, -b % 4, c), (-b % 4, -a % 4, c)):
            if q not in out:
                out.append(q)
    return out[::-1]


ORDER = dp_order()


def dp_partner(d, step):
    x, y, c = d // 8, (d // 2) % 4, d % 2
    return ((x + step[0]) % 4) * 8 + ((y + step[1]) % 4) * 2 + (c + step[2]) % 2


def owner_groups(owner_ref, owner):
    first, last = jnp.int32(G), jnp.int32(-1)
    for g in range(G):
        mine = owner_ref[g] == owner
        first = jnp.where(mine, jnp.minimum(first, g), first)
        last = jnp.where(mine, g, last)
    return jnp.clip(first, 0, G - 1), jnp.clip(last, 0, G - 1)


def prep_kernel(off_ref, own_ref, start_ref, pick_ref, merge_ref, windows_ref):
    d = lax.axis_index("dp")
    t = lax.axis_index("tensor")
    e = d // 2
    seg = [off_ref[i] // 2048 for i in range(4)]

    def picks(at, b):
        for n in range(PICKS):
            windows_ref[at + n] = pick_ref[((t * 16 + e) * BLOCKS + b) * PICKS + n]

    for shift in range(NT):
        g = owner_groups(own_ref, (t + shift) % NT)
        for s in range(4):
            b = seg[s // 2] + g[s % 2]
            for p in range(NP):
                windows_ref[p * 18 + shift * 4 + s] = start_ref[(p * NT + t) * BLOCKS + b]
            picks(W_PICK + (shift * 4 + s) * PICKS, b)
        for i in range(2):
            windows_ref[W_DT + shift * 2 + i] = 2 * g[i]
    for i in range(2):
        for p in range(NP):
            windows_ref[p * 18 + 16 + i] = start_ref[(p * NT + t) * BLOCKS + seg[2 + i]]
        picks(W_PICK + (16 + i) * PICKS, seg[2 + i])

    def merged(at, b, m, slot):
        for n in range(2):
            v = merge_ref[((e * BLOCKS + b) * 8 + m) * 2 + n]
            windows_ref[at + n] = jnp.where(v < 0, ZERO3, v + PICKS * slot)

    g = owner_groups(own_ref, t)
    for s in range(4):
        for m in range(8):
            merged(W_MERGE + (s * 8 + m) * 2, seg[s // 2] + g[s % 2], m, s)
    for i in range(2):
        for k in range(2):
            merged(W_MERGE + 64 + (i * 2 + k) * 2, seg[2 + i], g[k], 4 + i)
    mine = jnp.where(d < 16, g[0], g[1])
    windows_ref[W_HEAD] = 2 * mine + (d % 16) // 8
    windows_ref[W_HEAD + 1] = 32 * mine + 2 * (d % 16)
    windows_ref[W_HEAD + 2] = 16 * mine + d % 16


def prep(offsets, group_owner):
    smem = pl.BlockSpec(memory_space=pltpu.SMEM)
    return pl.pallas_call(
        prep_kernel,
        out_shape=jax.ShapeDtypeStruct((W_SIZE,), jnp.int32),
        in_specs=[smem] * 5,
        out_specs=smem,
        name="prep",
    )(
        offsets,
        group_owner,
        jnp.asarray(START.reshape(-1)),
        jnp.asarray(PICK.reshape(-1)),
        jnp.asarray(MERGE.reshape(-1)),
    )


def iota(shape, dim):
    return lax.broadcasted_iota(jnp.int32, shape, dim)


def exchange_kernel(
    windows_ref, rate_ref, bias_ref, skip_ref, gain_ref, hidden_ref, flat_ref, out_ref, dt_ref, mixed_ref, *scratch
):
    shifted = scratch[:NP]
    recv = scratch[NP : 2 * NP]
    send = scratch[2 * NP : 3 * NP]
    both = scratch[3 * NP : 4 * NP]
    dtbuf, dtsend, dp_send, dp_recv, z_send, z_recv, self_sem = scratch[4 * NP : 4 * NP + 7]
    hid, prod, precv, zsend, zcom, zrecv, hsend, hrecv, bsend, brecv, qsend, qrecv = scratch[4 * NP + 7 : 4 * NP + 19]
    ag_send, ag_recv, p_send, p_recv, zp_send, zp_recv, own_sem = scratch[4 * NP + 19 :]
    d = lax.axis_index("dp")
    t = lax.axis_index("tensor")
    x, y, c = d // 8, (d // 2) % 4, d % 2
    e, seq = d // 2, d % 2
    chunk = d * NT + t

    barrier = pltpu.get_barrier_semaphore()

    @pl.loop(1, NDP)
    def _(i):
        pl.semaphore_signal(barrier, inc=1, device_id=((d + i) % NDP, t), device_id_type=MESH)

    @pl.loop(1, NT)
    def _(i):
        pl.semaphore_signal(barrier, inc=1, device_id=(d, (t + i) % NT), device_id_type=MESH)

    pl.semaphore_wait(barrier, NDP - 1 + NT - 1)

    def remote(src, dst, ssem, rsem, device):
        cp = pltpu.make_async_remote_copy(
            src_ref=src, dst_ref=dst, send_sem=ssem, recv_sem=rsem, device_id=device, device_id_type=MESH
        )
        cp.start()
        return cp

    def await_bytes(ref, sem):
        pltpu.make_async_copy(ref, ref, sem).wait()

    copies = []

    phase = (ROWS * chunk) % TILE

    def shift_part(p):
        a, rows = STARTS[p] * TILE, PARTS[p] * TILE
        w0, w1 = max(a - TILE, 0), min(a + rows, ROWS)
        pick = jnp.where(iota((rows, w1 - w0), 0) + (a - phase) == iota((rows, w1 - w0), 1) + w0, 1.0, 0.0)
        pick = pick.astype(BF16)

        @pl.loop(0, D // 1024)
        def _(i):
            cols = pl.ds(pl.multiple_of(i * 1024, 1024), 1024)
            moved = jnp.dot(pick, flat_ref[w0:w1, cols], preferred_element_type=F32)
            shifted[p][:, :, cols] = moved.astype(BF16).reshape(PARTS[p], TILE, 1024)

    def send_part(p):
        mine = pl.ds(d * PARTS[p], PARTS[p])
        for step in ORDER:
            peer = dp_partner(d, step)
            remote(
                shifted[p].at[:, :, pl.ds(pl.multiple_of(peer * F, F), F)],
                recv[p].at[mine],
                dp_send.at[p],
                dp_recv.at[p],
                (peer, t),
            )
        pltpu.make_async_copy(
            shifted[p].at[:, :, pl.ds(pl.multiple_of(d * F, F), F)], recv[p].at[mine], dp_recv.at[p]
        ).start()

    def forward_part(p):
        await_bytes(recv[p], dp_recv.at[p])

        def pack(dst, window):
            first = windows_ref[window]

            @pl.loop(0, CAPS[p], unroll=2)
            def _(j):
                dst[j] = recv[p][first + j]

        for i in range(2):
            pack(both[p].at[i], p * 18 + 16 + i)
        for l in range(max(STARTS[p], 3), STARTS[p] + PARTS[p]):
            dtbuf[l - 3] = recv[p][31 * PARTS[p] + l - STARTS[p]]
        for shift in (1, 3, 2, 0):
            for s in range(4):
                pack(send[p].at[shift, s], p * 18 + shift * 4 + s)
            span = pl.ds(OFFS[p], CAPS[p])
            pairs = [(send[p].at[shift], out_ref.at[t, 0:4, span]), (both[p], out_ref.at[t, 4:6, span])]
            for n, (src, dst) in enumerate(pairs):
                if shift == 0:
                    cp = pltpu.make_async_copy(src, dst, self_sem.at[2 * p + n])
                    cp.start()
                else:
                    cp = remote(
                        src,
                        dst,
                        z_send.at[shift - 1, 2 * p + n],
                        z_recv.at[shift - 1, 2 * p + n],
                        (d, (t + shift) % NT),
                    )
                copies.append(cp)

    def forward_dt():
        for shift in (1, 3, 2, 0):
            for i in range(2):
                for j in range(2):
                    dtsend[shift, 2 * i + j] = dtbuf[windows_ref[W_DT + shift * 2 + i] + j]
            if shift == 0:
                cp = pltpu.make_async_copy(dtsend.at[0], dt_ref.at[t], self_sem.at[2 * NP])
                cp.start()
            else:
                cp = remote(
                    dtsend.at[shift],
                    dt_ref.at[t],
                    z_send.at[shift - 1, 2 * NP],
                    z_recv.at[shift - 1, 2 * NP],
                    (d, (t + shift) % NT),
                )
            copies.append(cp)

    def along_x(i):
        return (((x + i) % 4) * 8 + y * 2 + c, t)

    def along_y(i):
        return (x * 8 + ((y + i) % 4) * 2 + c, t)

    def gather_first():
        own = pltpu.make_async_copy(hidden_ref, hid.at[x, y, c], own_sem.at[0])
        own.start()
        for i in (1, 3, 2):
            remote(hidden_ref.at[0:L], hid.at[x, y, c, 0:L], ag_send.at[0], ag_recv.at[0], along_x(i))
            remote(hidden_ref.at[L:], hid.at[x, y, c, L:], ag_send.at[1], ag_recv.at[1], along_y(i))
        own.wait()

    def gather_second():
        await_bytes(hid.at[0:3, 0, 0, 0:L], ag_recv.at[0])
        for i in (1, 3, 2):
            remote(hid.at[:, y, c, 0:L], hid.at[:, y, c, 0:L], ag_send.at[2], ag_recv.at[2], along_y(i))
        await_bytes(hid.at[0:3, 0, 0, L:], ag_recv.at[1])
        for i in (1, 3, 2):
            remote(hid.at[x, :, c, L:], hid.at[x, :, c, L:], ag_send.at[3], ag_recv.at[3], along_x(i))

    def gather_third():
        await_bytes(hid.at[0:3, :, 0, 0:L], ag_recv.at[2])
        await_bytes(hid.at[0:3, :, 0, L:], ag_recv.at[3])
        remote(hid.at[:, :, c], hid.at[:, :, c], ag_send.at[4], ag_recv.at[4], (d + 1 - 2 * c, t))
        await_bytes(hid.at[:, :, 0], ag_recv.at[4])

    def multiply():
        prod[...] = jnp.zeros_like(prod)

        @pl.loop(0, NDP)
        def _(i):
            cols = pl.ds(pl.multiple_of(i * F, F), F)
            rows = jnp.concatenate(
                [shifted[p][:, :, cols].reshape(PARTS[p] * TILE, F) for p in range(NP)], axis=0
            )
            part = lax.dot_general(
                rows, hid[i // 8, (i // 2) % 4, i % 2], (((1,), (1,)), ((), ())), preferred_element_type=F32
            )
            for s in range(2):
                prod[s, 0:CHUNK] += part[:, s * L : (s + 1) * L].reshape(CHUNK, TILE, L)

    def product_tiles(i):
        low = (i // 2 + 16 * NDP * NT * CHUNK - first_tile(chunk)) % 16
        return low, i % 2

    def send_products():
        @pl.loop(1, NDP)
        def _(n):
            i = (d + n) % NDP
            low, s = product_tiles(i)
            for h in range(2):
                remote(prod.at[s, low + 16 * h], precv.at[2 * d + h], p_send.at[0], p_recv.at[0], (i, t))

        low, s = product_tiles(d)
        for h in range(2):
            pltpu.make_async_copy(prod.at[s, low + 16 * h], precv.at[2 * d + h], p_recv.at[0]).start()

    def forward_products():
        await_bytes(precv.at[0 : 2 * NDP], p_recv.at[0])
        for n in range(2 * PICKS):
            zcom[n] = precv[windows_ref[W_PICK + 16 * PICKS + n]]
        zcom[2 * PICKS] = precv[2 * 31 + (3 + e) // 16]
        for shift in (1, 3, 2, 0):
            for n in range(4 * PICKS):
                zsend[shift, n] = precv[windows_ref[W_PICK + shift * 4 * PICKS + n]]
            for j, (src, n0, n1) in enumerate([(zsend.at[shift], 0, 4 * PICKS), (zcom, 4 * PICKS, PT)]):
                dst = zrecv.at[pl.ds(t * PT + n0, n1 - n0)]
                if shift == 0:
                    cp = pltpu.make_async_copy(src, dst, own_sem.at[1 + j])
                    cp.start()
                else:
                    cp = remote(src, dst, zp_send.at[shift - 1, j], zp_recv.at[shift - 1, j], (d, (t + shift) % NT))
                pcopies.append(cp)

    pcopies = []

    def send_heads():
        for cp in pcopies:
            cp.wait()

        def total(at):
            return zrecv[windows_ref[at]] + zrecv[windows_ref[at + 1]]

        for k in range(2):
            for i in range(2):
                bsend[k, i] = total(W_MERGE + 64 + (i * 2 + k) * 2)
            bsend[k, 2] = zrecv[3 * PT + PT - 1]
        for k in range(2):
            for m in range(8):
                for i in range(2):
                    hsend[k * 8 + m, i] = total(W_MERGE + ((2 * i + k) * 8 + m) * 2)

        @pl.loop(1, NDP)
        def _(n):
            i = (d + n) % NDP
            remote(bsend.at[i // 16], brecv.at[seq, :, e], p_send.at[1], p_recv.at[1], (i, t))

        pltpu.make_async_copy(bsend.at[d // 16], brecv.at[seq, :, e], p_recv.at[1]).start()

        @pl.loop(0, 16)
        def _(n):
            i = 16 * (n // 8) + 2 * (n % 8) + e // 8
            dst = hrecv.at[seq, :, (e // 4) % 2, e % 4]

            @pl.when(i != d)
            def _():
                remote(hsend.at[n], dst, p_send.at[2], p_recv.at[2], (i, t))

            @pl.when(i == d)
            def _():
                pltpu.make_async_copy(hsend.at[n], dst, p_recv.at[2]).start()

    high = lax.Precision.HIGHEST
    values = []

    def mix():
        await_bytes(brecv, p_recv.at[1])
        await_bytes(hrecv, p_recv.at[2])
        head = windows_ref[W_HEAD + 1]
        lower = iota((L, L), 0) <= iota((L, L), 1)
        ones = jnp.where(lower, 1.0, 0.0).astype(F32)
        qsend[...] = jnp.zeros_like(qsend)
        for s in range(2):
            bmat = brecv[s, 0].reshape(N, L)
            cmat = brecv[s, 1].reshape(N, L)
            scores = lax.dot_general(bmat, cmat, (((0,), (0,)), ((), ())), precision=high, preferred_element_type=F32)
            raw = brecv[s, 2, windows_ref[W_HEAD]]
            squares = jnp.zeros((1, L), F32)
            for hh in range(2):
                r = 2 * (d % 8) + hh
                row = jnp.sum(jnp.where(iota((TILE, L), 0) == r, raw, 0.0), axis=0, keepdims=True)
                row = row + bias_ref[head + hh]
                step = jnp.maximum(row, 0.0) + jnp.log1p(jnp.exp(-jnp.abs(row)))
                rates = jnp.broadcast_to(step * -rate_ref[head + hh], (8, L))
                cumul = jnp.dot(rates, ones, precision=high, preferred_element_type=F32)
                across = jnp.broadcast_to(cumul[0:1], (L, L))
                diff = across - across.T
                decay = jnp.where(lower, jnp.exp(jnp.where(lower, diff, 0.0)), 0.0)
                weights = scores * decay * jnp.broadcast_to(step, (L, L)).T
                xt = hrecv[s, 1, hh].reshape(P_SIZE, L)
                zt = hrecv[s, 0, hh].reshape(P_SIZE, L)
                out = jnp.dot(xt, weights, precision=high, preferred_element_type=F32) + skip_ref[head + hh] * xt
                v = out * (zt * jax.nn.sigmoid(zt))
                squares = squares + jnp.sum(v * v, axis=0, keepdims=True)
                values.append(v)
            qsend[s : s + 1] = squares
        base = 16 * (d // 16)

        @pl.loop(1, 16)
        def _(n):
            i = base + (d + n) % 16
            remote(qsend, qrecv.at[d % 16], p_send.at[3], p_recv.at[3], (i, t))

        pltpu.make_async_copy(qsend, qrecv.at[d % 16], p_recv.at[3]).start()

    def finish():
        await_bytes(qrecv, p_recv.at[3])
        total = jnp.sum(qrecv[...], axis=0)
        scale = lax.rsqrt(total / (32 * P_SIZE) + 1e-05)
        gain = gain_ref[windows_ref[W_HEAD + 2]]
        for s in range(2):
            v = jnp.concatenate(values[2 * s : 2 * s + 2], axis=0) * scale[s : s + 1]
            mixed_ref[s * L : (s + 1) * L] = (v.T * gain).astype(BF16)

    zero = jnp.zeros((TILE, L), F32)
    precv[ZERO2] = zero
    zrecv[ZERO3] = zero
    shift_part(0)
    send_part(0)
    gather_first()
    shift_part(1)
    send_part(1)
    shift_part(2)
    shift_part(3)
    gather_second()
    forward_part(0)
    send_part(2)
    gather_third()
    multiply()
    send_products()
    forward_part(1)
    send_part(3)
    forward_products()
    forward_part(2)
    send_heads()
    forward_part(3)
    forward_dt()
    mix()
    finish()

    for cp in copies:
        cp.wait()
    for p in range(NP):
        await_bytes(shifted[p].at[:, :, 0 : (NDP - 1) * F], dp_send.at[p])
    await_bytes(hid.at[0:3, 0, 0, 0:L], ag_send.at[0])
    await_bytes(hid.at[0:3, 0, 0, L:], ag_send.at[1])
    await_bytes(hid.at[0:3, :, 0, 0:L], ag_send.at[2])
    await_bytes(hid.at[0:3, :, 0, L:], ag_send.at[3])
    await_bytes(hid.at[:, :, 0], ag_send.at[4])
    await_bytes(precv.at[0 : 2 * (NDP - 1)], p_send.at[0])
    await_bytes(brecv.at[0, :, 0:16], p_send.at[1])
    await_bytes(brecv.at[1, :, 0:15], p_send.at[1])
    itself = seq == e // 8

    @pl.when(itself)
    def _():
        await_bytes(hsend.at[0:15], p_send.at[2])

    @pl.when(jnp.logical_not(itself))
    def _():
        await_bytes(hsend, p_send.at[2])

    await_bytes(qrecv.at[0:15], p_send.at[3])


def exchange(windows, rate, bias, skip, gain, hidden, flat):
    any_ = pl.BlockSpec(memory_space=pl.ANY)
    smem = pl.BlockSpec(memory_space=pltpu.SMEM)
    vmem = pl.BlockSpec(memory_space=pltpu.VMEM)
    dma = pltpu.SemaphoreType.DMA
    return pl.pallas_call(
        exchange_kernel,
        out_shape=(
            jax.ShapeDtypeStruct((NT, 6, SLOT, TILE, F), BF16),
            jax.ShapeDtypeStruct((NT, 4, TILE, F), BF16),
            jax.ShapeDtypeStruct((2 * L, L), BF16),
        ),
        in_specs=[smem, smem, smem, smem, vmem, vmem, vmem],
        out_specs=(any_, any_, vmem),
        scratch_shapes=[pltpu.VMEM((w, TILE, D), BF16) for w in PARTS]
        + [pltpu.VMEM((NDP * w, TILE, F), BF16) for w in PARTS]
        + [pltpu.VMEM((NT, 4, c, TILE, F), BF16) for c in CAPS]
        + [pltpu.VMEM((2, c, TILE, F), BF16) for c in CAPS]
        + [
            pltpu.VMEM((16, TILE, F), BF16),
            pltpu.VMEM((NT, 4, TILE, F), BF16),
            dma((NP,)),
            dma((NP,)),
            dma((NT - 1, 2 * NP + 1)),
            dma((NT - 1, 2 * NP + 1)),
            dma((2 * NP + 1,)),
            pltpu.VMEM((4, 4, 2, 2 * L, F), BF16),
            pltpu.VMEM((2, 32, TILE, L), F32),
            pltpu.VMEM((ZERO2 + 1, TILE, L), F32),
            pltpu.VMEM((NT, 4 * PICKS, TILE, L), F32),
            pltpu.VMEM((2 * PICKS + 1, TILE, L), F32),
            pltpu.VMEM((ZERO3 + 1, TILE, L), F32),
            pltpu.VMEM((16, 2, TILE, L), F32),
            pltpu.VMEM((2, 2, 2, 4, TILE, L), F32),
            pltpu.VMEM((2, 3, TILE, L), F32),
            pltpu.VMEM((2, 3, 16, TILE, L), F32),
            pltpu.VMEM((8, L), F32),
            pltpu.VMEM((16, 8, L), F32),
            dma((5,)),
            dma((5,)),
            dma((4,)),
            dma((4,)),
            dma((NT - 1, 2)),
            dma((NT - 1, 2)),
            dma((3,)),
        ],
        compiler_params=pltpu.CompilerParams(
            collective_id=1, has_side_effects=True, vmem_limit_bytes=56 << 20
        ),
        name="exchange",
    )(windows, rate, bias, skip, gain, hidden, flat)


WIDE = 1024


def place_kernel(off_ref, own_ref, place_ref, got_ref, dt_ref, out_ref, rows_ref):
    step = pl.program_id(0)
    g = owner_groups(own_ref, lax.axis_index("tensor"))
    eye = jnp.where(
        lax.broadcasted_iota(jnp.int32, (F, F), 0) == lax.broadcasted_iota(jnp.int32, (F, F), 1), 1.0, 0.0
    ).astype(BF16)

    def tile(slot, block, tau):
        at = (block * BT + tau) * 2
        one, two = place_ref[at], place_ref[at + 1]
        base = slot * SLOT
        first = got_ref[one + base]
        second = got_ref[jnp.maximum(two, 0) + base]
        return first + jnp.where(two >= 0, second, jnp.zeros_like(second))

    def emit(width):
        out_ref[:, :width] = lax.dot_general(
            eye, rows_ref[:width], (((1,), (1,)), ((), ())), preferred_element_type=F32
        ).astype(BF16)

    @pl.when(step < 8)
    def _():
        k = step // 4
        gk = jnp.where(k == 0, g[0], g[1])
        for seg in range(2):
            block = off_ref[seg] // 2048 + gk
            for j in range(8):
                u = (step % 4) * 8 + j
                for q in range(4):
                    r = j * 128 + seg * 64 + q * TILE
                    rows_ref[r : r + TILE] = tile(2 * seg + k, block, 4 * u + q)
        emit(WIDE)

    @pl.when(step == 8)
    def _():
        for seg in range(2):
            block = off_ref[2 + seg] // 2048
            for k in range(2):
                for q in range(16):
                    r = (seg * 2 + k) * 256 + q * TILE
                    rows_ref[r : r + TILE] = tile(4 + seg, block, g[k] * 16 + q)
        emit(WIDE)

    @pl.when(step == 9)
    def _():
        for j in range(4):
            rows_ref[j * TILE : (j + 1) * TILE] = dt_ref[3, j]
        emit(128)


def place(offsets, group_owner, got, dt):
    smem = pl.BlockSpec(memory_space=pltpu.SMEM)
    table = jnp.asarray(PLACE.reshape(-1))
    got = got.reshape(NT * 6 * SLOT, TILE, F)
    return pl.pallas_call(
        place_kernel,
        grid=(10,),
        out_shape=jax.ShapeDtypeStruct((F, 9280), BF16),
        in_specs=[
            smem,
            smem,
            smem,
            pl.BlockSpec((NT * 6 * SLOT, TILE, F), lambda i: (0, 0, 0)),
            pl.BlockSpec((NT, 4, TILE, F), lambda i: (0, 0, 0, 0)),
        ],
        out_specs=pl.BlockSpec((F, WIDE), lambda i: (0, i)),
        scratch_shapes=[pltpu.VMEM((WIDE, F), BF16)],
        compiler_params=pltpu.CompilerParams(vmem_limit_bytes=48 << 20),
        name="place",
    )(offsets, group_owner, table, got, dt)


def shards(flat_weight, offsets, group_owner, hidden, decay_rate, dt_bias, skip_gain, norm_gain):
    windows = prep(offsets, group_owner)
    gain = norm_gain.reshape(H // 2, 1, 2 * P_SIZE)
    got, dt_rows, mixed = exchange(windows, decay_rate, dt_bias, skip_gain, gain, hidden, flat_weight)
    return place(offsets, group_owner, got, dt_rows), mixed


def solution(mesh):
    placed = (P(("dp", "tensor"), None), P(), P(), P(None, "dp"), P(), P(), P(), P())
    return jax.shard_map(
        shards,
        mesh=mesh,
        in_specs=placed,
        out_specs=(P("dp", "tensor"), P(None, ("dp", "tensor"))),
        check_vma=False,
    )
```

```python
import functools

import jax
import jax.numpy as jnp
import numpy as np
from jax import lax
from jax.experimental import pallas as pl
from jax.experimental.pallas import tpu as pltpu
from jax.sharding import PartitionSpec as P

H = 256
P_SIZE = 64
N = 256
G = 8
L = 128
ROWS = 290
D = 8192
F = 256
NDP = 32
NT = 4
TILE = 16
CHUNK = 19
BLOCKS = 18
BT = 128
PARTS = (4, 5, 5, 5)
STARTS = (0, 4, 9, 14)
MESH = pl.DeviceIdType.MESH
BF16 = jnp.bfloat16
F32 = jnp.float32


def first_tile(chunk):
    return ROWS * chunk // TILE


def make_tables():
    n = len(PARTS)
    lo = np.full((n, NT, BLOCKS), 10**6)
    hi = np.full((n, NT, BLOCKS), -1)
    where = {}
    for k in range(NDP * NT):
        for l in range(CHUNK):
            p = max(i for i in range(n) if STARTS[i] <= l)
            b, tau = divmod(first_tile(k) + l, BT)
            if b >= BLOCKS:
                continue
            i = (k // NT) * PARTS[p] + l - STARTS[p]
            where.setdefault((b, tau), []).append((k % NT, p, i))
            lo[p, k % NT, b] = min(lo[p, k % NT, b], i)
            hi[p, k % NT, b] = max(hi[p, k % NT, b], i)
    caps = [int((hi[p] - lo[p] + 1).max()) for p in range(n)]
    start = np.zeros((n, NT, BLOCKS), np.int32)
    for p in range(n):
        start[p] = np.clip(lo[p], 0, NDP * PARTS[p] - caps[p])
    offs = np.concatenate([[0], np.cumsum(caps)])
    slot = int(offs[-1])
    place = np.full((BLOCKS, BT, 2), -1, np.int32)
    for (b, tau), found in where.items():
        for e, (t, p, i) in enumerate(found):
            place[b, tau, e] = t * 6 * slot + offs[p] + i - start[p, t, b]
    return caps, [int(o) for o in offs], slot, start, place


PICKS = 3
PT = 6 * PICKS + 1
ZERO2 = 2 * NDP
ZERO3 = NT * PT


def make_product_tables():
    pick = np.full((NT, 16, BLOCKS, PICKS), ZERO2, np.int32)
    merge = np.full((16, BLOCKS, 8, 2), -1, np.int32)
    count = np.zeros((NT, 16, BLOCKS), np.int32)
    seen = np.zeros((16, BLOCKS, 8), np.int32)
    for k in range(NDP * NT):
        for l in range(CHUNK):
            tile = first_tile(k) + l
            b, tau = divmod(tile, BT)
            if b >= BLOCKS:
                continue
            t, e, m = k % NT, tau % 16, tau // 16
            n = count[t, e, b]
            pick[t, e, b, n] = (k // NT) * 2 + l // 16
            merge[e, b, m, seen[e, b, m]] = t * PT + n
            count[t, e, b] += 1
            seen[e, b, m] += 1
    return pick, merge


CAPS, OFFS, SLOT, START, PLACE = make_tables()
PICK, MERGE = make_product_tables()
NP = len(PARTS)
W_DT = NP * 18
W_PICK = W_DT + 8
W_MERGE = W_PICK + 18 * PICKS
W_HEAD = W_MERGE + 72
W_SIZE = W_HEAD + 3


def dp_order():
    steps = [(a, b, c) for a in range(4) for b in range(4) for c in range(2) if (a, b, c) != (0, 0, 0)]
    steps.sort(key=lambda s: -(min(s[0], 4 - s[0]) + min(s[1], 4 - s[1])))
    out = []
    for a, b, c in steps:
        for q in ((a, b, c), (b, a, c), (-a % 4, -b % 4, c), (-b % 4, -a % 4, c)):
            if q not in out:
                out.append(q)
    return out[::-1]


ORDER = dp_order()


def dp_partner(d, step):
    x, y, c = d // 8, (d // 2) % 4, d % 2
    return ((x + step[0]) % 4) * 8 + ((y + step[1]) % 4) * 2 + (c + step[2]) % 2


def owner_groups(owner_ref, owner):
    first, last = jnp.int32(G), jnp.int32(-1)
    for g in range(G):
        mine = owner_ref[g] == owner
        first = jnp.where(mine, jnp.minimum(first, g), first)
        last = jnp.where(mine, g, last)
    return jnp.clip(first, 0, G - 1), jnp.clip(last, 0, G - 1)


def prep_kernel(off_ref, own_ref, start_ref, pick_ref, merge_ref, windows_ref):
    d = lax.axis_index("dp")
    t = lax.axis_index("tensor")
    e = d // 2
    seg = [off_ref[i] // 2048 for i in range(4)]

    def picks(at, b):
        for n in range(PICKS):
            windows_ref[at + n] = pick_ref[((t * 16 + e) * BLOCKS + b) * PICKS + n]

    for shift in range(NT):
        g = owner_groups(own_ref, (t + shift) % NT)
        for s in range(4):
            b = seg[s // 2] + g[s % 2]
            for p in range(NP):
                windows_ref[p * 18 + shift * 4 + s] = start_ref[(p * NT + t) * BLOCKS + b]
            picks(W_PICK + (shift * 4 + s) * PICKS, b)
        for i in range(2):
            windows_ref[W_DT + shift * 2 + i] = 2 * g[i]
    for i in range(2):
        for p in range(NP):
            windows_ref[p * 18 + 16 + i] = start_ref[(p * NT + t) * BLOCKS + seg[2 + i]]
        picks(W_PICK + (16 + i) * PICKS, seg[2 + i])

    def merged(at, b, m, slot):
        for n in range(2):
            v = merge_ref[((e * BLOCKS + b) * 8 + m) * 2 + n]
            windows_ref[at + n] = jnp.where(v < 0, ZERO3, v + PICKS * slot)

    g = owner_groups(own_ref, t)
    for s in range(4):
        for m in range(8):
            merged(W_MERGE + (s * 8 + m) * 2, seg[s // 2] + g[s % 2], m, s)
    for i in range(2):
        for k in range(2):
            merged(W_MERGE + 64 + (i * 2 + k) * 2, seg[2 + i], g[k], 4 + i)
    mine = jnp.where(d < 16, g[0], g[1])
    windows_ref[W_HEAD] = 2 * mine + (d % 16) // 8
    windows_ref[W_HEAD + 1] = 32 * mine + 2 * (d % 16)
    windows_ref[W_HEAD + 2] = 16 * mine + d % 16


def prep(offsets, group_owner):
    smem = pl.BlockSpec(memory_space=pltpu.SMEM)
    return pl.pallas_call(
        prep_kernel,
        out_shape=jax.ShapeDtypeStruct((W_SIZE,), jnp.int32),
        in_specs=[smem] * 5,
        out_specs=smem,
        name="prep",
    )(
        offsets,
        group_owner,
        jnp.asarray(START.reshape(-1)),
        jnp.asarray(PICK.reshape(-1)),
        jnp.asarray(MERGE.reshape(-1)),
    )


def iota(shape, dim):
    return lax.broadcasted_iota(jnp.int32, shape, dim)


def exchange_kernel(
    windows_ref, rate_ref, bias_ref, skip_ref, gain_ref, hidden_ref, flat_ref, out_ref, dt_ref, mixed_ref, *scratch
):
    shifted = scratch[:NP]
    recv = scratch[NP : 2 * NP]
    send = scratch[2 * NP : 3 * NP]
    both = scratch[3 * NP : 4 * NP]
    dtbuf, dtsend, dp_send, dp_recv, z_send, z_recv, self_sem = scratch[4 * NP : 4 * NP + 7]
    hid, prod, precv, zsend, zcom, zrecv, hsend, hrecv, bsend, brecv, qsend, qrecv = scratch[4 * NP + 7 : 4 * NP + 19]
    ag_send, ag_recv, p_send, p_recv, zp_send, zp_recv, own_sem = scratch[4 * NP + 19 :]
    d = lax.axis_index("dp")
    t = lax.axis_index("tensor")
    x, y, c = d // 8, (d // 2) % 4, d % 2
    e, seq = d // 2, d % 2
    chunk = d * NT + t

    barrier = pltpu.get_barrier_semaphore()

    @pl.loop(1, NDP)
    def _(i):
        pl.semaphore_signal(barrier, inc=1, device_id=((d + i) % NDP, t), device_id_type=MESH)

    @pl.loop(1, NT)
    def _(i):
        pl.semaphore_signal(barrier, inc=1, device_id=(d, (t + i) % NT), device_id_type=MESH)

    pl.semaphore_wait(barrier, NDP - 1 + NT - 1)

    def remote(src, dst, ssem, rsem, device):
        cp = pltpu.make_async_remote_copy(
            src_ref=src, dst_ref=dst, send_sem=ssem, recv_sem=rsem, device_id=device, device_id_type=MESH
        )
        cp.start()
        return cp

    def await_bytes(ref, sem):
        pltpu.make_async_copy(ref, ref, sem).wait()

    copies = []

    phase = (ROWS * chunk) % TILE

    def shift_part(p):
        a, rows = STARTS[p] * TILE, PARTS[p] * TILE
        w0, w1 = max(a - TILE, 0), min(a + rows, ROWS)
        pick = jnp.where(iota((rows, w1 - w0), 0) + (a - phase) == iota((rows, w1 - w0), 1) + w0, 1.0, 0.0)
        pick = pick.astype(BF16)

        @pl.loop(0, D // 1024)
        def _(i):
            cols = pl.ds(pl.multiple_of(i * 1024, 1024), 1024)
            moved = jnp.dot(pick, flat_ref[w0:w1, cols], preferred_element_type=F32)
            shifted[p][:, :, cols] = moved.astype(BF16).reshape(PARTS[p], TILE, 1024)

    def send_part(p):
        mine = pl.ds(d * PARTS[p], PARTS[p])
        for step in ORDER:
            peer = dp_partner(d, step)
            remote(
                shifted[p].at[:, :, pl.ds(pl.multiple_of(peer * F, F), F)],
                recv[p].at[mine],
                dp_send.at[p],
                dp_recv.at[p],
                (peer, t),
            )
        pltpu.make_async_copy(
            shifted[p].at[:, :, pl.ds(pl.multiple_of(d * F, F), F)], recv[p].at[mine], dp_recv.at[p]
        ).start()

    def forward_part(p):
        await_bytes(recv[p], dp_recv.at[p])

        def pack(dst, window):
            first = windows_ref[window]

            @pl.loop(0, CAPS[p], unroll=2)
            def _(j):
                dst[j] = recv[p][first + j]

        for i in range(2):
            pack(both[p].at[i], p * 18 + 16 + i)
        for l in range(max(STARTS[p], 3), STARTS[p] + PARTS[p]):
            dtbuf[l - 3] = recv[p][31 * PARTS[p] + l - STARTS[p]]
        for shift in (1, 3, 2, 0):
            for s in range(4):
                pack(send[p].at[shift, s], p * 18 + shift * 4 + s)
            span = pl.ds(OFFS[p], CAPS[p])
            pairs = [(send[p].at[shift], out_ref.at[t, 0:4, span]), (both[p], out_ref.at[t, 4:6, span])]
            for n, (src, dst) in enumerate(pairs):
                if shift == 0:
                    cp = pltpu.make_async_copy(src, dst, self_sem.at[2 * p + n])
                    cp.start()
                else:
                    cp = remote(
                        src,
                        dst,
                        z_send.at[shift - 1, 2 * p + n],
                        z_recv.at[shift - 1, 2 * p + n],
                        (d, (t + shift) % NT),
                    )
                copies.append(cp)

    def forward_dt():
        for shift in (1, 3, 2, 0):
            for i in range(2):
                for j in range(2):
                    dtsend[shift, 2 * i + j] = dtbuf[windows_ref[W_DT + shift * 2 + i] + j]
            if shift == 0:
                cp = pltpu.make_async_copy(dtsend.at[0], dt_ref.at[t], self_sem.at[2 * NP])
                cp.start()
            else:
                cp = remote(
                    dtsend.at[shift],
                    dt_ref.at[t],
                    z_send.at[shift - 1, 2 * NP],
                    z_recv.at[shift - 1, 2 * NP],
                    (d, (t + shift) % NT),
                )
            copies.append(cp)

    def along_x(i):
        return (((x + i) % 4) * 8 + y * 2 + c, t)

    def along_y(i):
        return (x * 8 + ((y + i) % 4) * 2 + c, t)

    def gather_first():
        own = pltpu.make_async_copy(hidden_ref, hid.at[x, y, c], own_sem.at[0])
        own.start()
        for i in (1, 3, 2):
            remote(hidden_ref.at[0:L], hid.at[x, y, c, 0:L], ag_send.at[0], ag_recv.at[0], along_x(i))
            remote(hidden_ref.at[L:], hid.at[x, y, c, L:], ag_send.at[1], ag_recv.at[1], along_y(i))
        own.wait()

    def gather_second():
        await_bytes(hid.at[0:3, 0, 0, 0:L], ag_recv.at[0])
        for i in (1, 3, 2):
            remote(hid.at[:, y, c, 0:L], hid.at[:, y, c, 0:L], ag_send.at[2], ag_recv.at[2], along_y(i))
        await_bytes(hid.at[0:3, 0, 0, L:], ag_recv.at[1])
        for i in (1, 3, 2):
            remote(hid.at[x, :, c, L:], hid.at[x, :, c, L:], ag_send.at[3], ag_recv.at[3], along_x(i))

    def gather_third():
        await_bytes(hid.at[0:3, :, 0, 0:L], ag_recv.at[2])
        await_bytes(hid.at[0:3, :, 0, L:], ag_recv.at[3])
        remote(hid.at[:, :, c], hid.at[:, :, c], ag_send.at[4], ag_recv.at[4], (d + 1 - 2 * c, t))
        await_bytes(hid.at[:, :, 0], ag_recv.at[4])

    def multiply():
        prod[...] = jnp.zeros_like(prod)

        @pl.loop(0, NDP)
        def _(i):
            cols = pl.ds(pl.multiple_of(i * F, F), F)
            rows = jnp.concatenate(
                [shifted[p][:, :, cols].reshape(PARTS[p] * TILE, F) for p in range(NP)], axis=0
            )
            part = lax.dot_general(
                rows, hid[i // 8, (i // 2) % 4, i % 2], (((1,), (1,)), ((), ())), preferred_element_type=F32
            )
            for s in range(2):
                prod[s, 0:CHUNK] += part[:, s * L : (s + 1) * L].reshape(CHUNK, TILE, L)

    def product_tiles(i):
        low = (i // 2 + 16 * NDP * NT * CHUNK - first_tile(chunk)) % 16
        return low, i % 2

    def send_products():
        @pl.loop(1, NDP)
        def _(n):
            i = (d + n) % NDP
            low, s = product_tiles(i)
            for h in range(2):
                remote(prod.at[s, low + 16 * h], precv.at[2 * d + h], p_send.at[0], p_recv.at[0], (i, t))

        low, s = product_tiles(d)
        for h in range(2):
            pltpu.make_async_copy(prod.at[s, low + 16 * h], precv.at[2 * d + h], p_recv.at[0]).start()

    def forward_products():
        await_bytes(precv.at[0 : 2 * NDP], p_recv.at[0])
        for n in range(2 * PICKS):
            zcom[n] = precv[windows_ref[W_PICK + 16 * PICKS + n]]
        zcom[2 * PICKS] = precv[2 * 31 + (3 + e) // 16]
        for shift in (1, 3, 2, 0):
            for n in range(4 * PICKS):
                zsend[shift, n] = precv[windows_ref[W_PICK + shift * 4 * PICKS + n]]
            for j, (src, n0, n1) in enumerate([(zsend.at[shift], 0, 4 * PICKS), (zcom, 4 * PICKS, PT)]):
                dst = zrecv.at[pl.ds(t * PT + n0, n1 - n0)]
                if shift == 0:
                    cp = pltpu.make_async_copy(src, dst, own_sem.at[1 + j])
                    cp.start()
                else:
                    cp = remote(src, dst, zp_send.at[shift - 1, j], zp_recv.at[shift - 1, j], (d, (t + shift) % NT))
                pcopies.append(cp)

    pcopies = []

    def send_heads():
        for cp in pcopies:
            cp.wait()

        def total(at):
            return zrecv[windows_ref[at]] + zrecv[windows_ref[at + 1]]

        for k in range(2):
            for i in range(2):
                bsend[k, i] = total(W_MERGE + 64 + (i * 2 + k) * 2)
            bsend[k, 2] = zrecv[3 * PT + PT - 1]
        for k in range(2):
            for m in range(8):
                for i in range(2):
                    hsend[k * 8 + m, i] = total(W_MERGE + ((2 * i + k) * 8 + m) * 2)

        @pl.loop(1, NDP)
        def _(n):
            i = (d + n) % NDP
            remote(bsend.at[i // 16], brecv.at[seq, :, e], p_send.at[1], p_recv.at[1], (i, t))

        pltpu.make_async_copy(bsend.at[d // 16], brecv.at[seq, :, e], p_recv.at[1]).start()

        @pl.loop(0, 16)
        def _(n):
            i = 16 * (n // 8) + 2 * (n % 8) + e // 8
            dst = hrecv.at[seq, :, (e // 4) % 2, e % 4]

            @pl.when(i != d)
            def _():
                remote(hsend.at[n], dst, p_send.at[2], p_recv.at[2], (i, t))

            @pl.when(i == d)
            def _():
                pltpu.make_async_copy(hsend.at[n], dst, p_recv.at[2]).start()

    high = lax.Precision.HIGHEST
    values = []

    def mix():
        await_bytes(brecv, p_recv.at[1])
        await_bytes(hrecv, p_recv.at[2])
        head = windows_ref[W_HEAD + 1]
        lower = iota((L, L), 0) <= iota((L, L), 1)
        ones = jnp.where(lower, 1.0, 0.0).astype(F32)
        qsend[...] = jnp.zeros_like(qsend)
        for s in range(2):
            bmat = brecv[s, 0].reshape(N, L)
            cmat = brecv[s, 1].reshape(N, L)
            scores = lax.dot_general(bmat, cmat, (((0,), (0,)), ((), ())), precision=high, preferred_element_type=F32)
            raw = brecv[s, 2, windows_ref[W_HEAD]]
            squares = jnp.zeros((1, L), F32)
            for hh in range(2):
                r = 2 * (d % 8) + hh
                row = jnp.sum(jnp.where(iota((TILE, L), 0) == r, raw, 0.0), axis=0, keepdims=True)
                row = row + bias_ref[head + hh]
                step = jnp.maximum(row, 0.0) + jnp.log1p(jnp.exp(-jnp.abs(row)))
                rates = jnp.broadcast_to(step * -rate_ref[head + hh], (8, L))
                cumul = jnp.dot(rates, ones, precision=high, preferred_element_type=F32)
                across = jnp.broadcast_to(cumul[0:1], (L, L))
                diff = across - across.T
                decay = jnp.where(lower, jnp.exp(jnp.where(lower, diff, 0.0)), 0.0)
                weights = scores * decay * jnp.broadcast_to(step, (L, L)).T
                xt = hrecv[s, 1, hh].reshape(P_SIZE, L)
                zt = hrecv[s, 0, hh].reshape(P_SIZE, L)
                out = jnp.dot(xt, weights, precision=high, preferred_element_type=F32) + skip_ref[head + hh] * xt
                v = out * (zt * jax.nn.sigmoid(zt))
                squares = squares + jnp.sum(v * v, axis=0, keepdims=True)
                values.append(v)
            qsend[s : s + 1] = squares
        base = 16 * (d // 16)

        @pl.loop(1, 16)
        def _(n):
            i = base + (d + n) % 16
            remote(qsend, qrecv.at[d % 16], p_send.at[3], p_recv.at[3], (i, t))

        pltpu.make_async_copy(qsend, qrecv.at[d % 16], p_recv.at[3]).start()

    def finish():
        await_bytes(qrecv, p_recv.at[3])
        total = jnp.sum(qrecv[...], axis=0)
        scale = lax.rsqrt(total / (32 * P_SIZE) + 1e-05)
        gain = gain_ref[windows_ref[W_HEAD + 2]]
        for s in range(2):
            v = jnp.concatenate(values[2 * s : 2 * s + 2], axis=0) * scale[s : s + 1]
            mixed_ref[s * L : (s + 1) * L] = (v.T * gain).astype(BF16)

    zero = jnp.zeros((TILE, L), F32)
    precv[ZERO2] = zero
    zrecv[ZERO3] = zero
    gather_first()
    shift_part(0)
    send_part(0)
    gather_second()
    shift_part(1)
    send_part(1)
    shift_part(2)
    shift_part(3)
    send_part(2)
    forward_part(0)
    gather_third()
    send_part(3)
    forward_part(1)
    multiply()
    send_products()
    forward_part(2)
    forward_products()
    forward_part(3)
    send_heads()
    forward_dt()
    mix()
    finish()

    for cp in copies:
        cp.wait()
    for p in range(NP):
        await_bytes(shifted[p].at[:, :, 0 : (NDP - 1) * F], dp_send.at[p])
    await_bytes(hid.at[0:3, 0, 0, 0:L], ag_send.at[0])
    await_bytes(hid.at[0:3, 0, 0, L:], ag_send.at[1])
    await_bytes(hid.at[0:3, :, 0, 0:L], ag_send.at[2])
    await_bytes(hid.at[0:3, :, 0, L:], ag_send.at[3])
    await_bytes(hid.at[:, :, 0], ag_send.at[4])
    await_bytes(precv.at[0 : 2 * (NDP - 1)], p_send.at[0])
    await_bytes(brecv.at[0, :, 0:16], p_send.at[1])
    await_bytes(brecv.at[1, :, 0:15], p_send.at[1])
    itself = seq == e // 8

    @pl.when(itself)
    def _():
        await_bytes(hsend.at[0:15], p_send.at[2])

    @pl.when(jnp.logical_not(itself))
    def _():
        await_bytes(hsend, p_send.at[2])

    await_bytes(qrecv.at[0:15], p_send.at[3])


def exchange(windows, rate, bias, skip, gain, hidden, flat):
    any_ = pl.BlockSpec(memory_space=pl.ANY)
    smem = pl.BlockSpec(memory_space=pltpu.SMEM)
    vmem = pl.BlockSpec(memory_space=pltpu.VMEM)
    dma = pltpu.SemaphoreType.DMA
    return pl.pallas_call(
        exchange_kernel,
        out_shape=(
            pltpu.VMEM((NT, 6, SLOT, TILE, F), BF16),
            pltpu.VMEM((NT, 4, TILE, F), BF16),
            jax.ShapeDtypeStruct((2 * L, L), BF16),
        ),
        in_specs=[smem, smem, smem, smem, vmem, vmem, vmem],
        out_specs=(vmem, vmem, vmem),
        scratch_shapes=[pltpu.VMEM((w, TILE, D), BF16) for w in PARTS]
        + [pltpu.VMEM((NDP * w, TILE, F), BF16) for w in PARTS]
        + [pltpu.VMEM((NT, 4, c, TILE, F), BF16) for c in CAPS]
        + [pltpu.VMEM((2, c, TILE, F), BF16) for c in CAPS]
        + [
            pltpu.VMEM((16, TILE, F), BF16),
            pltpu.VMEM((NT, 4, TILE, F), BF16),
            dma((NP,)),
            dma((NP,)),
            dma((NT - 1, 2 * NP + 1)),
            dma((NT - 1, 2 * NP + 1)),
            dma((2 * NP + 1,)),
            pltpu.VMEM((4, 4, 2, 2 * L, F), BF16),
            pltpu.VMEM((2, 32, TILE, L), F32),
            pltpu.VMEM((ZERO2 + 1, TILE, L), F32),
            pltpu.VMEM((NT, 4 * PICKS, TILE, L), F32),
            pltpu.VMEM((2 * PICKS + 1, TILE, L), F32),
            pltpu.VMEM((ZERO3 + 1, TILE, L), F32),
            pltpu.VMEM((16, 2, TILE, L), F32),
            pltpu.VMEM((2, 2, 2, 4, TILE, L), F32),
            pltpu.VMEM((2, 3, TILE, L), F32),
            pltpu.VMEM((2, 3, 16, TILE, L), F32),
            pltpu.VMEM((8, L), F32),
            pltpu.VMEM((16, 8, L), F32),
            dma((5,)),
            dma((5,)),
            dma((4,)),
            dma((4,)),
            dma((NT - 1, 2)),
            dma((NT - 1, 2)),
            dma((3,)),
        ],
        compiler_params=pltpu.CompilerParams(
            collective_id=1, has_side_effects=True, vmem_limit_bytes=44 << 20
        ),
        name="exchange",
    )(windows, rate, bias, skip, gain, hidden, flat)


STEP = 64


def place_kernel(off_ref, own_ref, place_ref, got_ref, dt_ref, out_ref):
    step = pl.program_id(0)
    g = owner_groups(own_ref, lax.axis_index("tensor"))

    def tile(slot, block, tau):
        at = (block * BT + tau) * 2
        one, two = place_ref[at], place_ref[at + 1]
        base = slot * SLOT
        first = got_ref[one + base]
        second = got_ref[jnp.maximum(two, 0) + base]
        return first + jnp.where(two >= 0, second, jnp.zeros_like(second))

    @pl.when(step < 8)
    def _():
        k = step // 4
        gk = jnp.where(k == 0, g[0], g[1])
        for seg in range(2):
            block = off_ref[seg] // 2048 + gk
            for j in range(8):
                for q in range(4):
                    out_ref[j * 8 + seg * 4 + q] = tile(2 * seg + k, block, (step % 4) * 32 + 4 * j + q)

    @pl.when(step == 8)
    def _():
        for seg in range(2):
            block = off_ref[2 + seg] // 2048
            for k in range(2):
                for q in range(16):
                    out_ref[(seg * 2 + k) * 16 + q] = tile(4 + seg, block, g[k] * 16 + q)

    @pl.when(step == 9)
    def _():
        for j in range(4):
            out_ref[j] = dt_ref[3, j]


def place(offsets, group_owner, got, dt):
    smem = pl.BlockSpec(memory_space=pltpu.SMEM)
    table = jnp.asarray(PLACE.reshape(-1))
    got = got.reshape(NT * 6 * SLOT, TILE, F)
    rows = pl.pallas_call(
        place_kernel,
        grid=(10,),
        out_shape=jax.ShapeDtypeStruct((580, TILE, F), BF16),
        in_specs=[
            smem,
            smem,
            smem,
            pl.BlockSpec(memory_space=pltpu.VMEM),
            pl.BlockSpec(memory_space=pltpu.VMEM),
        ],
        out_specs=pl.BlockSpec((STEP, TILE, F), lambda i: (i, 0, 0)),
        compiler_params=pltpu.CompilerParams(vmem_limit_bytes=16 << 20),
        name="place",
    )(offsets, group_owner, table, got, dt)
    return rows.reshape(580 * TILE, F).T


def shards(flat_weight, offsets, group_owner, hidden, decay_rate, dt_bias, skip_gain, norm_gain):
    windows = prep(offsets, group_owner)
    gain = norm_gain.reshape(H // 2, 1, 2 * P_SIZE)
    got, dt_rows, mixed = exchange(windows, decay_rate, dt_bias, skip_gain, gain, hidden, flat_weight)
    return place(offsets, group_owner, got, dt_rows), mixed


def solution(mesh):
    placed = (P(("dp", "tensor"), None), P(), P(), P(None, "dp"), P(), P(), P(), P())
    return jax.shard_map(
        shards,
        mesh=mesh,
        in_specs=placed,
        out_specs=(P("dp", "tensor"), P(None, ("dp", "tensor"))),
        check_vma=False,
    )
```

```python
import functools

import jax
import jax.numpy as jnp
import numpy as np
from jax import lax
from jax.experimental import pallas as pl
from jax.experimental.pallas import tpu as pltpu
from jax.sharding import PartitionSpec as P

H = 256
P_SIZE = 64
N = 256
G = 8
L = 128
ROWS = 290
D = 8192
F = 256
NDP = 32
NT = 4
TILE = 16
CHUNK = 19
BLOCKS = 18
BT = 128
PARTS = (6, 5, 5, 3)
STARTS = (0, 6, 11, 16)
COMMON = (0, 1, 8, 9, 16, 17)
MESH = pl.DeviceIdType.MESH
BF16 = jnp.bfloat16
F32 = jnp.float32


def first_tile(chunk):
    return ROWS * chunk // TILE


def make_tables():
    n = len(PARTS)
    lo = np.full((n, NT, BLOCKS), 10**6)
    hi = np.full((n, NT, BLOCKS), -1)
    where = {}
    for k in range(NDP * NT):
        for l in range(CHUNK):
            p = max(i for i in range(n) if STARTS[i] <= l)
            b, tau = divmod(first_tile(k) + l, BT)
            if b >= BLOCKS:
                continue
            i = (k // NT) * PARTS[p] + l - STARTS[p]
            where.setdefault((b, tau), []).append((k % NT, p, i))
            lo[p, k % NT, b] = min(lo[p, k % NT, b], i)
            hi[p, k % NT, b] = max(hi[p, k % NT, b], i)
    caps = [int((hi[p] - lo[p] + 1).max()) for p in range(n)]
    start = np.zeros((n, NT, BLOCKS), np.int32)
    for p in range(n):
        start[p] = np.clip(lo[p], 0, NDP * PARTS[p] - caps[p])
    offs = np.concatenate([[0], np.cumsum(caps)])
    slot = int(offs[-1])
    place = np.full((BLOCKS, BT, 2), -1, np.int32)
    for (b, tau), found in where.items():
        for e, (t, p, i) in enumerate(found):
            place[b, tau, e] = t * 4 * slot + offs[p] + i - start[p, t, b]
    spread = {}
    for (b, tau), found in sorted(where.items()):
        for t, p, i in found:
            if b in COMMON:
                spread.setdefault((t, b, tau % 4), []).append((tau, offs[p] + i - start[p, t, b]))
    width = max(len(v) for v in spread.values())
    relay = np.full((NT, BLOCKS, 4, width), -1, np.int32)
    gathered = np.full((4, BLOCKS, 32, 2), -1, np.int32)
    for (t, b, r), found in spread.items():
        for n, (tau, at) in enumerate(found):
            relay[t, b, r, n] = at
            e = int(gathered[r, b, tau // 4, 0] >= 0)
            gathered[r, b, tau // 4, e] = t * 2 * width + n
    return caps, [int(o) for o in offs], slot, start, place, width, relay, gathered


PICKS = 3
PT = 6 * PICKS + 1
ZERO2 = 2 * NDP
ZERO3 = NT * PT


def make_product_tables():
    pick = np.full((NT, 16, BLOCKS, PICKS), ZERO2, np.int32)
    merge = np.full((16, BLOCKS, 8, 2), -1, np.int32)
    count = np.zeros((NT, 16, BLOCKS), np.int32)
    seen = np.zeros((16, BLOCKS, 8), np.int32)
    for k in range(NDP * NT):
        for l in range(CHUNK):
            tile = first_tile(k) + l
            b, tau = divmod(tile, BT)
            if b >= BLOCKS:
                continue
            t, e, m = k % NT, tau % 16, tau // 16
            n = count[t, e, b]
            pick[t, e, b, n] = (k // NT) * 2 + l // 16
            merge[e, b, m, seen[e, b, m]] = t * PT + n
            count[t, e, b] += 1
            seen[e, b, m] += 1
    return pick, merge


CAPS, OFFS, SLOT, START, PLACE, WIDTH, RELAY, GATHERED = make_tables()
PICK, MERGE = make_product_tables()
NP = len(PARTS)
W_DT = NP * 18
W_PICK = W_DT + 8
W_MERGE = W_PICK + 18 * PICKS
W_HEAD = W_MERGE + 72
W_RELAY = W_HEAD + 3
W_GATHER = W_RELAY + 8 * WIDTH
W_SIZE = W_GATHER + NT * 32
ZERO_B = 2 * SLOT
ZERO_R = NT * 2 * WIDTH


def dp_order():
    steps = [(a, b, c) for a in range(4) for b in range(4) for c in range(2) if (a, b, c) != (0, 0, 0)]
    steps.sort(key=lambda s: -(min(s[0], 4 - s[0]) + min(s[1], 4 - s[1])))
    out = []
    for a, b, c in steps:
        for q in ((a, b, c), (b, a, c), (-a % 4, -b % 4, c), (-b % 4, -a % 4, c)):
            if q not in out:
                out.append(q)
    return out[::-1]


ORDER = dp_order()


def dp_partner(d, step):
    x, y, c = d // 8, (d // 2) % 4, d % 2
    return ((x + step[0]) % 4) * 8 + ((y + step[1]) % 4) * 2 + (c + step[2]) % 2


def owner_groups(owner_ref, owner):
    first, last = jnp.int32(G), jnp.int32(-1)
    for g in range(G):
        mine = owner_ref[g] == owner
        first = jnp.where(mine, jnp.minimum(first, g), first)
        last = jnp.where(mine, g, last)
    return jnp.clip(first, 0, G - 1), jnp.clip(last, 0, G - 1)


def find_windows(
    off_ref, own_ref, start_ref, pick_ref, merge_ref, relay_ref, gathered_ref, windows_ref
):
    d = lax.axis_index("dp")
    t = lax.axis_index("tensor")
    e = d // 2
    seg = [off_ref[i] // 2048 for i in range(4)]

    def picks(at, b):
        for n in range(PICKS):
            windows_ref[at + n] = pick_ref[((t * 16 + e) * BLOCKS + b) * PICKS + n]

    for shift in range(NT):
        g = owner_groups(own_ref, (t + shift) % NT)
        for s in range(4):
            b = seg[s // 2] + g[s % 2]
            for p in range(NP):
                windows_ref[p * 18 + shift * 4 + s] = start_ref[(p * NT + t) * BLOCKS + b]
            picks(W_PICK + (shift * 4 + s) * PICKS, b)
        for i in range(2):
            windows_ref[W_DT + shift * 2 + i] = 2 * g[i]
    for i in range(2):
        for p in range(NP):
            windows_ref[p * 18 + 16 + i] = start_ref[(p * NT + t) * BLOCKS + seg[2 + i]]
        picks(W_PICK + (16 + i) * PICKS, seg[2 + i])

    def merged(at, b, m, slot):
        for n in range(2):
            v = merge_ref[((e * BLOCKS + b) * 8 + m) * 2 + n]
            windows_ref[at + n] = jnp.where(v < 0, ZERO3, v + PICKS * slot)

    g = owner_groups(own_ref, t)
    for s in range(4):
        for m in range(8):
            merged(W_MERGE + (s * 8 + m) * 2, seg[s // 2] + g[s % 2], m, s)
    for i in range(2):
        for k in range(2):
            merged(W_MERGE + 64 + (i * 2 + k) * 2, seg[2 + i], g[k], 4 + i)
    mine = jnp.where(d < 16, g[0], g[1])
    windows_ref[W_HEAD] = 2 * mine + (d % 16) // 8
    windows_ref[W_HEAD + 1] = 32 * mine + 2 * (d % 16)
    windows_ref[W_HEAD + 2] = 16 * mine + d % 16
    for shift in range(NT):
        g = owner_groups(own_ref, (t + shift) % NT)
        for i in range(2):
            for n in range(WIDTH):
                v = relay_ref[((t * BLOCKS + seg[2 + i]) * 4 + (t + shift) % NT) * WIDTH + n]
                windows_ref[W_RELAY + (shift * 2 + i) * WIDTH + n] = jnp.where(v < 0, ZERO_B, v + i * SLOT)
            for k in range(2):
                for u in range(4):
                    for n in range(2):
                        v = gathered_ref[((t * BLOCKS + seg[2 + i]) * 32 + g[k] * 4 + u) * 2 + n]
                        at = W_GATHER + shift * 32 + ((i * 2 + k) * 4 + u) * 2 + n
                        windows_ref[at] = jnp.where(v < 0, ZERO_R, v + i * WIDTH)


def iota(shape, dim):
    return lax.broadcasted_iota(jnp.int32, shape, dim)


class Table:
    def __init__(self, ref, base):
        self.ref, self.base = ref, base

    def __getitem__(self, i):
        return self.ref[self.base + i]


TABLES = np.concatenate([a.reshape(-1) for a in (START, PICK, MERGE, RELAY, GATHERED)])
BASES = np.cumsum([0, START.size, PICK.size, MERGE.size, RELAY.size])


def exchange_kernel(
    off_hbm,
    own_hbm,
    table_hbm,
    rate_hbm,
    bias_hbm,
    skip_hbm,
    gain_hbm,
    hidden_ref,
    flat_hbm,
    out_ref,
    bc_ref,
    dt_ref,
    mixed_ref,
    windows_ref,
    *scratch,
):
    loads = scratch[-9:]
    scratch = scratch[:-9]
    off_ref, own_ref, table_ref, rate_ref, bias_ref, skip_ref, gain_ref, flat_ref, load_sem = loads
    whole = [
        (flat_hbm, flat_ref),
        (off_hbm, off_ref),
        (own_hbm, own_ref),
        (table_hbm, table_ref),
        (rate_hbm, rate_ref),
        (bias_hbm, bias_ref),
        (skip_hbm, skip_ref),
        (gain_hbm, gain_ref),
    ]
    loading = [pltpu.make_async_copy(src, dst, load_sem.at[i]) for i, (src, dst) in enumerate(whole)]
    for cp in loading:
        cp.start()
    shifted = scratch[:NP]
    recv = scratch[NP : 2 * NP]
    send = scratch[2 * NP : 3 * NP]
    dtbuf, dtsend, dp_send, dp_recv, z_send, z_recv, self_sem = scratch[3 * NP : 3 * NP + 7]
    hid, prod, precv, zsend, zcom, zrecv, hsend, hrecv, bsend, brecv, qsend, qrecv = scratch[3 * NP + 7 : 3 * NP + 19]
    ag_send, ag_recv, p_send, p_recv, zp_send, zp_recv, own_sem = scratch[3 * NP + 19 : 3 * NP + 26]
    bcbuf, spread, gather, owned, b_send, b_recv, b_self = scratch[3 * NP + 26 :]
    d = lax.axis_index("dp")
    t = lax.axis_index("tensor")
    x, y, c = d // 8, (d // 2) % 4, d % 2
    e, seq = d // 2, d % 2
    chunk = d * NT + t

    barrier = pltpu.get_barrier_semaphore()

    @pl.loop(1, NDP)
    def _(i):
        pl.semaphore_signal(barrier, inc=1, device_id=((d + i) % NDP, t), device_id_type=MESH)

    @pl.loop(1, NT)
    def _(i):
        pl.semaphore_signal(barrier, inc=1, device_id=(d, (t + i) % NT), device_id_type=MESH)

    pl.semaphore_wait(barrier, NDP - 1 + NT - 1)

    def remote(src, dst, ssem, rsem, device):
        cp = pltpu.make_async_remote_copy(
            src_ref=src, dst_ref=dst, send_sem=ssem, recv_sem=rsem, device_id=device, device_id_type=MESH
        )
        cp.start()
        return cp

    def await_bytes(ref, sem):
        pltpu.make_async_copy(ref, ref, sem).wait()

    copies = []

    phase = (ROWS * chunk) % TILE

    def shift_part(p):
        a, rows = STARTS[p] * TILE, PARTS[p] * TILE
        w0, w1 = max(a - TILE, 0), min(a + rows, ROWS)
        pick = jnp.where(iota((rows, w1 - w0), 0) + (a - phase) == iota((rows, w1 - w0), 1) + w0, 1.0, 0.0)
        pick = pick.astype(BF16)

        @pl.loop(0, D // 1024)
        def _(i):
            cols = pl.ds(pl.multiple_of(i * 1024, 1024), 1024)
            moved = jnp.dot(pick, flat_ref[w0:w1, cols], preferred_element_type=F32)
            shifted[p][:, :, cols] = moved.astype(BF16).reshape(PARTS[p], TILE, 1024)

    def send_part(p):
        mine = pl.ds(d * PARTS[p], PARTS[p])
        for step in ORDER:
            peer = dp_partner(d, step)
            remote(
                shifted[p].at[:, :, pl.ds(pl.multiple_of(peer * F, F), F)],
                recv[p].at[mine],
                dp_send.at[p],
                dp_recv.at[p],
                (peer, t),
            )
        pltpu.make_async_copy(
            shifted[p].at[:, :, pl.ds(pl.multiple_of(d * F, F), F)], recv[p].at[mine], dp_recv.at[p]
        ).start()

    def forward_part(p):
        await_bytes(recv[p], dp_recv.at[p])

        def pack(dst, window, at=0):
            first = windows_ref[window]

            @pl.loop(0, CAPS[p], unroll=2)
            def _(j):
                dst[at + j] = recv[p][first + j]

        for i in range(2):
            pack(bcbuf, p * 18 + 16 + i, i * SLOT + OFFS[p])
        for l in range(max(STARTS[p], 3), STARTS[p] + PARTS[p]):
            dtbuf[l - 3] = recv[p][31 * PARTS[p] + l - STARTS[p]]
        if p == NP - 1:
            spread_common()
        for shift in (1, 3, 2, 0):
            for s in range(4):
                pack(send[p].at[shift, s], p * 18 + shift * 4 + s)
            src, dst = send[p].at[shift], out_ref.at[t, :, pl.ds(OFFS[p], CAPS[p])]
            to_owner(src, dst, shift, p)

    def to_owner(src, dst, shift, n):
        if shift == 0:
            cp = pltpu.make_async_copy(src, dst, self_sem.at[n])
            cp.start()
        else:
            cp = remote(src, dst, z_send.at[shift - 1, n], z_recv.at[shift - 1, n], (d, (t + shift) % NT))
        copies.append(cp)

    bcopies = []

    def spread_common():
        for shift in (1, 3, 2, 0):
            for n in range(2 * WIDTH):
                spread[shift, n] = bcbuf[windows_ref[W_RELAY + shift * 2 * WIDTH + n]]
            dst = gather.at[pl.ds(t * 2 * WIDTH, 2 * WIDTH)]
            if shift == 0:
                cp = pltpu.make_async_copy(spread.at[0], dst, b_self.at[0])
                cp.start()
            else:
                cp = remote(spread.at[shift], dst, b_send.at[shift - 1], b_recv.at[shift - 1], (d, (t + shift) % NT))
            bcopies.append(cp)

    def share_common():
        for cp in bcopies:
            cp.wait()
        for shift in (1, 3, 2, 0):
            for n in range(16):
                at = W_GATHER + shift * 32 + 2 * n
                owned[shift, n] = gather[windows_ref[at]] + gather[windows_ref[at + 1]]
            to_owner(owned.at[shift], bc_ref.at[t], shift, NP + 1)

    def forward_dt():
        for shift in (1, 3, 2, 0):
            for i in range(2):
                for j in range(2):
                    dtsend[shift, 2 * i + j] = dtbuf[windows_ref[W_DT + shift * 2 + i] + j]
            to_owner(dtsend.at[shift], dt_ref.at[t], shift, NP)

    def along_x(i):
        return (((x + i) % 4) * 8 + y * 2 + c, t)

    def along_y(i):
        return (x * 8 + ((y + i) % 4) * 2 + c, t)

    def gather_first():
        own = pltpu.make_async_copy(hidden_ref, hid.at[x, y, c], own_sem.at[0])
        own.start()
        for i in (1, 3, 2):
            remote(hidden_ref.at[0:L], hid.at[x, y, c, 0:L], ag_send.at[0], ag_recv.at[0], along_x(i))
            remote(hidden_ref.at[L:], hid.at[x, y, c, L:], ag_send.at[1], ag_recv.at[1], along_y(i))
        own.wait()

    def gather_second():
        await_bytes(hid.at[0:3, 0, 0, 0:L], ag_recv.at[0])
        for i in (1, 3, 2):
            remote(hid.at[:, y, c, 0:L], hid.at[:, y, c, 0:L], ag_send.at[2], ag_recv.at[2], along_y(i))
        await_bytes(hid.at[0:3, 0, 0, L:], ag_recv.at[1])
        for i in (1, 3, 2):
            remote(hid.at[x, :, c, L:], hid.at[x, :, c, L:], ag_send.at[3], ag_recv.at[3], along_x(i))

    def gather_third():
        await_bytes(hid.at[0:3, :, 0, 0:L], ag_recv.at[2])
        await_bytes(hid.at[0:3, :, 0, L:], ag_recv.at[3])
        remote(hid.at[:, :, c], hid.at[:, :, c], ag_send.at[4], ag_recv.at[4], (d + 1 - 2 * c, t))
        await_bytes(hid.at[:, :, 0], ag_recv.at[4])

    def multiply():
        prod[...] = jnp.zeros_like(prod)

        @pl.loop(0, NDP)
        def _(i):
            cols = pl.ds(pl.multiple_of(i * F, F), F)
            rows = jnp.concatenate(
                [shifted[p][:, :, cols].reshape(PARTS[p] * TILE, F) for p in range(NP)], axis=0
            )
            part = lax.dot_general(
                rows, hid[i // 8, (i // 2) % 4, i % 2], (((1,), (1,)), ((), ())), preferred_element_type=F32
            )
            for s in range(2):
                prod[s, 0:CHUNK] += part[:, s * L : (s + 1) * L].reshape(CHUNK, TILE, L)

    def product_tiles(i):
        low = (i // 2 + 16 * NDP * NT * CHUNK - first_tile(chunk)) % 16
        return low, i % 2

    def send_products():
        @pl.loop(1, NDP)
        def _(n):
            i = (d + n) % NDP
            low, s = product_tiles(i)
            for h in range(2):
                remote(prod.at[s, low + 16 * h], precv.at[2 * d + h], p_send.at[0], p_recv.at[0], (i, t))

        low, s = product_tiles(d)
        for h in range(2):
            pltpu.make_async_copy(prod.at[s, low + 16 * h], precv.at[2 * d + h], p_recv.at[0]).start()

    def forward_products():
        await_bytes(precv.at[0 : 2 * NDP], p_recv.at[0])
        for n in range(2 * PICKS):
            zcom[n] = precv[windows_ref[W_PICK + 16 * PICKS + n]]
        zcom[2 * PICKS] = precv[2 * 31 + (3 + e) // 16]
        for shift in (1, 3, 2, 0):
            for n in range(4 * PICKS):
                zsend[shift, n] = precv[windows_ref[W_PICK + shift * 4 * PICKS + n]]
            for j, (src, n0, n1) in enumerate([(zsend.at[shift], 0, 4 * PICKS), (zcom, 4 * PICKS, PT)]):
                dst = zrecv.at[pl.ds(t * PT + n0, n1 - n0)]
                if shift == 0:
                    cp = pltpu.make_async_copy(src, dst, own_sem.at[1 + j])
                    cp.start()
                else:
                    cp = remote(src, dst, zp_send.at[shift - 1, j], zp_recv.at[shift - 1, j], (d, (t + shift) % NT))
                pcopies.append(cp)

    pcopies = []

    def send_heads():
        for cp in pcopies:
            cp.wait()

        def total(at):
            return zrecv[windows_ref[at]] + zrecv[windows_ref[at + 1]]

        for k in range(2):
            for i in range(2):
                bsend[k, i] = total(W_MERGE + 64 + (i * 2 + k) * 2)
            bsend[k, 2] = zrecv[3 * PT + PT - 1]
        for k in range(2):
            for m in range(8):
                for i in range(2):
                    hsend[k * 8 + m, i] = total(W_MERGE + ((2 * i + k) * 8 + m) * 2)

        @pl.loop(1, 16)
        def _(n):
            i = (d + 2 * n) % NDP
            remote(bsend.at[i // 16], brecv.at[seq, :, e], p_send.at[1], p_recv.at[1], (i, t))

        pltpu.make_async_copy(bsend.at[d // 16], brecv.at[seq, :, e], p_recv.at[1]).start()

        @pl.loop(0, 16)
        def _(n):
            i = 16 * (n // 8) + 2 * (n % 8) + e // 8
            dst = hrecv.at[seq, :, (e // 4) % 2, e % 4]

            @pl.when(i != d)
            def _():
                remote(hsend.at[n], dst, p_send.at[2], p_recv.at[2], (i, t))

            @pl.when(i == d)
            def _():
                pltpu.make_async_copy(hsend.at[n], dst, p_recv.at[2]).start()

    high = lax.Precision.HIGHEST
    values = []

    def share_products():
        await_bytes(brecv.at[seq], p_recv.at[1])
        remote(brecv.at[seq], brecv.at[seq], p_send.at[4], p_recv.at[4], (d + 1 - 2 * c, t))

    def mix():
        await_bytes(brecv.at[seq], p_recv.at[4])
        await_bytes(hrecv, p_recv.at[2])
        head = windows_ref[W_HEAD + 1]
        lower = iota((L, L), 0) <= iota((L, L), 1)
        ones = jnp.where(lower, 1.0, 0.0).astype(F32)
        qsend[...] = jnp.zeros_like(qsend)
        for s in range(2):
            bmat = brecv[s, 0].reshape(N, L)
            cmat = brecv[s, 1].reshape(N, L)
            scores = lax.dot_general(bmat, cmat, (((0,), (0,)), ((), ())), precision=high, preferred_element_type=F32)
            raw = brecv[s, 2, windows_ref[W_HEAD]]
            squares = jnp.zeros((1, L), F32)
            for hh in range(2):
                r = 2 * (d % 8) + hh
                row = jnp.sum(jnp.where(iota((TILE, L), 0) == r, raw, 0.0), axis=0, keepdims=True)
                row = row + bias_ref[head + hh]
                step = jnp.maximum(row, 0.0) + jnp.log1p(jnp.exp(-jnp.abs(row)))
                rates = jnp.broadcast_to(step * -rate_ref[head + hh], (8, L))
                cumul = jnp.dot(rates, ones, precision=high, preferred_element_type=F32)
                across = jnp.broadcast_to(cumul[0:1], (L, L))
                diff = across - across.T
                decay = jnp.where(lower, jnp.exp(jnp.where(lower, diff, 0.0)), 0.0)
                weights = scores * decay * jnp.broadcast_to(step, (L, L)).T
                xt = hrecv[s, 1, hh].reshape(P_SIZE, L)
                zt = hrecv[s, 0, hh].reshape(P_SIZE, L)
                out = jnp.dot(xt, weights, precision=high, preferred_element_type=F32) + skip_ref[head + hh] * xt
                v = out * (zt * jax.nn.sigmoid(zt))
                squares = squares + jnp.sum(v * v, axis=0, keepdims=True)
                values.append(v)
            qsend[s : s + 1] = squares
        base = 16 * (d // 16)

        @pl.loop(1, 16)
        def _(n):
            i = base + (d + n) % 16
            remote(qsend, qrecv.at[d % 16], p_send.at[3], p_recv.at[3], (i, t))

        pltpu.make_async_copy(qsend, qrecv.at[d % 16], p_recv.at[3]).start()

    def finish():
        await_bytes(qrecv, p_recv.at[3])
        total = jnp.sum(qrecv[...], axis=0)
        scale = lax.rsqrt(total / (32 * P_SIZE) + 1e-05)
        gain = gain_ref[windows_ref[W_HEAD + 2]]
        for s in range(2):
            v = jnp.concatenate(values[2 * s : 2 * s + 2], axis=0) * scale[s : s + 1]
            mixed_ref[s * L : (s + 1) * L] = (v.T * gain).astype(BF16)

    zero = jnp.zeros((TILE, L), F32)
    bcbuf[ZERO_B] = jnp.zeros((TILE, F), BF16)
    gather[ZERO_R] = jnp.zeros((TILE, F), BF16)
    precv[ZERO2] = zero
    zrecv[ZERO3] = zero
    gather_first()
    loading[0].wait()
    shift_part(0)
    send_part(0)
    gather_second()
    shift_part(1)
    send_part(1)
    shift_part(2)
    shift_part(3)
    for cp in loading[1:]:
        cp.wait()
    find_windows(off_ref, own_ref, *[Table(table_ref, int(i)) for i in BASES], windows_ref)
    forward_part(0)
    gather_third()
    multiply()
    send_products()
    send_part(2)
    forward_part(1)
    forward_products()
    send_part(3)
    forward_part(2)
    send_heads()
    share_products()
    forward_part(3)
    forward_dt()
    mix()
    share_common()
    finish()

    for cp in copies:
        cp.wait()
    for p in range(NP):
        await_bytes(shifted[p].at[:, :, 0 : (NDP - 1) * F], dp_send.at[p])
    await_bytes(hid.at[0:3, 0, 0, 0:L], ag_send.at[0])
    await_bytes(hid.at[0:3, 0, 0, L:], ag_send.at[1])
    await_bytes(hid.at[0:3, :, 0, 0:L], ag_send.at[2])
    await_bytes(hid.at[0:3, :, 0, L:], ag_send.at[3])
    await_bytes(hid.at[:, :, 0], ag_send.at[4])
    await_bytes(precv.at[0 : 2 * (NDP - 1)], p_send.at[0])
    await_bytes(brecv.at[1, :, 0:15], p_send.at[1])
    await_bytes(brecv.at[1], p_send.at[4])
    itself = seq == e // 8

    @pl.when(itself)
    def _():
        await_bytes(hsend.at[0:15], p_send.at[2])

    @pl.when(jnp.logical_not(itself))
    def _():
        await_bytes(hsend, p_send.at[2])

    await_bytes(qrecv.at[0:15], p_send.at[3])


def exchange(offsets, owner, rate, bias, skip, gain, hidden, flat):
    hbm = pl.BlockSpec(memory_space=pltpu.HBM)
    vmem = pl.BlockSpec(memory_space=pltpu.VMEM)
    dma = pltpu.SemaphoreType.DMA
    return pl.pallas_call(
        exchange_kernel,
        out_shape=(
            pltpu.VMEM((NT, 4, SLOT, TILE, F), BF16),
            pltpu.VMEM((NT, 16, TILE, F), BF16),
            pltpu.VMEM((NT, 4, TILE, F), BF16),
            jax.ShapeDtypeStruct((2 * L, L), BF16),
        ),
        in_specs=[hbm] * 9,
        out_specs=(vmem,) * 4,
        scratch_shapes=[pltpu.SMEM((W_SIZE,), jnp.int32)]
        + [pltpu.VMEM((w, TILE, D), BF16) for w in PARTS]
        + [pltpu.VMEM((NDP * w, TILE, F), BF16) for w in PARTS]
        + [pltpu.VMEM((NT, 4, c, TILE, F), BF16) for c in CAPS]
        + [
            pltpu.VMEM((16, TILE, F), BF16),
            pltpu.VMEM((NT, 4, TILE, F), BF16),
            dma((NP,)),
            dma((NP,)),
            dma((NT - 1, NP + 2)),
            dma((NT - 1, NP + 2)),
            dma((NP + 2,)),
            pltpu.VMEM((4, 4, 2, 2 * L, F), BF16),
            pltpu.VMEM((2, 32, TILE, L), F32),
            pltpu.VMEM((ZERO2 + 1, TILE, L), F32),
            pltpu.VMEM((NT, 4 * PICKS, TILE, L), F32),
            pltpu.VMEM((2 * PICKS + 1, TILE, L), F32),
            pltpu.VMEM((ZERO3 + 1, TILE, L), F32),
            pltpu.VMEM((16, 2, TILE, L), F32),
            pltpu.VMEM((2, 2, 2, 4, TILE, L), F32),
            pltpu.VMEM((2, 3, TILE, L), F32),
            pltpu.VMEM((2, 3, 16, TILE, L), F32),
            pltpu.VMEM((8, L), F32),
            pltpu.VMEM((16, 8, L), F32),
            dma((5,)),
            dma((5,)),
            dma((5,)),
            dma((5,)),
            dma((NT - 1, 2)),
            dma((NT - 1, 2)),
            dma((3,)),
            pltpu.VMEM((ZERO_B + 1, TILE, F), BF16),
            pltpu.VMEM((NT, 2 * WIDTH, TILE, F), BF16),
            pltpu.VMEM((ZERO_R + 1, TILE, F), BF16),
            pltpu.VMEM((NT, 16, TILE, F), BF16),
            dma((NT - 1,)),
            dma((NT - 1,)),
            dma((1,)),
            pltpu.SMEM((5,), jnp.int32),
            pltpu.SMEM((G,), jnp.int32),
            pltpu.SMEM(TABLES.shape, jnp.int32),
            pltpu.SMEM((H,), F32),
            pltpu.SMEM((H,), F32),
            pltpu.SMEM((H,), F32),
            pltpu.VMEM((H // 2, 1, 2 * P_SIZE), F32),
            pltpu.VMEM((ROWS, D), BF16),
            dma((8,)),
        ],
        compiler_params=pltpu.CompilerParams(
            collective_id=1, has_side_effects=True, vmem_limit_bytes=58 << 20
        ),
        name="exchange",
    )(offsets, owner, jnp.asarray(TABLES), rate, bias, skip, gain, hidden, flat)


STEP = 64


def place_kernel(off_ref, own_ref, place_ref, got_ref, bc_ref, dt_ref, out_ref):
    step = pl.program_id(0)
    g = owner_groups(own_ref, lax.axis_index("tensor"))

    def tile(slot, block, tau):
        at = (block * BT + tau) * 2
        one, two = place_ref[at], place_ref[at + 1]
        base = slot * SLOT
        first = got_ref[one + base]
        second = got_ref[jnp.maximum(two, 0) + base]
        return first + jnp.where(two >= 0, second, jnp.zeros_like(second))

    @pl.when(step < 8)
    def _():
        k = step // 4
        gk = jnp.where(k == 0, g[0], g[1])
        for seg in range(2):
            block = off_ref[seg] // 2048 + gk
            for j in range(8):
                for q in range(4):
                    out_ref[j * 8 + seg * 4 + q] = tile(2 * seg + k, block, (step % 4) * 32 + 4 * j + q)

    @pl.when(step == 8)
    def _():
        for n in range(4):
            for q in range(16):
                out_ref[n * 16 + q] = bc_ref[q % 4, n * 4 + q // 4]

    @pl.when(step == 9)
    def _():
        for j in range(4):
            out_ref[j] = dt_ref[3, j]


def place(offsets, group_owner, got, bc, dt):
    smem = pl.BlockSpec(memory_space=pltpu.SMEM)
    table = jnp.asarray(PLACE.reshape(-1))
    got = got.reshape(NT * 4 * SLOT, TILE, F)
    rows = pl.pallas_call(
        place_kernel,
        grid=(10,),
        out_shape=jax.ShapeDtypeStruct((580, TILE, F), BF16),
        in_specs=[
            smem,
            smem,
            smem,
            pl.BlockSpec(memory_space=pltpu.VMEM),
            pl.BlockSpec(memory_space=pltpu.VMEM),
            pl.BlockSpec(memory_space=pltpu.VMEM),
        ],
        out_specs=pl.BlockSpec((STEP, TILE, F), lambda i: (i, 0, 0)),
        compiler_params=pltpu.CompilerParams(vmem_limit_bytes=16 << 20),
        name="place",
    )(offsets, group_owner, table, got, bc, dt)
    return rows.reshape(580 * TILE, F).T


def shards(flat_weight, offsets, group_owner, hidden, decay_rate, dt_bias, skip_gain, norm_gain):
    gain = norm_gain.reshape(H // 2, 1, 2 * P_SIZE)
    got, bc, dt_rows, mixed = exchange(
        offsets, group_owner, decay_rate, dt_bias, skip_gain, gain, hidden, flat_weight
    )
    return place(offsets, group_owner, got, bc, dt_rows), mixed


def solution(mesh):
    placed = (P(("dp", "tensor"), None), P(), P(), P(None, "dp"), P(), P(), P(), P())
    return jax.shard_map(
        shards,
        mesh=mesh,
        in_specs=placed,
        out_specs=(P("dp", "tensor"), P(None, ("dp", "tensor"))),
        check_vma=False,
    )
```

```python
import functools

import jax
import jax.numpy as jnp
import numpy as np
from jax import lax
from jax.experimental import pallas as pl
from jax.experimental.pallas import tpu as pltpu
from jax.sharding import PartitionSpec as P

H = 256
P_SIZE = 64
N = 256
G = 8
L = 128
ROWS = 290
D = 8192
F = 256
NDP = 32
NT = 4
TILE = 16
CHUNK = 19
BLOCKS = 18
BT = 128
PARTS = (4, 4, 4, 4, 3)
STARTS = (0, 4, 8, 12, 16)
COMMON = (0, 1, 8, 9, 16, 17)
MESH = pl.DeviceIdType.MESH
BF16 = jnp.bfloat16
F32 = jnp.float32


def first_tile(chunk):
    return ROWS * chunk // TILE


def make_tables():
    n = len(PARTS)
    lo = np.full((n, NT, BLOCKS), 10**6)
    hi = np.full((n, NT, BLOCKS), -1)
    where = {}
    for k in range(NDP * NT):
        for l in range(CHUNK):
            p = max(i for i in range(n) if STARTS[i] <= l)
            b, tau = divmod(first_tile(k) + l, BT)
            if b >= BLOCKS:
                continue
            i = (k // NT) * PARTS[p] + l - STARTS[p]
            where.setdefault((b, tau), []).append((k % NT, p, i))
            lo[p, k % NT, b] = min(lo[p, k % NT, b], i)
            hi[p, k % NT, b] = max(hi[p, k % NT, b], i)
    caps = [int((hi[p] - lo[p] + 1).max()) for p in range(n)]
    start = np.zeros((n, NT, BLOCKS), np.int32)
    for p in range(n):
        start[p] = np.clip(lo[p], 0, NDP * PARTS[p] - caps[p])
    offs = np.concatenate([[0], np.cumsum(caps)])
    slot = int(offs[-1])
    place = np.full((BLOCKS, BT, 2), -1, np.int32)
    for (b, tau), found in where.items():
        for e, (t, p, i) in enumerate(found):
            place[b, tau, e] = t * 4 * slot + offs[p] + i - start[p, t, b]
    spread = {}
    for (b, tau), found in sorted(where.items()):
        for t, p, i in found:
            if b in COMMON:
                key = (t, b, tau % 4)
                spread.setdefault(key, ([], []))[int(p == n - 1)].append((tau, offs[p] + i - start[p, t, b]))
    early = max(len(v[0]) for v in spread.values())
    width = early + max(len(v[1]) for v in spread.values())
    relay = np.full((NT, BLOCKS, 4, width), -1, np.int32)
    gathered = np.full((4, BLOCKS, 32, 2), -1, np.int32)
    for (t, b, r), found in spread.items():
        for m, tiles in enumerate(found):
            for j, (tau, at) in enumerate(tiles, m * early):
                relay[t, b, r, j] = at
                e = int(gathered[r, b, tau // 4, 0] >= 0)
                gathered[r, b, tau // 4, e] = t * 2 * width + j
    return caps, [int(o) for o in offs], slot, start, place, early, width, relay, gathered


PICKS = 3
PT = 6 * PICKS + 1
ZERO2 = 2 * NDP
ZERO3 = NT * PT


def make_product_tables():
    pick = np.full((NT, 16, BLOCKS, PICKS), ZERO2, np.int32)
    merge = np.full((16, BLOCKS, 8, 2), -1, np.int32)
    count = np.zeros((NT, 16, BLOCKS), np.int32)
    seen = np.zeros((16, BLOCKS, 8), np.int32)
    for k in range(NDP * NT):
        for l in range(CHUNK):
            tile = first_tile(k) + l
            b, tau = divmod(tile, BT)
            if b >= BLOCKS:
                continue
            t, e, m = k % NT, tau % 16, tau // 16
            n = count[t, e, b]
            pick[t, e, b, n] = (k // NT) * 2 + l // 16
            merge[e, b, m, seen[e, b, m]] = t * PT + n
            count[t, e, b] += 1
            seen[e, b, m] += 1
    return pick, merge


CAPS, OFFS, SLOT, START, PLACE, EARLY, WIDTH, RELAY, GATHERED = make_tables()
PICK, MERGE = make_product_tables()
NP = len(PARTS)
FIXES = 2


def make_fixes():
    fixes = np.full((BLOCKS, 4, FIXES, 3), -1, np.int32)
    for b in range(BLOCKS):
        for quarter in range(4):
            found = [q for q in range(32) if PLACE[b, quarter * 32 + q, 1] >= 0]
            for n, q in enumerate(found):
                fixes[b, quarter, n] = q, *PLACE[b, quarter * 32 + q]
    return fixes


FIX = make_fixes()
W_DT = NP * 18
W_PICK = W_DT + 8
W_MERGE = W_PICK + 18 * PICKS
W_HEAD = W_MERGE + 72
W_RELAY = W_HEAD + 3
W_GATHER = W_RELAY + 8 * WIDTH
W_SIZE = W_GATHER + NT * 32
ZERO_B = 2 * SLOT
ZERO_R = NT * 2 * WIDTH


def dp_order():
    steps = [(a, b, c) for a in range(4) for b in range(4) for c in range(2) if (a, b, c) != (0, 0, 0)]
    steps.sort(key=lambda s: -(min(s[0], 4 - s[0]) + min(s[1], 4 - s[1])))
    out = []
    for a, b, c in steps:
        for q in ((a, b, c), (b, a, c), (-a % 4, -b % 4, c), (-b % 4, -a % 4, c)):
            if q not in out:
                out.append(q)
    return out


ORDER = dp_order()


def dp_partner(d, step):
    x, y, c = d // 8, (d // 2) % 4, d % 2
    return ((x + step[0]) % 4) * 8 + ((y + step[1]) % 4) * 2 + (c + step[2]) % 2


def owner_groups(owner_ref, owner):
    first, last = jnp.int32(G), jnp.int32(-1)
    for g in range(G):
        mine = owner_ref[g] == owner
        first = jnp.where(mine, jnp.minimum(first, g), first)
        last = jnp.where(mine, g, last)
    return jnp.clip(first, 0, G - 1), jnp.clip(last, 0, G - 1)


def find_windows(
    off_ref, own_ref, start_ref, pick_ref, merge_ref, relay_ref, gathered_ref, windows_ref
):
    d = lax.axis_index("dp")
    t = lax.axis_index("tensor")
    e = d // 2
    seg = [off_ref[i] // 2048 for i in range(4)]

    def picks(at, b):
        for n in range(PICKS):
            windows_ref[at + n] = pick_ref[((t * 16 + e) * BLOCKS + b) * PICKS + n]

    for shift in range(NT):
        g = owner_groups(own_ref, (t + shift) % NT)
        for s in range(4):
            b = seg[s // 2] + g[s % 2]
            for p in range(NP):
                windows_ref[p * 18 + shift * 4 + s] = start_ref[(p * NT + t) * BLOCKS + b]
            picks(W_PICK + (shift * 4 + s) * PICKS, b)
        for i in range(2):
            windows_ref[W_DT + shift * 2 + i] = 2 * g[i]
    for i in range(2):
        for p in range(NP):
            windows_ref[p * 18 + 16 + i] = start_ref[(p * NT + t) * BLOCKS + seg[2 + i]]
        picks(W_PICK + (16 + i) * PICKS, seg[2 + i])

    def merged(at, b, m, slot):
        for n in range(2):
            v = merge_ref[((e * BLOCKS + b) * 8 + m) * 2 + n]
            windows_ref[at + n] = jnp.where(v < 0, ZERO3, v + PICKS * slot)

    g = owner_groups(own_ref, t)
    for s in range(4):
        for m in range(8):
            merged(W_MERGE + (s * 8 + m) * 2, seg[s // 2] + g[s % 2], m, s)
    for i in range(2):
        for k in range(2):
            merged(W_MERGE + 64 + (i * 2 + k) * 2, seg[2 + i], g[k], 4 + i)
    mine = jnp.where(d < 16, g[0], g[1])
    windows_ref[W_HEAD] = 2 * mine + (d % 16) // 8
    windows_ref[W_HEAD + 1] = 32 * mine + 2 * (d % 16)
    windows_ref[W_HEAD + 2] = 16 * mine + d % 16
    for shift in range(NT):
        g = owner_groups(own_ref, (t + shift) % NT)
        for i in range(2):
            for n in range(WIDTH):
                v = relay_ref[((t * BLOCKS + seg[2 + i]) * 4 + (t + shift) % NT) * WIDTH + n]
                windows_ref[W_RELAY + (shift * 2 + i) * WIDTH + n] = jnp.where(v < 0, ZERO_B, v + i * SLOT)
            for k in range(2):
                for u in range(4):
                    for n in range(2):
                        v = gathered_ref[((t * BLOCKS + seg[2 + i]) * 32 + g[k] * 4 + u) * 2 + n]
                        at = W_GATHER + shift * 32 + ((i * 2 + k) * 4 + u) * 2 + n
                        windows_ref[at] = jnp.where(v < 0, ZERO_R, v + i * WIDTH)


def iota(shape, dim):
    return lax.broadcasted_iota(jnp.int32, shape, dim)


class Table:
    def __init__(self, ref, base):
        self.ref, self.base = ref, base

    def __getitem__(self, i):
        return self.ref[self.base + i]


TABLES = np.concatenate([a.reshape(-1) for a in (START, PICK, MERGE, RELAY, GATHERED)])
BASES = np.cumsum([0, START.size, PICK.size, MERGE.size, RELAY.size])


def exchange_kernel(
    off_hbm,
    own_hbm,
    table_hbm,
    rate_hbm,
    bias_hbm,
    skip_hbm,
    gain_hbm,
    hidden_ref,
    flat_hbm,
    out_ref,
    bc_ref,
    dt_ref,
    mixed_ref,
    windows_ref,
    *scratch,
):
    loads = scratch[-9:]
    scratch = scratch[:-9]
    off_ref, own_ref, table_ref, rate_ref, bias_ref, skip_ref, gain_ref, flat_ref, load_sem = loads
    whole = [
        (flat_hbm, flat_ref),
        (off_hbm, off_ref),
        (own_hbm, own_ref),
        (table_hbm, table_ref),
        (rate_hbm, rate_ref),
        (bias_hbm, bias_ref),
        (skip_hbm, skip_ref),
        (gain_hbm, gain_ref),
    ]
    loading = [pltpu.make_async_copy(src, dst, load_sem.at[i]) for i, (src, dst) in enumerate(whole)]
    for cp in loading:
        cp.start()
    shifted = scratch[:NP]
    recv = scratch[NP : 2 * NP]
    send = scratch[2 * NP : 3 * NP]
    dtbuf, dtsend, dp_send, dp_recv, z_send, z_recv, self_sem = scratch[3 * NP : 3 * NP + 7]
    hid, prod, precv, zsend, zcom, zrecv, hsend, hrecv, bsend, brecv, qsend, qrecv = scratch[3 * NP + 7 : 3 * NP + 19]
    ag_send, ag_recv, p_send, p_recv, zp_send, zp_recv, own_sem = scratch[3 * NP + 19 : 3 * NP + 26]
    bcbuf, spread, gather, owned, b_send, b_recv, b_self = scratch[3 * NP + 26 :]
    d = lax.axis_index("dp")
    t = lax.axis_index("tensor")
    x, y, c = d // 8, (d // 2) % 4, d % 2
    e, seq = d // 2, d % 2
    chunk = d * NT + t

    barrier = pltpu.get_barrier_semaphore()

    @pl.loop(1, NDP)
    def _(i):
        pl.semaphore_signal(barrier, inc=1, device_id=((d + i) % NDP, t), device_id_type=MESH)

    @pl.loop(1, NT)
    def _(i):
        pl.semaphore_signal(barrier, inc=1, device_id=(d, (t + i) % NT), device_id_type=MESH)

    pl.semaphore_wait(barrier, NDP - 1 + NT - 1)

    def remote(src, dst, ssem, rsem, device):
        cp = pltpu.make_async_remote_copy(
            src_ref=src, dst_ref=dst, send_sem=ssem, recv_sem=rsem, device_id=device, device_id_type=MESH
        )
        cp.start()
        return cp

    def await_bytes(ref, sem):
        pltpu.make_async_copy(ref, ref, sem).wait()

    copies = []

    phase = (ROWS * chunk) % TILE

    def shift_part(p):
        a, rows = STARTS[p] * TILE, PARTS[p] * TILE
        w0, w1 = max(a - TILE, 0), min(a + rows, ROWS)
        pick = jnp.where(iota((rows, w1 - w0), 0) + (a - phase) == iota((rows, w1 - w0), 1) + w0, 1.0, 0.0)
        pick = pick.astype(BF16)

        @pl.loop(0, D // 1024)
        def _(i):
            cols = pl.ds(pl.multiple_of(i * 1024, 1024), 1024)
            moved = jnp.dot(pick, flat_ref[w0:w1, cols], preferred_element_type=F32)
            shifted[p][:, :, cols] = moved.astype(BF16).reshape(PARTS[p], TILE, 1024)

    def send_part(p):
        mine = pl.ds(d * PARTS[p], PARTS[p])
        for step in ORDER:
            peer = dp_partner(d, step)
            remote(
                shifted[p].at[:, :, pl.ds(pl.multiple_of(peer * F, F), F)],
                recv[p].at[mine],
                dp_send.at[p],
                dp_recv.at[p],
                (peer, t),
            )
        pltpu.make_async_copy(
            shifted[p].at[:, :, pl.ds(pl.multiple_of(d * F, F), F)], recv[p].at[mine], dp_recv.at[p]
        ).start()

    def forward_part(p):
        await_bytes(recv[p], dp_recv.at[p])

        def pack(dst, window, at=0):
            first = windows_ref[window]

            @pl.loop(0, CAPS[p], unroll=2)
            def _(j):
                dst[at + j] = recv[p][first + j]

        for i in range(2):
            pack(bcbuf, p * 18 + 16 + i, i * SLOT + OFFS[p])
        for l in range(max(STARTS[p], 3), STARTS[p] + PARTS[p]):
            dtbuf[l - 3] = recv[p][31 * PARTS[p] + l - STARTS[p]]
        if p >= NP - 2:
            spread_common(p - (NP - 2))
        for shift in (1, 3, 2, 0):
            for s in range(4):
                pack(send[p].at[shift, s], p * 18 + shift * 4 + s)
            src, dst = send[p].at[shift], out_ref.at[t, :, pl.ds(OFFS[p], CAPS[p])]
            to_owner(src, dst, shift, p)

    def to_owner(src, dst, shift, n):
        if shift == 0:
            cp = pltpu.make_async_copy(src, dst, self_sem.at[n])
            cp.start()
        else:
            cp = remote(src, dst, z_send.at[shift - 1, n], z_recv.at[shift - 1, n], (d, (t + shift) % NT))
        copies.append(cp)

    bcopies = []

    def spread_common(late):
        low, high = (EARLY, WIDTH) if late else (0, EARLY)
        for shift in (1, 3, 2, 0):
            for i in range(2):
                for n in range(i * WIDTH + low, i * WIDTH + high):
                    spread[shift, n] = bcbuf[windows_ref[W_RELAY + shift * 2 * WIDTH + n]]
                src = spread.at[shift, pl.ds(i * WIDTH + low, high - low)]
                dst = gather.at[pl.ds((t * 2 + i) * WIDTH + low, high - low)]
                j = 2 * late + i
                if shift == 0:
                    cp = pltpu.make_async_copy(src, dst, b_self.at[j])
                    cp.start()
                else:
                    sems = b_send.at[shift - 1, j], b_recv.at[shift - 1, j]
                    cp = remote(src, dst, *sems, (d, (t + shift) % NT))
                bcopies.append(cp)

    def share_common():
        for cp in bcopies:
            cp.wait()
        for shift in (1, 3, 2, 0):
            for n in range(16):
                at = W_GATHER + shift * 32 + 2 * n
                owned[shift, n] = gather[windows_ref[at]] + gather[windows_ref[at + 1]]
            to_owner(owned.at[shift], bc_ref.at[t], shift, NP + 1)

    def forward_dt():
        for shift in (1, 3, 2, 0):
            for i in range(2):
                for j in range(2):
                    dtsend[shift, 2 * i + j] = dtbuf[windows_ref[W_DT + shift * 2 + i] + j]
            to_owner(dtsend.at[shift], dt_ref.at[t], shift, NP)

    def along_x(i):
        return (((x + i) % 4) * 8 + y * 2 + c, t)

    def along_y(i):
        return (x * 8 + ((y + i) % 4) * 2 + c, t)

    quarter = L // NT
    pieces = []
    for first, size in ((pl.multiple_of(t * quarter, TILE), quarter // 2), (L, L // 2)):
        pieces.append((pl.ds(first, size), size, along_x, along_y))
        pieces.append((pl.ds(first + size, size), size, along_y, along_x))

    def gather_first():
        owns = []
        for n, (first, size) in enumerate(((pl.multiple_of(t * quarter, TILE), quarter), (L, L))):
            tokens = pl.ds(first, size)
            owns.append(pltpu.make_async_copy(hidden_ref.at[tokens], hid.at[x, y, c, tokens], own_sem.at[3 * n]))
            owns[n].start()
        for j, (tokens, _, partner, _) in enumerate(pieces):
            for i in (2, 1, 3):
                remote(hidden_ref.at[tokens], hid.at[x, y, c, tokens], ag_send.at[j], ag_recv.at[j], partner(i))
        for cp in owns:
            cp.wait()

    def gather_second():
        for j, (tokens, size, first, then) in enumerate(pieces):
            await_bytes(hid.at[0:3, 0, 0, 0:size], ag_recv.at[j])
            line = hid.at[:, y, c, tokens] if first is along_x else hid.at[x, :, c, tokens]
            for i in (2, 1, 3):
                remote(line, line, ag_send.at[4 + j], ag_recv.at[4 + j], then(i))

    def gather_planes():
        for j in range(2):
            await_bytes(hid.at[0:3, :, 0, 0 : pieces[j][1]], ag_recv.at[4 + j])
        part = hid.at[:, :, c, pl.ds(pl.multiple_of(t * quarter, TILE), quarter)]
        for i in (2, 1, 3):
            remote(part, part, ag_send.at[8], ag_recv.at[8], (d, (t + i) % NT))

    def gather_third():
        for j in range(2, 4):
            await_bytes(hid.at[0:3, :, 0, 0 : pieces[j][1]], ag_recv.at[4 + j])
        await_bytes(hid.at[:, :, 0, 0 : 3 * quarter], ag_recv.at[8])
        remote(hid.at[:, :, c], hid.at[:, :, c], ag_send.at[9], ag_recv.at[9], (d + 1 - 2 * c, t))

    def multiply_half(core):
        @pl.loop(0, 4)
        def _(i):
            part = jnp.zeros((CHUNK * TILE, 2 * L), F32)
            for j in range(4):
                cols = pl.ds(pl.multiple_of((i * 8 + j * 2 + core) * F, F), F)
                rows = jnp.concatenate(
                    [shifted[p][:, :, cols].reshape(PARTS[p] * TILE, F) for p in range(NP)], axis=0
                )
                part += lax.dot_general(
                    rows, hid[i, j, core], (((1,), (1,)), ((), ())), preferred_element_type=F32
                )
            for s in range(2):
                prod[s, 0:CHUNK] += part[:, s * L : (s + 1) * L].reshape(CHUNK, TILE, L)

    def multiply():
        multiply_half(c)
        await_bytes(hid.at[:, :, 0], ag_recv.at[9])
        multiply_half(1 - c)

    def product_tiles(i):
        low = (i // 2 + 16 * NDP * NT * CHUNK - first_tile(chunk)) % 16
        return low, i % 2

    def send_products():
        @pl.loop(1, NDP)
        def _(n):
            i = (d + n) % NDP
            low, s = product_tiles(i)
            for h in range(2):
                remote(prod.at[s, low + 16 * h], precv.at[2 * d + h], p_send.at[0], p_recv.at[0], (i, t))

        low, s = product_tiles(d)
        for h in range(2):
            pltpu.make_async_copy(prod.at[s, low + 16 * h], precv.at[2 * d + h], p_recv.at[0]).start()

    def forward_products():
        await_bytes(precv.at[0 : 2 * NDP], p_recv.at[0])
        for n in range(2 * PICKS):
            zcom[n] = precv[windows_ref[W_PICK + 16 * PICKS + n]]
        zcom[2 * PICKS] = precv[2 * 31 + (3 + e) // 16]
        for shift in (1, 3, 2, 0):
            for n in range(4 * PICKS):
                zsend[shift, n] = precv[windows_ref[W_PICK + shift * 4 * PICKS + n]]
            for j, (src, n0, n1) in enumerate([(zsend.at[shift], 0, 4 * PICKS), (zcom, 4 * PICKS, PT)]):
                dst = zrecv.at[pl.ds(t * PT + n0, n1 - n0)]
                if shift == 0:
                    cp = pltpu.make_async_copy(src, dst, own_sem.at[1 + j])
                    cp.start()
                else:
                    cp = remote(src, dst, zp_send.at[shift - 1, j], zp_recv.at[shift - 1, j], (d, (t + shift) % NT))
                pcopies.append(cp)

    pcopies = []

    def send_heads():
        for cp in pcopies:
            cp.wait()

        def total(at):
            return zrecv[windows_ref[at]] + zrecv[windows_ref[at + 1]]

        for k in range(2):
            for i in range(2):
                bsend[k, i] = total(W_MERGE + 64 + (i * 2 + k) * 2)
            bsend[k, 2] = zrecv[3 * PT + PT - 1]
        for k in range(2):
            for m in range(8):
                for i in range(2):
                    hsend[k * 8 + m, i] = total(W_MERGE + ((2 * i + k) * 8 + m) * 2)

        @pl.loop(1, 16)
        def _(n):
            i = (d + 2 * n) % NDP
            remote(bsend.at[i // 16], brecv.at[seq, :, e], p_send.at[1], p_recv.at[1], (i, t))

        pltpu.make_async_copy(bsend.at[d // 16], brecv.at[seq, :, e], p_recv.at[1]).start()

        @pl.loop(0, 16)
        def _(n):
            i = 16 * (n // 8) + 2 * (n % 8) + e // 8
            dst = hrecv.at[seq, :, (e // 4) % 2, e % 4]

            @pl.when(i != d)
            def _():
                remote(hsend.at[n], dst, p_send.at[2], p_recv.at[2], (i, t))

            @pl.when(i == d)
            def _():
                pltpu.make_async_copy(hsend.at[n], dst, p_recv.at[2]).start()

    high = lax.Precision.HIGHEST
    values = []

    def share_products():
        await_bytes(brecv.at[seq], p_recv.at[1])
        remote(brecv.at[seq], brecv.at[seq], p_send.at[4], p_recv.at[4], (d + 1 - 2 * c, t))

    def mix():
        await_bytes(brecv.at[seq], p_recv.at[4])
        await_bytes(hrecv, p_recv.at[2])
        head = windows_ref[W_HEAD + 1]
        lower = iota((L, L), 0) <= iota((L, L), 1)
        ones = jnp.where(lower, 1.0, 0.0).astype(F32)
        qsend[...] = jnp.zeros_like(qsend)
        for s in range(2):
            bmat = brecv[s, 0].reshape(N, L)
            cmat = brecv[s, 1].reshape(N, L)
            scores = lax.dot_general(bmat, cmat, (((0,), (0,)), ((), ())), precision=high, preferred_element_type=F32)
            raw = brecv[s, 2, windows_ref[W_HEAD]]
            squares = jnp.zeros((1, L), F32)
            for hh in range(2):
                r = 2 * (d % 8) + hh
                row = jnp.sum(jnp.where(iota((TILE, L), 0) == r, raw, 0.0), axis=0, keepdims=True)
                row = row + bias_ref[head + hh]
                step = jnp.maximum(row, 0.0) + jnp.log1p(jnp.exp(-jnp.abs(row)))
                rates = jnp.broadcast_to(step * -rate_ref[head + hh], (8, L))
                cumul = jnp.dot(rates, ones, precision=high, preferred_element_type=F32)
                across = jnp.broadcast_to(cumul[0:1], (L, L))
                diff = across - across.T
                decay = jnp.where(lower, jnp.exp(jnp.where(lower, diff, 0.0)), 0.0)
                weights = scores * decay * jnp.broadcast_to(step, (L, L)).T
                xt = hrecv[s, 1, hh].reshape(P_SIZE, L)
                zt = hrecv[s, 0, hh].reshape(P_SIZE, L)
                out = jnp.dot(xt, weights, precision=high, preferred_element_type=F32) + skip_ref[head + hh] * xt
                v = out * (zt * jax.nn.sigmoid(zt))
                squares = squares + jnp.sum(v * v, axis=0, keepdims=True)
                values.append(v)
            qsend[s : s + 1] = squares
        base = 16 * (d // 16)

        @pl.loop(1, 16)
        def _(n):
            i = base + (d + n) % 16
            remote(qsend, qrecv.at[d % 16], p_send.at[3], p_recv.at[3], (i, t))

        pltpu.make_async_copy(qsend, qrecv.at[d % 16], p_recv.at[3]).start()

    def finish():
        await_bytes(qrecv, p_recv.at[3])
        total = jnp.sum(qrecv[...], axis=0)
        scale = lax.rsqrt(total / (32 * P_SIZE) + 1e-05)
        gain = gain_ref[windows_ref[W_HEAD + 2]]
        for s in range(2):
            v = jnp.concatenate(values[2 * s : 2 * s + 2], axis=0) * scale[s : s + 1]
            mixed_ref[s * L : (s + 1) * L] = (v.T * gain).astype(BF16)

    prod[...] = jnp.zeros_like(prod)
    zero = jnp.zeros((TILE, L), F32)
    bcbuf[ZERO_B] = jnp.zeros((TILE, F), BF16)
    gather[ZERO_R] = jnp.zeros((TILE, F), BF16)
    precv[ZERO2] = zero
    zrecv[ZERO3] = zero
    gather_first()
    loading[0].wait()
    shift_part(0)
    gather_second()
    send_part(0)
    gather_planes()
    shift_part(1)
    send_part(1)
    shift_part(2)
    shift_part(3)
    shift_part(4)
    for cp in loading[1:]:
        cp.wait()
    find_windows(off_ref, own_ref, *[Table(table_ref, int(i)) for i in BASES], windows_ref)
    gather_third()
    multiply()
    send_products()
    send_part(2)
    forward_part(0)
    forward_part(1)
    send_part(3)
    forward_products()
    send_part(4)
    forward_part(2)
    send_heads()
    forward_part(3)
    share_products()
    forward_part(4)
    forward_dt()
    mix()
    share_common()
    finish()

    for cp in copies:
        cp.wait()
    for p in range(NP):
        await_bytes(shifted[p].at[:, :, 0 : (NDP - 1) * F], dp_send.at[p])
    for j, (_, size, _, _) in enumerate(pieces):
        await_bytes(hid.at[0:3, 0, 0, 0:size], ag_send.at[j])
        await_bytes(hid.at[0:3, :, 0, 0:size], ag_send.at[4 + j])
    await_bytes(hid.at[:, :, 0, 0 : 3 * quarter], ag_send.at[8])
    await_bytes(hid.at[:, :, 0], ag_send.at[9])
    await_bytes(precv.at[0 : 2 * (NDP - 1)], p_send.at[0])
    await_bytes(brecv.at[1, :, 0:15], p_send.at[1])
    await_bytes(brecv.at[1], p_send.at[4])
    itself = seq == e // 8

    @pl.when(itself)
    def _():
        await_bytes(hsend.at[0:15], p_send.at[2])

    @pl.when(jnp.logical_not(itself))
    def _():
        await_bytes(hsend, p_send.at[2])

    await_bytes(qrecv.at[0:15], p_send.at[3])


def exchange(offsets, owner, rate, bias, skip, gain, hidden, flat):
    hbm = pl.BlockSpec(memory_space=pltpu.HBM)
    vmem = pl.BlockSpec(memory_space=pltpu.VMEM)
    dma = pltpu.SemaphoreType.DMA
    return pl.pallas_call(
        exchange_kernel,
        out_shape=(
            pltpu.VMEM((NT, 4, SLOT, TILE, F), BF16),
            pltpu.VMEM((NT, 16, TILE, F), BF16),
            pltpu.VMEM((NT, 4, TILE, F), BF16),
            jax.ShapeDtypeStruct((2 * L, L), BF16),
        ),
        in_specs=[hbm] * 9,
        out_specs=(vmem,) * 4,
        scratch_shapes=[pltpu.SMEM((W_SIZE,), jnp.int32)]
        + [pltpu.VMEM((w, TILE, D), BF16) for w in PARTS]
        + [pltpu.VMEM((NDP * w, TILE, F), BF16) for w in PARTS]
        + [pltpu.VMEM((NT, 4, c, TILE, F), BF16) for c in CAPS]
        + [
            pltpu.VMEM((16, TILE, F), BF16),
            pltpu.VMEM((NT, 4, TILE, F), BF16),
            dma((NP,)),
            dma((NP,)),
            dma((NT - 1, NP + 2)),
            dma((NT - 1, NP + 2)),
            dma((NP + 2,)),
            pltpu.VMEM((4, 4, 2, 2 * L, F), BF16),
            pltpu.VMEM((2, 32, TILE, L), F32),
            pltpu.VMEM((ZERO2 + 1, TILE, L), F32),
            pltpu.VMEM((NT, 4 * PICKS, TILE, L), F32),
            pltpu.VMEM((2 * PICKS + 1, TILE, L), F32),
            pltpu.VMEM((ZERO3 + 1, TILE, L), F32),
            pltpu.VMEM((16, 2, TILE, L), F32),
            pltpu.VMEM((2, 2, 2, 4, TILE, L), F32),
            pltpu.VMEM((2, 3, TILE, L), F32),
            pltpu.VMEM((2, 3, 16, TILE, L), F32),
            pltpu.VMEM((8, L), F32),
            pltpu.VMEM((16, 8, L), F32),
            dma((10,)),
            dma((10,)),
            dma((5,)),
            dma((5,)),
            dma((NT - 1, 2)),
            dma((NT - 1, 2)),
            dma((4,)),
            pltpu.VMEM((ZERO_B + 1, TILE, F), BF16),
            pltpu.VMEM((NT, 2 * WIDTH, TILE, F), BF16),
            pltpu.VMEM((ZERO_R + 1, TILE, F), BF16),
            pltpu.VMEM((NT, 16, TILE, F), BF16),
            dma((NT - 1, 4)),
            dma((NT - 1, 4)),
            dma((4,)),
            pltpu.SMEM((5,), jnp.int32),
            pltpu.SMEM((G,), jnp.int32),
            pltpu.SMEM(TABLES.shape, jnp.int32),
            pltpu.SMEM((H,), F32),
            pltpu.SMEM((H,), F32),
            pltpu.SMEM((H,), F32),
            pltpu.VMEM((H // 2, 1, 2 * P_SIZE), F32),
            pltpu.VMEM((ROWS, D), BF16),
            dma((8,)),
        ],
        compiler_params=pltpu.CompilerParams(
            collective_id=1, has_side_effects=True, vmem_limit_bytes=58 << 20
        ),
        name="exchange",
    )(offsets, owner, jnp.asarray(TABLES), rate, bias, skip, gain, hidden, flat)


STEP = 64


def place_kernel(off_ref, own_ref, place_ref, got_ref, bc_ref, dt_ref, out_ref):
    step = pl.program_id(0)
    g = owner_groups(own_ref, lax.axis_index("tensor"))

    @pl.when(step < 8)
    def _():
        k = step // 4
        gk = jnp.where(k == 0, g[0], g[1])
        for seg in range(2):
            block = off_ref[seg] // 2048 + gk
            slot = (2 * seg + k) * SLOT
            first = block * BT + (step % 4) * 32
            for j in range(0, 8, 2):
                tiles = [got_ref[place_ref[first + 4 * j + q] + slot] for q in range(8)]
                for q in range(8):
                    out_ref[(j + q // 4) * 8 + seg * 4 + q % 4] = tiles[q]
            for n in range(FIXES):
                at = BLOCKS * BT + ((block * 4 + step % 4) * FIXES + n) * 3
                q = place_ref[at]

                @pl.when(q >= 0)
                def _():
                    both = got_ref[place_ref[at + 1] + slot] + got_ref[place_ref[at + 2] + slot]
                    out_ref[(q // 4) * 8 + seg * 4 + q % 4] = both

    @pl.when(step == 8)
    def _():
        for n in range(4):
            for q in range(16):
                out_ref[n * 16 + q] = bc_ref[q % 4, n * 4 + q // 4]

    @pl.when(step == 9)
    def _():
        for j in range(4):
            out_ref[j] = dt_ref[3, j]


def place(offsets, group_owner, got, bc, dt):
    smem = pl.BlockSpec(memory_space=pltpu.SMEM)
    table = jnp.asarray(np.concatenate([PLACE[:, :, 0].reshape(-1), FIX.reshape(-1)]))
    got = got.reshape(NT * 4 * SLOT, TILE, F)
    rows = pl.pallas_call(
        place_kernel,
        grid=(10,),
        out_shape=jax.ShapeDtypeStruct((580, TILE, F), BF16),
        in_specs=[
            smem,
            smem,
            smem,
            pl.BlockSpec(memory_space=pltpu.VMEM),
            pl.BlockSpec(memory_space=pltpu.VMEM),
            pl.BlockSpec(memory_space=pltpu.VMEM),
        ],
        out_specs=pl.BlockSpec((STEP, TILE, F), lambda i: (i, 0, 0)),
        compiler_params=pltpu.CompilerParams(vmem_limit_bytes=16 << 20),
        name="place",
    )(offsets, group_owner, table, got, bc, dt)
    return rows.reshape(580 * TILE, F).T


def shards(flat_weight, offsets, group_owner, hidden, decay_rate, dt_bias, skip_gain, norm_gain):
    gain = norm_gain.reshape(H // 2, 1, 2 * P_SIZE)
    got, bc, dt_rows, mixed = exchange(
        offsets, group_owner, decay_rate, dt_bias, skip_gain, gain, hidden, flat_weight
    )
    return place(offsets, group_owner, got, bc, dt_rows), mixed


def solution(mesh):
    placed = (P(("dp", "tensor"), None), P(), P(), P(None, "dp"), P(), P(), P(), P())
    return jax.shard_map(
        shards,
        mesh=mesh,
        in_specs=placed,
        out_specs=(P("dp", "tensor"), P(None, ("dp", "tensor"))),
        check_vma=False,
    )
```

```python
import functools

import jax
import jax.numpy as jnp
import numpy as np
from jax import lax
from jax.experimental import pallas as pl
from jax.experimental.pallas import tpu as pltpu
from jax.sharding import PartitionSpec as P

H = 256
P_SIZE = 64
N = 256
G = 8
L = 128
ROWS = 290
D = 8192
F = 256
NDP = 32
NT = 4
TILE = 16
CHUNK = 19
BLOCKS = 18
BT = 128
PARTS = (4, 4, 4, 4, 3)
STARTS = (0, 4, 8, 12, 16)
COMMON = (0, 1, 8, 9, 16, 17)
MESH = pl.DeviceIdType.MESH
BF16 = jnp.bfloat16
F32 = jnp.float32


def first_tile(chunk):
    return ROWS * chunk // TILE


def make_tables():
    n = len(PARTS)
    lo = np.full((n, NT, BLOCKS), 10**6)
    hi = np.full((n, NT, BLOCKS), -1)
    where = {}
    for k in range(NDP * NT):
        for l in range(CHUNK):
            p = max(i for i in range(n) if STARTS[i] <= l)
            b, tau = divmod(first_tile(k) + l, BT)
            if b >= BLOCKS:
                continue
            i = (k // NT) * PARTS[p] + l - STARTS[p]
            where.setdefault((b, tau), []).append((k % NT, p, i))
            lo[p, k % NT, b] = min(lo[p, k % NT, b], i)
            hi[p, k % NT, b] = max(hi[p, k % NT, b], i)
    caps = [int((hi[p] - lo[p] + 1).max()) for p in range(n)]
    start = np.zeros((n, NT, BLOCKS), np.int32)
    for p in range(n):
        start[p] = np.clip(lo[p], 0, NDP * PARTS[p] - caps[p])
    offs = np.concatenate([[0], np.cumsum(caps)])
    slot = int(offs[-1])
    place = np.full((BLOCKS, BT, 2), -1, np.int32)
    for (b, tau), found in where.items():
        for e, (t, p, i) in enumerate(found):
            place[b, tau, e] = t * 4 * slot + offs[p] + i - start[p, t, b]
    spread = {}
    for (b, tau), found in sorted(where.items()):
        for t, p, i in found:
            if b in COMMON:
                key = (t, b, tau % 4)
                spread.setdefault(key, ([], []))[int(p == n - 1)].append((tau, offs[p] + i - start[p, t, b]))
    early = max(len(v[0]) for v in spread.values())
    width = early + max(len(v[1]) for v in spread.values())
    relay = np.full((NT, BLOCKS, 4, width), -1, np.int32)
    gathered = np.full((4, BLOCKS, 32, 2), -1, np.int32)
    for (t, b, r), found in spread.items():
        for m, tiles in enumerate(found):
            for j, (tau, at) in enumerate(tiles, m * early):
                relay[t, b, r, j] = at
                e = int(gathered[r, b, tau // 4, 0] >= 0)
                gathered[r, b, tau // 4, e] = t * 2 * width + j
    return caps, [int(o) for o in offs], slot, start, place, early, width, relay, gathered


PICKS = 3
PT = 6 * PICKS + 1
ZERO2 = 2 * NDP
ZERO3 = NT * PT


def make_product_tables():
    pick = np.full((NT, 16, BLOCKS, PICKS), ZERO2, np.int32)
    merge = np.full((16, BLOCKS, 8, 2), -1, np.int32)
    count = np.zeros((NT, 16, BLOCKS), np.int32)
    seen = np.zeros((16, BLOCKS, 8), np.int32)
    for k in range(NDP * NT):
        for l in range(CHUNK):
            tile = first_tile(k) + l
            b, tau = divmod(tile, BT)
            if b >= BLOCKS:
                continue
            t, e, m = k % NT, tau % 16, tau // 16
            n = count[t, e, b]
            pick[t, e, b, n] = (k // NT) * 2 + l // 16
            merge[e, b, m, seen[e, b, m]] = t * PT + n
            count[t, e, b] += 1
            seen[e, b, m] += 1
    return pick, merge


CAPS, OFFS, SLOT, START, PLACE, EARLY, WIDTH, RELAY, GATHERED = make_tables()
PICK, MERGE = make_product_tables()
NP = len(PARTS)
FIXES = 2


def make_fixes():
    fixes = np.full((BLOCKS, 4, FIXES, 3), -1, np.int32)
    for b in range(BLOCKS):
        for quarter in range(4):
            found = [q for q in range(32) if PLACE[b, quarter * 32 + q, 1] >= 0]
            for n, q in enumerate(found):
                fixes[b, quarter, n] = q, *PLACE[b, quarter * 32 + q]
    return fixes


FIX = make_fixes()
W_DT = NP * 18
W_PICK = W_DT + 8
W_MERGE = W_PICK + 18 * PICKS
W_HEAD = W_MERGE + 72
W_RELAY = W_HEAD + 3
W_GATHER = W_RELAY + 8 * WIDTH
W_SIZE = W_GATHER + NT * 32
ZERO_B = 2 * SLOT
ZERO_R = NT * 2 * WIDTH


def dp_order():
    steps = [(a, b, c) for a in range(4) for b in range(4) for c in range(2) if (a, b, c) != (0, 0, 0)]
    steps.sort(key=lambda s: -(min(s[0], 4 - s[0]) + min(s[1], 4 - s[1])))
    out = []
    for a, b, c in steps:
        for q in ((a, b, c), (b, a, c), (-a % 4, -b % 4, c), (-b % 4, -a % 4, c)):
            if q not in out:
                out.append(q)
    return out


ORDER = dp_order()


def dp_partner(d, step):
    x, y, c = d // 8, (d // 2) % 4, d % 2
    return ((x + step[0]) % 4) * 8 + ((y + step[1]) % 4) * 2 + (c + step[2]) % 2


def owner_groups(owner_ref, owner):
    first, last = jnp.int32(G), jnp.int32(-1)
    for g in range(G):
        mine = owner_ref[g] == owner
        first = jnp.where(mine, jnp.minimum(first, g), first)
        last = jnp.where(mine, g, last)
    return jnp.clip(first, 0, G - 1), jnp.clip(last, 0, G - 1)


def find_windows(
    off_ref, own_ref, start_ref, pick_ref, merge_ref, relay_ref, gathered_ref, windows_ref
):
    d = lax.axis_index("dp")
    t = lax.axis_index("tensor")
    e = d // 2
    seg = [off_ref[i] // 2048 for i in range(4)]

    def picks(at, b):
        for n in range(PICKS):
            windows_ref[at + n] = pick_ref[((t * 16 + e) * BLOCKS + b) * PICKS + n]

    for shift in range(NT):
        g = owner_groups(own_ref, (t + shift) % NT)
        for s in range(4):
            b = seg[s // 2] + g[s % 2]
            for p in range(NP):
                windows_ref[p * 18 + shift * 4 + s] = start_ref[(p * NT + t) * BLOCKS + b]
            picks(W_PICK + (shift * 4 + s) * PICKS, b)
        for i in range(2):
            windows_ref[W_DT + shift * 2 + i] = 2 * g[i]
    for i in range(2):
        for p in range(NP):
            windows_ref[p * 18 + 16 + i] = start_ref[(p * NT + t) * BLOCKS + seg[2 + i]]
        picks(W_PICK + (16 + i) * PICKS, seg[2 + i])

    def merged(at, b, m, slot):
        for n in range(2):
            v = merge_ref[((e * BLOCKS + b) * 8 + m) * 2 + n]
            windows_ref[at + n] = jnp.where(v < 0, ZERO3, v + PICKS * slot)

    g = owner_groups(own_ref, t)
    for s in range(4):
        for m in range(8):
            merged(W_MERGE + (s * 8 + m) * 2, seg[s // 2] + g[s % 2], m, s)
    for i in range(2):
        for k in range(2):
            merged(W_MERGE + 64 + (i * 2 + k) * 2, seg[2 + i], g[k], 4 + i)
    mine = jnp.where(d < 16, g[0], g[1])
    windows_ref[W_HEAD] = 2 * mine + (d % 16) // 8
    windows_ref[W_HEAD + 1] = 32 * mine + 2 * (d % 16)
    windows_ref[W_HEAD + 2] = 16 * mine + d % 16
    for shift in range(NT):
        g = owner_groups(own_ref, (t + shift) % NT)
        for i in range(2):
            for n in range(WIDTH):
                v = relay_ref[((t * BLOCKS + seg[2 + i]) * 4 + (t + shift) % NT) * WIDTH + n]
                windows_ref[W_RELAY + (shift * 2 + i) * WIDTH + n] = jnp.where(v < 0, ZERO_B, v + i * SLOT)
            for k in range(2):
                for u in range(4):
                    for n in range(2):
                        v = gathered_ref[((t * BLOCKS + seg[2 + i]) * 32 + g[k] * 4 + u) * 2 + n]
                        at = W_GATHER + shift * 32 + ((i * 2 + k) * 4 + u) * 2 + n
                        windows_ref[at] = jnp.where(v < 0, ZERO_R, v + i * WIDTH)


def iota(shape, dim):
    return lax.broadcasted_iota(jnp.int32, shape, dim)


class Table:
    def __init__(self, ref, base):
        self.ref, self.base = ref, base

    def __getitem__(self, i):
        return self.ref[self.base + i]


TABLES = np.concatenate([a.reshape(-1) for a in (START, PICK, MERGE, RELAY, GATHERED)])
BASES = np.cumsum([0, START.size, PICK.size, MERGE.size, RELAY.size])


def exchange_kernel(
    off_hbm,
    own_hbm,
    table_hbm,
    rate_hbm,
    bias_hbm,
    skip_hbm,
    gain_hbm,
    hidden_ref,
    flat_hbm,
    out_ref,
    bc_ref,
    dt_ref,
    mixed_ref,
    windows_ref,
    *scratch,
):
    loads = scratch[-9:]
    scratch = scratch[:-9]
    off_ref, own_ref, table_ref, rate_ref, bias_ref, skip_ref, gain_ref, flat_ref, load_sem = loads
    whole = [
        (flat_hbm, flat_ref),
        (off_hbm, off_ref),
        (own_hbm, own_ref),
        (table_hbm, table_ref),
        (rate_hbm, rate_ref),
        (bias_hbm, bias_ref),
        (skip_hbm, skip_ref),
        (gain_hbm, gain_ref),
    ]
    loading = [pltpu.make_async_copy(src, dst, load_sem.at[i]) for i, (src, dst) in enumerate(whole)]
    for cp in loading:
        cp.start()
    shifted = scratch[:NP]
    recv = scratch[NP : 2 * NP]
    send = scratch[2 * NP : 3 * NP]
    dtbuf, dtsend, dp_send, dp_recv, z_send, z_recv, self_sem = scratch[3 * NP : 3 * NP + 7]
    hid, prod, precv, zsend, zcom, zrecv, hsend, hrecv, bsend, brecv, qsend, qrecv = scratch[3 * NP + 7 : 3 * NP + 19]
    ag_send, ag_recv, p_send, p_recv, zp_send, zp_recv, own_sem = scratch[3 * NP + 19 : 3 * NP + 26]
    bcbuf, spread, gather, owned, b_send, b_recv, b_self = scratch[3 * NP + 26 :]
    d = lax.axis_index("dp")
    t = lax.axis_index("tensor")
    x, y, c = d // 8, (d // 2) % 4, d % 2
    e, seq = d // 2, d % 2
    chunk = d * NT + t

    barrier = pltpu.get_barrier_semaphore()

    @pl.loop(1, NDP)
    def _(i):
        pl.semaphore_signal(barrier, inc=1, device_id=((d + i) % NDP, t), device_id_type=MESH)

    @pl.loop(1, NT)
    def _(i):
        pl.semaphore_signal(barrier, inc=1, device_id=(d, (t + i) % NT), device_id_type=MESH)

    pl.semaphore_wait(barrier, NDP - 1 + NT - 1)

    def remote(src, dst, ssem, rsem, device):
        cp = pltpu.make_async_remote_copy(
            src_ref=src, dst_ref=dst, send_sem=ssem, recv_sem=rsem, device_id=device, device_id_type=MESH
        )
        cp.start()
        return cp

    def await_bytes(ref, sem):
        pltpu.make_async_copy(ref, ref, sem).wait()

    copies = []

    phase = (ROWS * chunk) % TILE

    def shift_part(p):
        a, rows = STARTS[p] * TILE, PARTS[p] * TILE
        w0, w1 = max(a - TILE, 0), min(a + rows, ROWS)
        pick = jnp.where(iota((rows, w1 - w0), 0) + (a - phase) == iota((rows, w1 - w0), 1) + w0, 1.0, 0.0)
        pick = pick.astype(BF16)

        @pl.loop(0, D // 1024)
        def _(i):
            cols = pl.ds(pl.multiple_of(i * 1024, 1024), 1024)
            moved = jnp.dot(pick, flat_ref[w0:w1, cols], preferred_element_type=F32)
            shifted[p][:, :, cols] = moved.astype(BF16).reshape(PARTS[p], TILE, 1024)

    def send_part(p):
        mine = pl.ds(d * PARTS[p], PARTS[p])
        for step in ORDER:
            peer = dp_partner(d, step)
            remote(
                shifted[p].at[:, :, pl.ds(pl.multiple_of(peer * F, F), F)],
                recv[p].at[mine],
                dp_send.at[p],
                dp_recv.at[p],
                (peer, t),
            )
        pltpu.make_async_copy(
            shifted[p].at[:, :, pl.ds(pl.multiple_of(d * F, F), F)], recv[p].at[mine], dp_recv.at[p]
        ).start()

    def forward_part(p):
        await_bytes(recv[p], dp_recv.at[p])

        def pack(dst, window, at=0):
            first = windows_ref[window]

            @pl.loop(0, CAPS[p], unroll=2)
            def _(j):
                dst[at + j] = recv[p][first + j]

        for i in range(2):
            pack(bcbuf, p * 18 + 16 + i, i * SLOT + OFFS[p])
        for l in range(max(STARTS[p], 3), STARTS[p] + PARTS[p]):
            dtbuf[l - 3] = recv[p][31 * PARTS[p] + l - STARTS[p]]
        if p >= NP - 2:
            spread_common(p - (NP - 2))
        for shift in (1, 3, 2, 0):
            for s in range(4):
                pack(send[p].at[shift, s], p * 18 + shift * 4 + s)
            src, dst = send[p].at[shift], out_ref.at[t, :, pl.ds(OFFS[p], CAPS[p])]
            to_owner(src, dst, shift, p)

    def to_owner(src, dst, shift, n):
        if shift == 0:
            cp = pltpu.make_async_copy(src, dst, self_sem.at[n])
            cp.start()
        else:
            cp = remote(src, dst, z_send.at[shift - 1, n], z_recv.at[shift - 1, n], (d, (t + shift) % NT))
        copies.append(cp)

    bcopies = []

    def spread_common(late):
        low, high = (EARLY, WIDTH) if late else (0, EARLY)
        for shift in (1, 3, 2, 0):
            for i in range(2):
                for n in range(i * WIDTH + low, i * WIDTH + high):
                    spread[shift, n] = bcbuf[windows_ref[W_RELAY + shift * 2 * WIDTH + n]]
                src = spread.at[shift, pl.ds(i * WIDTH + low, high - low)]
                dst = gather.at[pl.ds((t * 2 + i) * WIDTH + low, high - low)]
                j = 2 * late + i
                if shift == 0:
                    cp = pltpu.make_async_copy(src, dst, b_self.at[j])
                    cp.start()
                else:
                    sems = b_send.at[shift - 1, j], b_recv.at[shift - 1, j]
                    cp = remote(src, dst, *sems, (d, (t + shift) % NT))
                bcopies.append(cp)

    def share_common():
        for cp in bcopies:
            cp.wait()
        for shift in (1, 3, 2, 0):
            for n in range(16):
                at = W_GATHER + shift * 32 + 2 * n
                owned[shift, n] = gather[windows_ref[at]] + gather[windows_ref[at + 1]]
            to_owner(owned.at[shift], bc_ref.at[t], shift, NP + 1)

    def forward_dt():
        for shift in (1, 3, 2, 0):
            for i in range(2):
                for j in range(2):
                    dtsend[shift, 2 * i + j] = dtbuf[windows_ref[W_DT + shift * 2 + i] + j]
            to_owner(dtsend.at[shift], dt_ref.at[t], shift, NP)

    def along_x(i):
        return (((x + i) % 4) * 8 + y * 2 + c, t)

    def along_y(i):
        return (x * 8 + ((y + i) % 4) * 2 + c, t)

    quarter = L // NT
    pieces = []
    for first, size in ((pl.multiple_of(t * quarter, TILE), quarter // 2), (L, L // 2)):
        pieces.append((pl.ds(first, size), size, along_x, along_y))
        pieces.append((pl.ds(first + size, size), size, along_y, along_x))

    def gather_first():
        owns = []
        for n, (first, size) in enumerate(((pl.multiple_of(t * quarter, TILE), quarter), (L, L))):
            tokens = pl.ds(first, size)
            owns.append(pltpu.make_async_copy(hidden_ref.at[tokens], hid.at[x, y, c, tokens], own_sem.at[3 * n]))
            owns[n].start()
        for j, (tokens, _, partner, _) in enumerate(pieces):
            for i in (2, 1, 3):
                remote(hidden_ref.at[tokens], hid.at[x, y, c, tokens], ag_send.at[j], ag_recv.at[j], partner(i))
        for cp in owns:
            cp.wait()

    def gather_second():
        for j, (tokens, size, first, then) in enumerate(pieces):
            await_bytes(hid.at[0:3, 0, 0, 0:size], ag_recv.at[j])
            line = hid.at[:, y, c, tokens] if first is along_x else hid.at[x, :, c, tokens]
            for i in (2, 1, 3):
                remote(line, line, ag_send.at[4 + j], ag_recv.at[4 + j], then(i))

    def gather_planes():
        for j in range(2):
            await_bytes(hid.at[0:3, :, 0, 0 : pieces[j][1]], ag_recv.at[4 + j])
        part = hid.at[:, :, c, pl.ds(pl.multiple_of(t * quarter, TILE), quarter)]
        for i in (2, 1, 3):
            remote(part, part, ag_send.at[8], ag_recv.at[8], (d, (t + i) % NT))

    def gather_third():
        for j in range(2, 4):
            await_bytes(hid.at[0:3, :, 0, 0 : pieces[j][1]], ag_recv.at[4 + j])
        await_bytes(hid.at[:, :, 0, 0 : 3 * quarter], ag_recv.at[8])
        remote(hid.at[:, :, c], hid.at[:, :, c], ag_send.at[9], ag_recv.at[9], (d + 1 - 2 * c, t))

    def multiply_half(core):
        @pl.loop(0, 4)
        def _(i):
            part = jnp.zeros((CHUNK * TILE, 2 * L), F32)
            for j in range(4):
                cols = pl.ds(pl.multiple_of((i * 8 + j * 2 + core) * F, F), F)
                rows = jnp.concatenate(
                    [shifted[p][:, :, cols].reshape(PARTS[p] * TILE, F) for p in range(NP)], axis=0
                )
                part += lax.dot_general(
                    rows, hid[i, j, core], (((1,), (1,)), ((), ())), preferred_element_type=F32
                )
            for s in range(2):
                prod[s, 0:CHUNK] += part[:, s * L : (s + 1) * L].reshape(CHUNK, TILE, L)

    def multiply():
        multiply_half(c)
        await_bytes(hid.at[:, :, 0], ag_recv.at[9])
        multiply_half(1 - c)

    def product_tiles(i):
        low = (i // 2 + 16 * NDP * NT * CHUNK - first_tile(chunk)) % 16
        return low, i % 2

    def send_products():
        @pl.loop(1, NDP)
        def _(n):
            i = (d + n) % NDP
            low, s = product_tiles(i)
            for h in range(2):
                remote(prod.at[s, low + 16 * h], precv.at[2 * d + h], p_send.at[0], p_recv.at[0], (i, t))

        low, s = product_tiles(d)
        for h in range(2):
            pltpu.make_async_copy(prod.at[s, low + 16 * h], precv.at[2 * d + h], p_recv.at[0]).start()

    def forward_products():
        await_bytes(precv.at[0 : 2 * NDP], p_recv.at[0])
        for n in range(2 * PICKS):
            zcom[n] = precv[windows_ref[W_PICK + 16 * PICKS + n]]
        zcom[2 * PICKS] = precv[2 * 31 + (3 + e) // 16]
        for shift in (1, 3, 2, 0):
            for n in range(4 * PICKS):
                zsend[shift, n] = precv[windows_ref[W_PICK + shift * 4 * PICKS + n]]
            for j, (src, n0, n1) in enumerate([(zsend.at[shift], 0, 4 * PICKS), (zcom, 4 * PICKS, PT)]):
                dst = zrecv.at[pl.ds(t * PT + n0, n1 - n0)]
                if shift == 0:
                    cp = pltpu.make_async_copy(src, dst, own_sem.at[1 + j])
                    cp.start()
                else:
                    cp = remote(src, dst, zp_send.at[shift - 1, j], zp_recv.at[shift - 1, j], (d, (t + shift) % NT))
                pcopies.append(cp)

    pcopies = []

    def send_heads():
        for cp in pcopies:
            cp.wait()

        def total(at):
            return zrecv[windows_ref[at]] + zrecv[windows_ref[at + 1]]

        for k in range(2):
            for i in range(2):
                bsend[k, i] = total(W_MERGE + 64 + (i * 2 + k) * 2)
            bsend[k, 2] = zrecv[3 * PT + PT - 1]
        for k in range(2):
            for m in range(8):
                for i in range(2):
                    hsend[k * 8 + m, i] = total(W_MERGE + ((2 * i + k) * 8 + m) * 2)

        @pl.loop(1, 16)
        def _(n):
            i = (d + 2 * n) % NDP
            remote(bsend.at[i // 16], brecv.at[seq, :, e], p_send.at[1], p_recv.at[1], (i, t))

        pltpu.make_async_copy(bsend.at[d // 16], brecv.at[seq, :, e], p_recv.at[1]).start()

        @pl.loop(0, 16)
        def _(n):
            i = 16 * (n // 8) + 2 * (n % 8) + e // 8
            dst = hrecv.at[seq, :, (e // 4) % 2, e % 4]

            @pl.when(i != d)
            def _():
                remote(hsend.at[n], dst, p_send.at[2], p_recv.at[2], (i, t))

            @pl.when(i == d)
            def _():
                pltpu.make_async_copy(hsend.at[n], dst, p_recv.at[2]).start()

    high = lax.Precision.HIGHEST
    values = []

    def share_products():
        await_bytes(brecv.at[seq], p_recv.at[1])
        remote(brecv.at[seq], brecv.at[seq], p_send.at[4], p_recv.at[4], (d + 1 - 2 * c, t))

    def mix():
        await_bytes(brecv.at[seq], p_recv.at[4])
        await_bytes(hrecv, p_recv.at[2])
        head = windows_ref[W_HEAD + 1]
        lower = iota((L, L), 0) <= iota((L, L), 1)
        ones = jnp.where(lower, 1.0, 0.0).astype(F32)
        qsend[...] = jnp.zeros_like(qsend)
        for s in range(2):
            bmat = brecv[s, 0].reshape(N, L)
            cmat = brecv[s, 1].reshape(N, L)
            scores = lax.dot_general(bmat, cmat, (((0,), (0,)), ((), ())), precision=high, preferred_element_type=F32)
            raw = brecv[s, 2, windows_ref[W_HEAD]]
            squares = jnp.zeros((1, L), F32)
            for hh in range(2):
                r = 2 * (d % 8) + hh
                row = jnp.sum(jnp.where(iota((TILE, L), 0) == r, raw, 0.0), axis=0, keepdims=True)
                row = row + bias_ref[head + hh]
                step = jnp.maximum(row, 0.0) + jnp.log1p(jnp.exp(-jnp.abs(row)))
                rates = jnp.broadcast_to(step * -rate_ref[head + hh], (8, L))
                cumul = jnp.dot(rates, ones, precision=high, preferred_element_type=F32)
                across = jnp.broadcast_to(cumul[0:1], (L, L))
                diff = across - across.T
                decay = jnp.where(lower, jnp.exp(jnp.where(lower, diff, 0.0)), 0.0)
                weights = scores * decay * jnp.broadcast_to(step, (L, L)).T
                xt = hrecv[s, 1, hh].reshape(P_SIZE, L)
                zt = hrecv[s, 0, hh].reshape(P_SIZE, L)
                out = jnp.dot(xt, weights, precision=high, preferred_element_type=F32) + skip_ref[head + hh] * xt
                v = out * (zt * jax.nn.sigmoid(zt))
                squares = squares + jnp.sum(v * v, axis=0, keepdims=True)
                values.append(v)
            qsend[s : s + 1] = squares
        base = 16 * (d // 16)

        @pl.loop(1, 16)
        def _(n):
            i = base + (d + n) % 16
            remote(qsend, qrecv.at[d % 16], p_send.at[3], p_recv.at[3], (i, t))

        pltpu.make_async_copy(qsend, qrecv.at[d % 16], p_recv.at[3]).start()

    def finish():
        await_bytes(qrecv, p_recv.at[3])
        total = jnp.sum(qrecv[...], axis=0)
        scale = lax.rsqrt(total / (32 * P_SIZE) + 1e-05)
        gain = gain_ref[windows_ref[W_HEAD + 2]]
        for s in range(2):
            v = jnp.concatenate(values[2 * s : 2 * s + 2], axis=0) * scale[s : s + 1]
            mixed_ref[s * L : (s + 1) * L] = (v.T * gain).astype(BF16)

    prod[...] = jnp.zeros_like(prod)
    zero = jnp.zeros((TILE, L), F32)
    bcbuf[ZERO_B] = jnp.zeros((TILE, F), BF16)
    gather[ZERO_R] = jnp.zeros((TILE, F), BF16)
    precv[ZERO2] = zero
    zrecv[ZERO3] = zero
    gather_first()
    loading[0].wait()
    shift_part(0)
    gather_second()
    send_part(0)
    gather_planes()
    shift_part(1)
    send_part(1)
    shift_part(2)
    shift_part(3)
    shift_part(4)
    for cp in loading[1:]:
        cp.wait()
    find_windows(off_ref, own_ref, *[Table(table_ref, int(i)) for i in BASES], windows_ref)
    gather_third()
    multiply()
    send_products()
    send_part(2)
    forward_part(0)
    forward_part(1)
    send_part(3)
    forward_products()
    send_part(4)
    forward_part(2)
    send_heads()
    forward_part(3)
    share_products()
    forward_part(4)
    forward_dt()
    mix()
    share_common()
    finish()

    for cp in copies:
        cp.wait()
    for p in range(NP):
        await_bytes(shifted[p].at[:, :, 0 : (NDP - 1) * F], dp_send.at[p])
    for j, (_, size, _, _) in enumerate(pieces):
        await_bytes(hid.at[0:3, 0, 0, 0:size], ag_send.at[j])
        await_bytes(hid.at[0:3, :, 0, 0:size], ag_send.at[4 + j])
    await_bytes(hid.at[:, :, 0, 0 : 3 * quarter], ag_send.at[8])
    await_bytes(hid.at[:, :, 0], ag_send.at[9])
    await_bytes(precv.at[0 : 2 * (NDP - 1)], p_send.at[0])
    await_bytes(brecv.at[1, :, 0:15], p_send.at[1])
    await_bytes(brecv.at[1], p_send.at[4])
    itself = seq == e // 8

    @pl.when(itself)
    def _():
        await_bytes(hsend.at[0:15], p_send.at[2])

    @pl.when(jnp.logical_not(itself))
    def _():
        await_bytes(hsend, p_send.at[2])

    await_bytes(qrecv.at[0:15], p_send.at[3])


def exchange(offsets, owner, rate, bias, skip, gain, hidden, flat):
    hbm = pl.BlockSpec(memory_space=pltpu.HBM)
    vmem = pl.BlockSpec(memory_space=pltpu.VMEM)
    dma = pltpu.SemaphoreType.DMA
    return pl.pallas_call(
        exchange_kernel,
        out_shape=(
            pltpu.VMEM((NT, 4, SLOT, TILE, F), BF16),
            pltpu.VMEM((NT, 16, TILE, F), BF16),
            pltpu.VMEM((NT, 4, TILE, F), BF16),
            jax.ShapeDtypeStruct((2 * L, L), BF16),
        ),
        in_specs=[hbm] * 9,
        out_specs=(vmem,) * 4,
        scratch_shapes=[pltpu.SMEM((W_SIZE,), jnp.int32)]
        + [pltpu.VMEM((w, TILE, D), BF16) for w in PARTS]
        + [pltpu.VMEM((NDP * w, TILE, F), BF16) for w in PARTS]
        + [pltpu.VMEM((NT, 4, c, TILE, F), BF16) for c in CAPS]
        + [
            pltpu.VMEM((16, TILE, F), BF16),
            pltpu.VMEM((NT, 4, TILE, F), BF16),
            dma((NP,)),
            dma((NP,)),
            dma((NT - 1, NP + 2)),
            dma((NT - 1, NP + 2)),
            dma((NP + 2,)),
            pltpu.VMEM((4, 4, 2, 2 * L, F), BF16),
            pltpu.VMEM((2, 32, TILE, L), F32),
            pltpu.VMEM((ZERO2 + 1, TILE, L), F32),
            pltpu.VMEM((NT, 4 * PICKS, TILE, L), F32),
            pltpu.VMEM((2 * PICKS + 1, TILE, L), F32),
            pltpu.VMEM((ZERO3 + 1, TILE, L), F32),
            pltpu.VMEM((16, 2, TILE, L), F32),
            pltpu.VMEM((2, 2, 2, 4, TILE, L), F32),
            pltpu.VMEM((2, 3, TILE, L), F32),
            pltpu.VMEM((2, 3, 16, TILE, L), F32),
            pltpu.VMEM((8, L), F32),
            pltpu.VMEM((16, 8, L), F32),
            dma((10,)),
            dma((10,)),
            dma((5,)),
            dma((5,)),
            dma((NT - 1, 2)),
            dma((NT - 1, 2)),
            dma((4,)),
            pltpu.VMEM((ZERO_B + 1, TILE, F), BF16),
            pltpu.VMEM((NT, 2 * WIDTH, TILE, F), BF16),
            pltpu.VMEM((ZERO_R + 1, TILE, F), BF16),
            pltpu.VMEM((NT, 16, TILE, F), BF16),
            dma((NT - 1, 4)),
            dma((NT - 1, 4)),
            dma((4,)),
            pltpu.SMEM((5,), jnp.int32),
            pltpu.SMEM((G,), jnp.int32),
            pltpu.SMEM(TABLES.shape, jnp.int32),
            pltpu.SMEM((H,), F32),
            pltpu.SMEM((H,), F32),
            pltpu.SMEM((H,), F32),
            pltpu.VMEM((H // 2, 1, 2 * P_SIZE), F32),
            pltpu.VMEM((ROWS, D), BF16),
            dma((8,)),
        ],
        compiler_params=pltpu.CompilerParams(
            collective_id=1, has_side_effects=True, vmem_limit_bytes=58 << 20
        ),
        name="exchange",
    )(offsets, owner, jnp.asarray(TABLES), rate, bias, skip, gain, hidden, flat)


STEP = 64


def place_kernel(off_ref, own_ref, place_ref, got_ref, bc_ref, dt_ref, rows_ref, out_ref, sem):
    g = owner_groups(own_ref, lax.axis_index("tensor"))
    writes = []

    def write(first, size):
        tiles = pl.ds(first, size)
        cp = pltpu.make_async_copy(out_ref.at[tiles], rows_ref.at[tiles], sem.at[len(writes)])
        cp.start()
        writes.append(cp)

    for n in range(4):
        for q in range(16):
            out_ref[512 + n * 16 + q] = bc_ref[q % 4, n * 4 + q // 4]
    for j in range(4):
        out_ref[576 + j] = dt_ref[3, j]
    write(512, 68)
    for k in range(2):
        for quarter in range(4):
            base = (k * 4 + quarter) * STEP
            for seg in range(2):
                block = off_ref[seg] // 2048 + g[k]
                slot = (2 * seg + k) * SLOT
                first = block * BT + quarter * 32
                for j in range(0, 8, 2):
                    tiles = [got_ref[place_ref[first + 4 * j + q] + slot] for q in range(8)]
                    for q in range(8):
                        out_ref[base + (j + q // 4) * 8 + seg * 4 + q % 4] = tiles[q]
                for n in range(FIXES):
                    at = BLOCKS * BT + ((block * 4 + quarter) * FIXES + n) * 3
                    q = place_ref[at]

                    @pl.when(q >= 0)
                    def _():
                        both = got_ref[place_ref[at + 1] + slot] + got_ref[place_ref[at + 2] + slot]
                        out_ref[base + (q // 4) * 8 + seg * 4 + q % 4] = both

            write(base, STEP)
    for cp in writes:
        cp.wait()


def place(offsets, group_owner, got, bc, dt):
    smem = pl.BlockSpec(memory_space=pltpu.SMEM)
    vmem = pl.BlockSpec(memory_space=pltpu.VMEM)
    table = jnp.asarray(np.concatenate([PLACE[:, :, 0].reshape(-1), FIX.reshape(-1)]))
    got = got.reshape(NT * 4 * SLOT, TILE, F)
    rows = pl.pallas_call(
        place_kernel,
        out_shape=jax.ShapeDtypeStruct((580, TILE, F), BF16),
        in_specs=[smem, smem, smem, vmem, vmem, vmem],
        out_specs=pl.BlockSpec(memory_space=pl.ANY),
        scratch_shapes=[pltpu.VMEM((580, TILE, F), BF16), pltpu.SemaphoreType.DMA((9,))],
        compiler_params=pltpu.CompilerParams(vmem_limit_bytes=16 << 20),
        name="place",
    )(offsets, group_owner, table, got, bc, dt)
    return rows.reshape(580 * TILE, F).T


def shards(flat_weight, offsets, group_owner, hidden, decay_rate, dt_bias, skip_gain, norm_gain):
    gain = norm_gain.reshape(H // 2, 1, 2 * P_SIZE)
    got, bc, dt_rows, mixed = exchange(
        offsets, group_owner, decay_rate, dt_bias, skip_gain, gain, hidden, flat_weight
    )
    return place(offsets, group_owner, got, bc, dt_rows), mixed


def solution(mesh):
    placed = (P(("dp", "tensor"), None), P(), P(), P(None, "dp"), P(), P(), P(), P())
    return jax.shard_map(
        shards,
        mesh=mesh,
        in_specs=placed,
        out_specs=(P("dp", "tensor"), P(None, ("dp", "tensor"))),
        check_vma=False,
    )
```

```python
import functools

import jax
import jax.numpy as jnp
import numpy as np
from jax import lax
from jax.experimental import pallas as pl
from jax.experimental.pallas import tpu as pltpu
from jax.sharding import PartitionSpec as P

H = 256
P_SIZE = 64
N = 256
G = 8
L = 128
ROWS = 290
D = 8192
F = 256
NDP = 32
NT = 4
TILE = 16
CHUNK = 19
BLOCKS = 18
BT = 128
PARTS = (4, 4, 4, 4, 3)
STARTS = (0, 4, 8, 12, 16)
COMMON = (0, 1, 8, 9, 16, 17)
MESH = pl.DeviceIdType.MESH
BF16 = jnp.bfloat16
F32 = jnp.float32


def first_tile(chunk):
    return ROWS * chunk // TILE


def make_tables():
    n = len(PARTS)
    lo = np.full((n, NT, BLOCKS), 10**6)
    hi = np.full((n, NT, BLOCKS), -1)
    where = {}
    for k in range(NDP * NT):
        for l in range(CHUNK):
            p = max(i for i in range(n) if STARTS[i] <= l)
            b, tau = divmod(first_tile(k) + l, BT)
            if b >= BLOCKS:
                continue
            i = (k // NT) * PARTS[p] + l - STARTS[p]
            where.setdefault((b, tau), []).append((k % NT, p, i))
            lo[p, k % NT, b] = min(lo[p, k % NT, b], i)
            hi[p, k % NT, b] = max(hi[p, k % NT, b], i)
    caps = [int((hi[p] - lo[p] + 1).max()) for p in range(n)]
    start = np.zeros((n, NT, BLOCKS), np.int32)
    for p in range(n):
        start[p] = np.clip(lo[p], 0, NDP * PARTS[p] - caps[p])
    offs = np.concatenate([[0], np.cumsum(caps)])
    slot = int(offs[-1])
    place = np.full((BLOCKS, BT, 2), -1, np.int32)
    for (b, tau), found in where.items():
        for e, (t, p, i) in enumerate(found):
            place[b, tau, e] = t * 4 * slot + offs[p] + i - start[p, t, b]
    spread = {}
    for (b, tau), found in sorted(where.items()):
        for t, p, i in found:
            if b in COMMON:
                key = (t, b, tau % 4)
                spread.setdefault(key, ([], []))[int(p == n - 1)].append((tau, offs[p] + i - start[p, t, b]))
    early = max(len(v[0]) for v in spread.values())
    width = early + max(len(v[1]) for v in spread.values())
    relay = np.full((NT, BLOCKS, 4, width), -1, np.int32)
    gathered = np.full((4, BLOCKS, 32, 2), -1, np.int32)
    for (t, b, r), found in spread.items():
        for m, tiles in enumerate(found):
            for j, (tau, at) in enumerate(tiles, m * early):
                relay[t, b, r, j] = at
                e = int(gathered[r, b, tau // 4, 0] >= 0)
                gathered[r, b, tau // 4, e] = t * 2 * width + j
    return caps, [int(o) for o in offs], slot, start, place, early, width, relay, gathered


PICKS = 3
PT = 6 * PICKS + 1
ZERO2 = 2 * NDP
ZERO3 = NT * PT


def make_product_tables():
    pick = np.full((NT, 16, BLOCKS, PICKS), ZERO2, np.int32)
    merge = np.full((16, BLOCKS, 8, 2), -1, np.int32)
    count = np.zeros((NT, 16, BLOCKS), np.int32)
    seen = np.zeros((16, BLOCKS, 8), np.int32)
    for k in range(NDP * NT):
        for l in range(CHUNK):
            tile = first_tile(k) + l
            b, tau = divmod(tile, BT)
            if b >= BLOCKS:
                continue
            t, e, m = k % NT, tau % 16, tau // 16
            n = count[t, e, b]
            pick[t, e, b, n] = (k // NT) * 2 + l // 16
            merge[e, b, m, seen[e, b, m]] = t * PT + n
            count[t, e, b] += 1
            seen[e, b, m] += 1
    return pick, merge


CAPS, OFFS, SLOT, START, PLACE, EARLY, WIDTH, RELAY, GATHERED = make_tables()
PICK, MERGE = make_product_tables()
NP = len(PARTS)
FIXES = 2


def make_fixes():
    fixes = np.full((BLOCKS, 4, FIXES, 3), -1, np.int32)
    for b in range(BLOCKS):
        for quarter in range(4):
            found = [q for q in range(32) if PLACE[b, quarter * 32 + q, 1] >= 0]
            for n, q in enumerate(found):
                fixes[b, quarter, n] = q, *PLACE[b, quarter * 32 + q]
    return fixes


FIX = make_fixes()
W_DT = NP * 18
W_PICK = W_DT + 8
W_MERGE = W_PICK + 18 * PICKS
W_HEAD = W_MERGE + 72
W_RELAY = W_HEAD + 3
W_GATHER = W_RELAY + 8 * WIDTH
W_SIZE = W_GATHER + NT * 32
ZERO_B = 2 * SLOT
ZERO_R = NT * 2 * WIDTH


def dp_order():
    steps = [(a, b, c) for a in range(4) for b in range(4) for c in range(2) if (a, b, c) != (0, 0, 0)]
    steps.sort(key=lambda s: -(min(s[0], 4 - s[0]) + min(s[1], 4 - s[1])))
    out = []
    for a, b, c in steps:
        for q in ((a, b, c), (b, a, c), (-a % 4, -b % 4, c), (-b % 4, -a % 4, c)):
            if q not in out:
                out.append(q)
    return out


ORDER = dp_order()


def dp_partner(d, step):
    x, y, c = d // 8, (d // 2) % 4, d % 2
    return ((x + step[0]) % 4) * 8 + ((y + step[1]) % 4) * 2 + (c + step[2]) % 2


def owner_groups(owner_ref, owner):
    first, last = jnp.int32(G), jnp.int32(-1)
    for g in range(G):
        mine = owner_ref[g] == owner
        first = jnp.where(mine, jnp.minimum(first, g), first)
        last = jnp.where(mine, g, last)
    return jnp.clip(first, 0, G - 1), jnp.clip(last, 0, G - 1)


def find_windows(
    off_ref, own_ref, start_ref, pick_ref, merge_ref, relay_ref, gathered_ref, windows_ref
):
    d = lax.axis_index("dp")
    t = lax.axis_index("tensor")
    e = d // 2
    seg = [off_ref[i] // 2048 for i in range(4)]

    def picks(at, b):
        for n in range(PICKS):
            windows_ref[at + n] = pick_ref[((t * 16 + e) * BLOCKS + b) * PICKS + n]

    for shift in range(NT):
        g = owner_groups(own_ref, (t + shift) % NT)
        for s in range(4):
            b = seg[s // 2] + g[s % 2]
            for p in range(NP):
                windows_ref[p * 18 + shift * 4 + s] = start_ref[(p * NT + t) * BLOCKS + b]
            picks(W_PICK + (shift * 4 + s) * PICKS, b)
        for i in range(2):
            windows_ref[W_DT + shift * 2 + i] = 2 * g[i]
    for i in range(2):
        for p in range(NP):
            windows_ref[p * 18 + 16 + i] = start_ref[(p * NT + t) * BLOCKS + seg[2 + i]]
        picks(W_PICK + (16 + i) * PICKS, seg[2 + i])

    def merged(at, b, m, slot):
        for n in range(2):
            v = merge_ref[((e * BLOCKS + b) * 8 + m) * 2 + n]
            windows_ref[at + n] = jnp.where(v < 0, ZERO3, v + PICKS * slot)

    g = owner_groups(own_ref, t)
    for s in range(4):
        for m in range(8):
            merged(W_MERGE + (s * 8 + m) * 2, seg[s // 2] + g[s % 2], m, s)
    for i in range(2):
        for k in range(2):
            merged(W_MERGE + 64 + (i * 2 + k) * 2, seg[2 + i], g[k], 4 + i)
    mine = jnp.where(d < 16, g[0], g[1])
    windows_ref[W_HEAD] = 2 * mine + (d % 16) // 8
    windows_ref[W_HEAD + 1] = 32 * mine + 2 * (d % 16)
    windows_ref[W_HEAD + 2] = 16 * mine + d % 16
    for shift in range(NT):
        g = owner_groups(own_ref, (t + shift) % NT)
        for i in range(2):
            for n in range(WIDTH):
                v = relay_ref[((t * BLOCKS + seg[2 + i]) * 4 + (t + shift) % NT) * WIDTH + n]
                windows_ref[W_RELAY + (shift * 2 + i) * WIDTH + n] = jnp.where(v < 0, ZERO_B, v + i * SLOT)
            for k in range(2):
                for u in range(4):
                    for n in range(2):
                        v = gathered_ref[((t * BLOCKS + seg[2 + i]) * 32 + g[k] * 4 + u) * 2 + n]
                        at = W_GATHER + shift * 32 + ((i * 2 + k) * 4 + u) * 2 + n
                        windows_ref[at] = jnp.where(v < 0, ZERO_R, v + i * WIDTH)


def iota(shape, dim):
    return lax.broadcasted_iota(jnp.int32, shape, dim)


class Table:
    def __init__(self, ref, base):
        self.ref, self.base = ref, base

    def __getitem__(self, i):
        return self.ref[self.base + i]


TABLES = np.concatenate([a.reshape(-1) for a in (START, PICK, MERGE, RELAY, GATHERED)])
BASES = np.cumsum([0, START.size, PICK.size, MERGE.size, RELAY.size])


def exchange_kernel(
    off_hbm,
    own_hbm,
    table_hbm,
    rate_hbm,
    bias_hbm,
    skip_hbm,
    gain_hbm,
    hidden_ref,
    flat_hbm,
    out_ref,
    bc_ref,
    dt_ref,
    mixed_ref,
    windows_ref,
    *scratch,
):
    loads = scratch[-9:]
    scratch = scratch[:-9]
    off_ref, own_ref, table_ref, rate_ref, bias_ref, skip_ref, gain_ref, flat_ref, load_sem = loads
    whole = [
        (flat_hbm, flat_ref),
        (off_hbm, off_ref),
        (own_hbm, own_ref),
        (table_hbm, table_ref),
        (rate_hbm, rate_ref),
        (bias_hbm, bias_ref),
        (skip_hbm, skip_ref),
        (gain_hbm, gain_ref),
    ]
    loading = [pltpu.make_async_copy(src, dst, load_sem.at[i]) for i, (src, dst) in enumerate(whole)]
    for cp in loading:
        cp.start()
    shifted = scratch[:NP]
    recv = scratch[NP : 2 * NP]
    send = scratch[2 * NP : 3 * NP]
    dtbuf, dtsend, dp_send, dp_recv, z_send, z_recv, self_sem = scratch[3 * NP : 3 * NP + 7]
    hid, prod, precv, zsend, zcom, zrecv, hsend, hrecv, bsend, brecv, qsend, qrecv = scratch[3 * NP + 7 : 3 * NP + 19]
    ag_send, ag_recv, p_send, p_recv, zp_send, zp_recv, own_sem = scratch[3 * NP + 19 : 3 * NP + 26]
    bcbuf, spread, gather, owned, b_send, b_recv, b_self = scratch[3 * NP + 26 :]
    d = lax.axis_index("dp")
    t = lax.axis_index("tensor")
    x, y, c = d // 8, (d // 2) % 4, d % 2
    e, seq = d // 2, d % 2
    chunk = d * NT + t

    barrier = pltpu.get_barrier_semaphore()

    @pl.loop(1, NDP)
    def _(i):
        pl.semaphore_signal(barrier, inc=1, device_id=((d + i) % NDP, t), device_id_type=MESH)

    @pl.loop(1, NT)
    def _(i):
        pl.semaphore_signal(barrier, inc=1, device_id=(d, (t + i) % NT), device_id_type=MESH)

    pl.semaphore_wait(barrier, NDP - 1 + NT - 1)

    def remote(src, dst, ssem, rsem, device):
        cp = pltpu.make_async_remote_copy(
            src_ref=src, dst_ref=dst, send_sem=ssem, recv_sem=rsem, device_id=device, device_id_type=MESH
        )
        cp.start()
        return cp

    def await_bytes(ref, sem):
        pltpu.make_async_copy(ref, ref, sem).wait()

    copies = []

    phase = (ROWS * chunk) % TILE

    def shift_part(p):
        a, rows = STARTS[p] * TILE, PARTS[p] * TILE
        w0, w1 = max(a - TILE, 0), min(a + rows, ROWS)
        pick = jnp.where(iota((rows, w1 - w0), 0) + (a - phase) == iota((rows, w1 - w0), 1) + w0, 1.0, 0.0)
        pick = pick.astype(BF16)

        @pl.loop(0, D // 1024)
        def _(i):
            cols = pl.ds(pl.multiple_of(i * 1024, 1024), 1024)
            moved = jnp.dot(pick, flat_ref[w0:w1, cols], preferred_element_type=F32)
            shifted[p][:, :, cols] = moved.astype(BF16).reshape(PARTS[p], TILE, 1024)

    def send_part(p):
        mine = pl.ds(d * PARTS[p], PARTS[p])
        for step in ORDER:
            peer = dp_partner(d, step)
            remote(
                shifted[p].at[:, :, pl.ds(pl.multiple_of(peer * F, F), F)],
                recv[p].at[mine],
                dp_send.at[p],
                dp_recv.at[p],
                (peer, t),
            )
        pltpu.make_async_copy(
            shifted[p].at[:, :, pl.ds(pl.multiple_of(d * F, F), F)], recv[p].at[mine], dp_recv.at[p]
        ).start()

    def forward_part(p):
        await_bytes(recv[p], dp_recv.at[p])

        def pack(dst, window, at=0):
            first = windows_ref[window]

            @pl.loop(0, CAPS[p], unroll=2)
            def _(j):
                dst[at + j] = recv[p][first + j]

        for i in range(2):
            pack(bcbuf, p * 18 + 16 + i, i * SLOT + OFFS[p])
        for l in range(max(STARTS[p], 3), STARTS[p] + PARTS[p]):
            dtbuf[l - 3] = recv[p][31 * PARTS[p] + l - STARTS[p]]
        if p >= NP - 2:
            spread_common(p - (NP - 2))
        for shift in (1, 3, 2, 0):
            for s in range(4):
                pack(send[p].at[shift, s], p * 18 + shift * 4 + s)
            src, dst = send[p].at[shift], out_ref.at[t, :, pl.ds(OFFS[p], CAPS[p])]
            to_owner(src, dst, shift, p)

    def to_owner(src, dst, shift, n):
        if shift == 0:
            cp = pltpu.make_async_copy(src, dst, self_sem.at[n])
            cp.start()
        else:
            cp = remote(src, dst, z_send.at[shift - 1, n], z_recv.at[shift - 1, n], (d, (t + shift) % NT))
        copies.append(cp)

    bcopies = []

    def spread_common(late):
        low, high = (EARLY, WIDTH) if late else (0, EARLY)
        for shift in (1, 3, 2, 0):
            for i in range(2):
                for n in range(i * WIDTH + low, i * WIDTH + high):
                    spread[shift, n] = bcbuf[windows_ref[W_RELAY + shift * 2 * WIDTH + n]]
                src = spread.at[shift, pl.ds(i * WIDTH + low, high - low)]
                dst = gather.at[pl.ds((t * 2 + i) * WIDTH + low, high - low)]
                j = 2 * late + i
                if shift == 0:
                    cp = pltpu.make_async_copy(src, dst, b_self.at[j])
                    cp.start()
                else:
                    sems = b_send.at[shift - 1, j], b_recv.at[shift - 1, j]
                    cp = remote(src, dst, *sems, (d, (t + shift) % NT))
                bcopies.append(cp)

    def share_common():
        for cp in bcopies:
            cp.wait()
        for shift in (1, 3, 2, 0):
            for n in range(16):
                at = W_GATHER + shift * 32 + 2 * n
                owned[shift, n] = gather[windows_ref[at]] + gather[windows_ref[at + 1]]
            to_owner(owned.at[shift], bc_ref.at[t], shift, NP + 1)

    def forward_dt():
        for shift in (1, 3, 2, 0):
            for i in range(2):
                for j in range(2):
                    dtsend[shift, 2 * i + j] = dtbuf[windows_ref[W_DT + shift * 2 + i] + j]
            to_owner(dtsend.at[shift], dt_ref.at[t], shift, NP)

    def along_x(i):
        return (((x + i) % 4) * 8 + y * 2 + c, t)

    def along_y(i):
        return (x * 8 + ((y + i) % 4) * 2 + c, t)

    quarter = L // NT
    pieces = []
    for first, size in ((pl.multiple_of(t * quarter, TILE), quarter // 2), (L, L // 2)):
        pieces.append((pl.ds(first, size), size, along_x, along_y))
        pieces.append((pl.ds(first + size, size), size, along_y, along_x))

    def gather_first():
        owns = []
        for n, (first, size) in enumerate(((pl.multiple_of(t * quarter, TILE), quarter), (L, L))):
            tokens = pl.ds(first, size)
            owns.append(pltpu.make_async_copy(hidden_ref.at[tokens], hid.at[x, y, c, tokens], own_sem.at[3 * n]))
            owns[n].start()
        for j, (tokens, _, partner, _) in enumerate(pieces):
            for i in (2, 1, 3):
                remote(hidden_ref.at[tokens], hid.at[x, y, c, tokens], ag_send.at[j], ag_recv.at[j], partner(i))
        for cp in owns:
            cp.wait()

    def gather_second():
        for j, (tokens, size, first, then) in enumerate(pieces):
            await_bytes(hid.at[0:3, 0, 0, 0:size], ag_recv.at[j])
            line = hid.at[:, y, c, tokens] if first is along_x else hid.at[x, :, c, tokens]
            for i in (2, 1, 3):
                remote(line, line, ag_send.at[4 + j], ag_recv.at[4 + j], then(i))

    def gather_planes():
        for j in range(2):
            await_bytes(hid.at[0:3, :, 0, 0 : pieces[j][1]], ag_recv.at[4 + j])
        part = hid.at[:, :, c, pl.ds(pl.multiple_of(t * quarter, TILE), quarter)]
        for i in (2, 1, 3):
            remote(part, part, ag_send.at[8], ag_recv.at[8], (d, (t + i) % NT))

    def gather_third():
        for j in range(2, 4):
            await_bytes(hid.at[0:3, :, 0, 0 : pieces[j][1]], ag_recv.at[4 + j])
        await_bytes(hid.at[:, :, 0, 0 : 3 * quarter], ag_recv.at[8])
        remote(hid.at[:, :, c], hid.at[:, :, c], ag_send.at[9], ag_recv.at[9], (d + 1 - 2 * c, t))

    def multiply_half(core):
        @pl.loop(0, 4)
        def _(i):
            part = jnp.zeros((CHUNK * TILE, 2 * L), F32)
            for j in range(4):
                cols = pl.ds(pl.multiple_of((i * 8 + j * 2 + core) * F, F), F)
                rows = jnp.concatenate(
                    [shifted[p][:, :, cols].reshape(PARTS[p] * TILE, F) for p in range(NP)], axis=0
                )
                part += lax.dot_general(
                    rows, hid[i, j, core], (((1,), (1,)), ((), ())), preferred_element_type=F32
                )
            for s in range(2):
                tiles = part[:, s * L : (s + 1) * L].reshape(CHUNK, TILE, L)
                prod[s, 0] += tiles[:16]
                prod[s, 1, 0 : CHUNK - 16] += tiles[16:]

    def multiply():
        multiply_half(c)
        await_bytes(hid.at[:, :, 0], ag_recv.at[9])
        multiply_half(1 - c)

    def product_tiles(i):
        low = (i // 2 + 16 * NDP * NT * CHUNK - first_tile(chunk)) % 16
        return low, i % 2

    def send_products():
        @pl.loop(1, NDP)
        def _(n):
            i = (d + n) % NDP
            low, s = product_tiles(i)
            remote(prod.at[s, :, low], precv.at[pl.ds(2 * d, 2)], p_send.at[0], p_recv.at[0], (i, t))

        low, s = product_tiles(d)
        pltpu.make_async_copy(prod.at[s, :, low], precv.at[pl.ds(2 * d, 2)], p_recv.at[0]).start()

    def forward_products():
        await_bytes(precv.at[0 : 2 * NDP], p_recv.at[0])
        for n in range(2 * PICKS):
            zcom[n] = precv[windows_ref[W_PICK + 16 * PICKS + n]]
        zcom[2 * PICKS] = precv[2 * 31 + (3 + e) // 16]
        for shift in (1, 3, 2, 0):
            for n in range(4 * PICKS):
                zsend[shift, n] = precv[windows_ref[W_PICK + shift * 4 * PICKS + n]]
            for j, (src, n0, n1) in enumerate([(zsend.at[shift], 0, 4 * PICKS), (zcom, 4 * PICKS, PT)]):
                dst = zrecv.at[pl.ds(t * PT + n0, n1 - n0)]
                if shift == 0:
                    cp = pltpu.make_async_copy(src, dst, own_sem.at[1 + j])
                    cp.start()
                else:
                    cp = remote(src, dst, zp_send.at[shift - 1, j], zp_recv.at[shift - 1, j], (d, (t + shift) % NT))
                pcopies.append(cp)

    pcopies = []

    def send_heads():
        for cp in pcopies:
            cp.wait()

        def total(at):
            return zrecv[windows_ref[at]] + zrecv[windows_ref[at + 1]]

        for k in range(2):
            for i in range(2):
                bsend[k, i] = total(W_MERGE + 64 + (i * 2 + k) * 2)
            bsend[k, 2] = zrecv[3 * PT + PT - 1]
        for k in range(2):
            for m in range(8):
                for i in range(2):
                    hsend[k * 8 + m, i] = total(W_MERGE + ((2 * i + k) * 8 + m) * 2)

        @pl.loop(1, 16)
        def _(n):
            i = (d + 2 * n) % NDP
            remote(bsend.at[i // 16], brecv.at[seq, :, e], p_send.at[1], p_recv.at[1], (i, t))

        pltpu.make_async_copy(bsend.at[d // 16], brecv.at[seq, :, e], p_recv.at[1]).start()

        @pl.loop(0, 16)
        def _(n):
            i = 16 * (n // 8) + 2 * (n % 8) + e // 8
            dst = hrecv.at[seq, :, (e // 4) % 2, e % 4]

            @pl.when(i != d)
            def _():
                remote(hsend.at[n], dst, p_send.at[2], p_recv.at[2], (i, t))

            @pl.when(i == d)
            def _():
                pltpu.make_async_copy(hsend.at[n], dst, p_recv.at[2]).start()

    high = lax.Precision.HIGHEST
    values = []

    def share_products():
        await_bytes(brecv.at[seq], p_recv.at[1])
        remote(brecv.at[seq], brecv.at[seq], p_send.at[4], p_recv.at[4], (d + 1 - 2 * c, t))

    def mix():
        await_bytes(brecv.at[seq], p_recv.at[4])
        await_bytes(hrecv, p_recv.at[2])
        head = windows_ref[W_HEAD + 1]
        lower = iota((L, L), 0) <= iota((L, L), 1)
        ones = jnp.where(lower, 1.0, 0.0).astype(F32)
        qsend[...] = jnp.zeros_like(qsend)
        for s in range(2):
            bmat = brecv[s, 0].reshape(N, L)
            cmat = brecv[s, 1].reshape(N, L)
            scores = lax.dot_general(bmat, cmat, (((0,), (0,)), ((), ())), precision=high, preferred_element_type=F32)
            raw = brecv[s, 2, windows_ref[W_HEAD]]
            squares = jnp.zeros((1, L), F32)
            for hh in range(2):
                r = 2 * (d % 8) + hh
                row = jnp.sum(jnp.where(iota((TILE, L), 0) == r, raw, 0.0), axis=0, keepdims=True)
                row = row + bias_ref[head + hh]
                step = jnp.maximum(row, 0.0) + jnp.log1p(jnp.exp(-jnp.abs(row)))
                rates = jnp.broadcast_to(step * -rate_ref[head + hh], (8, L))
                cumul = jnp.dot(rates, ones, precision=high, preferred_element_type=F32)
                across = jnp.broadcast_to(cumul[0:1], (L, L))
                diff = across - across.T
                decay = jnp.where(lower, jnp.exp(jnp.where(lower, diff, 0.0)), 0.0)
                weights = scores * decay * jnp.broadcast_to(step, (L, L)).T
                xt = hrecv[s, 1, hh].reshape(P_SIZE, L)
                zt = hrecv[s, 0, hh].reshape(P_SIZE, L)
                out = jnp.dot(xt, weights, precision=high, preferred_element_type=F32) + skip_ref[head + hh] * xt
                v = out * (zt * jax.nn.sigmoid(zt))
                squares = squares + jnp.sum(v * v, axis=0, keepdims=True)
                values.append(v)
            qsend[s : s + 1] = squares
        base = 16 * (d // 16)

        @pl.loop(1, 16)
        def _(n):
            i = base + (d + n) % 16
            remote(qsend, qrecv.at[d % 16], p_send.at[3], p_recv.at[3], (i, t))

        pltpu.make_async_copy(qsend, qrecv.at[d % 16], p_recv.at[3]).start()

    def finish():
        await_bytes(qrecv, p_recv.at[3])
        total = jnp.sum(qrecv[...], axis=0)
        scale = lax.rsqrt(total / (32 * P_SIZE) + 1e-05)
        gain = gain_ref[windows_ref[W_HEAD + 2]]
        for s in range(2):
            v = jnp.concatenate(values[2 * s : 2 * s + 2], axis=0) * scale[s : s + 1]
            mixed_ref[s * L : (s + 1) * L] = (v.T * gain).astype(BF16)

    prod[...] = jnp.zeros_like(prod)
    zero = jnp.zeros((TILE, L), F32)
    bcbuf[ZERO_B] = jnp.zeros((TILE, F), BF16)
    gather[ZERO_R] = jnp.zeros((TILE, F), BF16)
    precv[ZERO2] = zero
    zrecv[ZERO3] = zero
    gather_first()
    loading[0].wait()
    shift_part(0)
    gather_second()
    send_part(0)
    gather_planes()
    shift_part(1)
    send_part(1)
    shift_part(2)
    shift_part(3)
    shift_part(4)
    for cp in loading[1:]:
        cp.wait()
    find_windows(off_ref, own_ref, *[Table(table_ref, int(i)) for i in BASES], windows_ref)
    gather_third()
    multiply()
    send_products()
    send_part(2)
    forward_part(0)
    forward_part(1)
    send_part(3)
    forward_products()
    send_part(4)
    forward_part(2)
    send_heads()
    forward_part(3)
    share_products()
    forward_part(4)
    forward_dt()
    mix()
    share_common()
    finish()

    for cp in copies:
        cp.wait()
    for p in range(NP):
        await_bytes(shifted[p].at[:, :, 0 : (NDP - 1) * F], dp_send.at[p])
    for j, (_, size, _, _) in enumerate(pieces):
        await_bytes(hid.at[0:3, 0, 0, 0:size], ag_send.at[j])
        await_bytes(hid.at[0:3, :, 0, 0:size], ag_send.at[4 + j])
    await_bytes(hid.at[:, :, 0, 0 : 3 * quarter], ag_send.at[8])
    await_bytes(hid.at[:, :, 0], ag_send.at[9])
    await_bytes(precv.at[0 : 2 * (NDP - 1)], p_send.at[0])
    await_bytes(brecv.at[1, :, 0:15], p_send.at[1])
    await_bytes(brecv.at[1], p_send.at[4])
    itself = seq == e // 8

    @pl.when(itself)
    def _():
        await_bytes(hsend.at[0:15], p_send.at[2])

    @pl.when(jnp.logical_not(itself))
    def _():
        await_bytes(hsend, p_send.at[2])

    await_bytes(qrecv.at[0:15], p_send.at[3])


def exchange(offsets, owner, rate, bias, skip, gain, hidden, flat):
    hbm = pl.BlockSpec(memory_space=pltpu.HBM)
    vmem = pl.BlockSpec(memory_space=pltpu.VMEM)
    dma = pltpu.SemaphoreType.DMA
    return pl.pallas_call(
        exchange_kernel,
        out_shape=(
            pltpu.VMEM((NT, 4, SLOT, TILE, F), BF16),
            pltpu.VMEM((NT, 16, TILE, F), BF16),
            pltpu.VMEM((NT, 4, TILE, F), BF16),
            jax.ShapeDtypeStruct((2 * L, L), BF16),
        ),
        in_specs=[hbm] * 9,
        out_specs=(vmem,) * 4,
        scratch_shapes=[pltpu.SMEM((W_SIZE,), jnp.int32)]
        + [pltpu.VMEM((w, TILE, D), BF16) for w in PARTS]
        + [pltpu.VMEM((NDP * w, TILE, F), BF16) for w in PARTS]
        + [pltpu.VMEM((NT, 4, c, TILE, F), BF16) for c in CAPS]
        + [
            pltpu.VMEM((16, TILE, F), BF16),
            pltpu.VMEM((NT, 4, TILE, F), BF16),
            dma((NP,)),
            dma((NP,)),
            dma((NT - 1, NP + 2)),
            dma((NT - 1, NP + 2)),
            dma((NP + 2,)),
            pltpu.VMEM((4, 4, 2, 2 * L, F), BF16),
            pltpu.VMEM((2, 2, 16, TILE, L), F32),
            pltpu.VMEM((ZERO2 + 1, TILE, L), F32),
            pltpu.VMEM((NT, 4 * PICKS, TILE, L), F32),
            pltpu.VMEM((2 * PICKS + 1, TILE, L), F32),
            pltpu.VMEM((ZERO3 + 1, TILE, L), F32),
            pltpu.VMEM((16, 2, TILE, L), F32),
            pltpu.VMEM((2, 2, 2, 4, TILE, L), F32),
            pltpu.VMEM((2, 3, TILE, L), F32),
            pltpu.VMEM((2, 3, 16, TILE, L), F32),
            pltpu.VMEM((8, L), F32),
            pltpu.VMEM((16, 8, L), F32),
            dma((10,)),
            dma((10,)),
            dma((5,)),
            dma((5,)),
            dma((NT - 1, 2)),
            dma((NT - 1, 2)),
            dma((4,)),
            pltpu.VMEM((ZERO_B + 1, TILE, F), BF16),
            pltpu.VMEM((NT, 2 * WIDTH, TILE, F), BF16),
            pltpu.VMEM((ZERO_R + 1, TILE, F), BF16),
            pltpu.VMEM((NT, 16, TILE, F), BF16),
            dma((NT - 1, 4)),
            dma((NT - 1, 4)),
            dma((4,)),
            pltpu.SMEM((5,), jnp.int32),
            pltpu.SMEM((G,), jnp.int32),
            pltpu.SMEM(TABLES.shape, jnp.int32),
            pltpu.SMEM((H,), F32),
            pltpu.SMEM((H,), F32),
            pltpu.SMEM((H,), F32),
            pltpu.VMEM((H // 2, 1, 2 * P_SIZE), F32),
            pltpu.VMEM((ROWS, D), BF16),
            dma((8,)),
        ],
        compiler_params=pltpu.CompilerParams(
            collective_id=1, has_side_effects=True, vmem_limit_bytes=58 << 20
        ),
        name="exchange",
    )(offsets, owner, jnp.asarray(TABLES), rate, bias, skip, gain, hidden, flat)


STEP = 64


def place_kernel(off_ref, own_ref, place_ref, got_ref, bc_ref, dt_ref, rows_ref, out_ref, sem):
    g = owner_groups(own_ref, lax.axis_index("tensor"))
    writes = []

    def write(first, size):
        tiles = pl.ds(first, size)
        cp = pltpu.make_async_copy(out_ref.at[tiles], rows_ref.at[tiles], sem.at[len(writes)])
        cp.start()
        writes.append(cp)

    for n in range(4):
        for q in range(16):
            out_ref[512 + n * 16 + q] = bc_ref[q % 4, n * 4 + q // 4]
    for j in range(4):
        out_ref[576 + j] = dt_ref[3, j]
    write(512, 68)
    for k in range(2):
        for quarter in range(4):
            base = (k * 4 + quarter) * STEP
            for seg in range(2):
                block = off_ref[seg] // 2048 + g[k]
                slot = (2 * seg + k) * SLOT
                first = block * BT + quarter * 32
                for j in range(0, 8, 2):
                    tiles = [got_ref[place_ref[first + 4 * j + q] + slot] for q in range(8)]
                    for q in range(8):
                        out_ref[base + (j + q // 4) * 8 + seg * 4 + q % 4] = tiles[q]
                for n in range(FIXES):
                    at = BLOCKS * BT + ((block * 4 + quarter) * FIXES + n) * 3
                    q = place_ref[at]

                    @pl.when(q >= 0)
                    def _():
                        both = got_ref[place_ref[at + 1] + slot] + got_ref[place_ref[at + 2] + slot]
                        out_ref[base + (q // 4) * 8 + seg * 4 + q % 4] = both

            write(base, STEP)
    for cp in writes:
        cp.wait()


def place(offsets, group_owner, got, bc, dt):
    smem = pl.BlockSpec(memory_space=pltpu.SMEM)
    vmem = pl.BlockSpec(memory_space=pltpu.VMEM)
    table = jnp.asarray(np.concatenate([PLACE[:, :, 0].reshape(-1), FIX.reshape(-1)]))
    got = got.reshape(NT * 4 * SLOT, TILE, F)
    rows = pl.pallas_call(
        place_kernel,
        out_shape=jax.ShapeDtypeStruct((580, TILE, F), BF16),
        in_specs=[smem, smem, smem, vmem, vmem, vmem],
        out_specs=pl.BlockSpec(memory_space=pl.ANY),
        scratch_shapes=[pltpu.VMEM((580, TILE, F), BF16), pltpu.SemaphoreType.DMA((9,))],
        compiler_params=pltpu.CompilerParams(vmem_limit_bytes=16 << 20),
        name="place",
    )(offsets, group_owner, table, got, bc, dt)
    return rows.reshape(580 * TILE, F).T


def shards(flat_weight, offsets, group_owner, hidden, decay_rate, dt_bias, skip_gain, norm_gain):
    gain = norm_gain.reshape(H // 2, 1, 2 * P_SIZE)
    got, bc, dt_rows, mixed = exchange(
        offsets, group_owner, decay_rate, dt_bias, skip_gain, gain, hidden, flat_weight
    )
    return place(offsets, group_owner, got, bc, dt_rows), mixed


def solution(mesh):
    placed = (P(("dp", "tensor"), None), P(), P(), P(None, "dp"), P(), P(), P(), P())
    return jax.shard_map(
        shards,
        mesh=mesh,
        in_specs=placed,
        out_specs=(P("dp", "tensor"), P(None, ("dp", "tensor"))),
        check_vma=False,
    )
```
